32 devices in a mesh: ctx: 8 (over y, x, core), head: 4 (over z).
Axes of the slice: x: 2, y: 2, z: 4, core: 2. Of those that a mesh axis runs over, the one named last changes fastest.
Arguments:
- kda_inputs: bfloat16 [3, 1024, 4096], P(None, 'ctx', 'head'), may hold values from -4 to 4
- gate_log: float32 [1024, 4096], P('ctx', 'head'), may hold values from -2.2 to 0
- beta: float32 [1024, 32], P('ctx', 'head'), may hold values from 0.1 to 0.9
- conv_weight: float32 [3, 4, 4096], P(None, None, 'head'), may hold values from -3 to 3
- kda_out_weight: bfloat16 [4096, 2304], P('head'), may hold values from -3 to 3
- residual: bfloat16 [1024, 2304], P('ctx'), may hold values from -3 to 3
- norm_gain: float32 [2304], replicated, may hold values from 0.1 to 1.9
- latent_weight: bfloat16 [2304, 512], replicated, may hold values from -0.125 to 0.125
- latent_gain: float32 [512], replicated, may hold values from 0.1 to 1.9
- query_weight: bfloat16 [2304, 2048], P(None, 'head'), may hold values from -0.27083333 to 0.27083333
- up_weight: bfloat16 [512, 2, 2048], P(None, None, 'head'), may hold values from -0.5745243 to 0.5745243
Outputs:
- stream_out: bfloat16 [1024, 2304], P('ctx')
- attention_out: bfloat16 [1024, 2048], P('ctx', 'head')
The draws below stay inside these ranges and needn't reach their ends.
All inputs are finite; a program needn't handle non-finite values.
Results may differ from the reference program's by a relative error of at most 0.04.
Values may be sent and summed in bfloat16 or wider, within the bound.
No kernel may reach another device: no remote copies, remote signals or barrier semaphores. Data moves between devices by JAX's collectives and lax.ppermute only.
A program may use at most 128 MiB of HBM per device.

```python
import math
import jax
import jax.numpy as jnp
from jax import lax

D = 2304
HK = 32
DK = 128
CONV = 4
LAT = 512
HM = 16
DH = 128
TOK_DEV = 128
SEQUENCE_TOKENS = 1024


def draw_gate_log(key, part):
    channel_count = HK * DK
    blocks = SEQUENCE_TOKENS // TOK_DEV
    collected_keys = jax.random.split(key, 7)
    fast_share = 0.5
    chooser = jax.random.uniform(collected_keys[0], (channel_count,), jnp.float32)
    slow_rate = jnp.exp(jax.random.uniform(collected_keys[1], (channel_count,), jnp.float32, math.log(0.03), math.log(0.3))) / SEQUENCE_TOKENS
    fast_rate = jnp.exp(jax.random.uniform(collected_keys[2], (channel_count,), jnp.float32, math.log(1.0 / 50.0), math.log(1.0 / 30.0)))
    base_rate = jnp.where(chooser < fast_share, fast_rate, slow_rate)
    block_factor = jnp.exp(jax.random.uniform(collected_keys[3], (blocks, 1, channel_count), jnp.float32, -math.log(2.0), math.log(2.0)))
    roughness = jax.random.uniform(collected_keys[4], (blocks, TOK_DEV, channel_count), jnp.float32, 0.5, 1.5)
    log_decay_rates = -(base_rate * block_factor * roughness).reshape(SEQUENCE_TOKENS, channel_count)
    segment_rows = jax.random.randint(collected_keys[5], (3,), 0, SEQUENCE_TOKENS)
    segment_decay_total = jnp.log(jax.random.uniform(collected_keys[6], (3, channel_count), jnp.float32, 0.5, 0.8))
    token_positions = jnp.arange(SEQUENCE_TOKENS)[:, None]
    for segment_index in range(3):
        log_decay_rates = log_decay_rates + jnp.where(token_positions == segment_rows[segment_index], segment_decay_total[segment_index][None, :], 0.0)
    return log_decay_rates


def draw_kda_inputs(key, part):
    channel_count = HK * DK
    entries = jnp.clip(jax.random.normal(jax.random.fold_in(key, 3), (3, SEQUENCE_TOKENS, channel_count), jnp.float32), -4.0, 4.0)
    head_keys = jax.random.split(jax.random.fold_in(key, 4), HK)
    ranking = jax.vmap(lambda head_key: jax.random.permutation(head_key, DK))(head_keys)
    strong = ranking < DK // 8
    faint_scale = math.sqrt(3.0 * (DK // 8) / SEQUENCE_TOKENS)
    key_scale = jnp.where(strong, 1.0, faint_scale).astype(jnp.float32).reshape(channel_count)
    part_scale = jnp.stack([jnp.ones_like(key_scale), key_scale, jnp.ones_like(key_scale)])
    return (entries * part_scale[:, None, :]).astype(jnp.bfloat16)


def head_strength(key, strongest):
    ranking = jax.random.permutation(jax.random.fold_in(key, 71), HM)
    return jnp.float32(strongest) ** (ranking.astype(jnp.float32) / (HM - 1))


def draw_query_weight(key, part):
    strongest = 8.0
    entries = jnp.clip(jax.random.normal(jax.random.fold_in(key, 5), (D, HM * DH), jnp.float32), -3.0, 3.0)
    column_scale = jnp.repeat(jnp.sqrt(head_strength(key, strongest)), DH)
    return (entries * column_scale[None, :] / math.sqrt(D)).astype(jnp.bfloat16)


def draw_up_weight(key, part):
    strongest = 8.0
    entries = jnp.clip(jax.random.normal(jax.random.fold_in(key, 6), (LAT, 2, HM * DH), jnp.float32), -3.0, 3.0)
    key_scale = jnp.repeat(jnp.sqrt(head_strength(key, strongest)), DH)
    both_scales = jnp.stack([key_scale, jnp.ones_like(key_scale)])
    return (entries * both_scales[None, :, :] / math.sqrt(LAT)).astype(jnp.bfloat16)


def level_of(stream_key, shape, cuts, low, high):
    loudness = 1.0
    for dim, parts in cuts:
        steps = jax.random.uniform(jax.random.fold_in(jax.random.fold_in(stream_key, 6), dim), (parts,), jnp.float32, low / len(cuts), high / len(cuts))
        loudness = loudness * jnp.repeat(jnp.exp(steps), shape[dim] // parts).reshape((-1,) + (1,) * (len(shape) - 1 - dim))
    return loudness


def scatter_about(rng, shape, deviation, bound, shards=(), kind=jnp.bfloat16):
    result = jax.random.normal(rng, shape, jnp.float32) * deviation
    if len(shards) > 0:
        result = level_of(rng, shape, shards, -0.22, 0.18) * result
    return jnp.clip(result, min=-bound, max=bound).astype(kind)


def setup_inputs(seed: int = 0) -> dict:
    keys = jax.random.split(jax.random.key(seed), 12)
    return {
        "kda_inputs": draw_kda_inputs(jax.random.fold_in(keys[11], 71), 0),
        "gate_log": draw_gate_log(jax.random.fold_in(keys[11], 71), 0),
        "beta": jnp.clip(0.1 + 0.79999997 * jax.random.uniform(keys[2], (SEQUENCE_TOKENS, HK), jnp.float32) ** level_of(keys[2], (SEQUENCE_TOKENS, HK), ((0, 8), (1, 4)), -0.2, 0.2), 0.1, 0.9),
        "conv_weight": scatter_about(keys[3], (3, CONV, HK * DK), 0.5, 3.0, ((2, 4),), jnp.float32),
        "kda_out_weight": scatter_about(keys[4], (HK * DK, D), (HK // 8) ** -0.5, 3.0, ((0, 4),)),
        "residual": scatter_about(keys[5], (SEQUENCE_TOKENS, D), 0.5, 3.0, ((0, 8),)),
        "norm_gain": jnp.clip(1.0 + 0.18 * jax.random.normal(keys[6], (D,), jnp.float32), 0.1, 1.9),
        "latent_weight": scatter_about(keys[7], (D, LAT), D ** -0.5, 0.125),
        "latent_gain": jnp.clip(1.0 + 0.18 * jax.random.normal(keys[8], (LAT,), jnp.float32), 0.1, 1.9),
        "query_weight": draw_query_weight(jax.random.fold_in(keys[11], 71), 0),
        "up_weight": draw_up_weight(jax.random.fold_in(keys[11], 71), 0),
    }


eps_norm = 1e-06
highest_precision = lax.Precision.HIGHEST

def rounded(values):
    return lax.optimization_barrier(values.astype(jnp.bfloat16))

def short_conv(signal, weights):
    widened = signal.astype(jnp.float32)
    length = widened.shape[0]
    padded = jnp.concatenate([jnp.zeros((CONV - 1, widened.shape[1]), jnp.float32), widened], axis=0)
    running = jnp.zeros_like(widened)
    for tap_index in range(CONV):
        running = running + weights[tap_index] * padded[tap_index:tap_index + length]
    return jax.nn.silu(running)

def unit_heads(activated):
    grouped = activated.reshape(activated.shape[0], -1, DK)
    scaled = grouped * lax.rsqrt(lax.optimization_barrier(jnp.sum(grouped * grouped, axis=-1, keepdims=True)) + eps_norm)
    return scaled.reshape(activated.shape)

def prepare(stream, norm_gain, latent_weight, latent_gain):
    widened = stream.astype(jnp.float32)
    normed = (widened * lax.rsqrt(lax.optimization_barrier(jnp.mean(widened * widened, axis=-1, keepdims=True)) + eps_norm) * norm_gain).astype(jnp.bfloat16)
    latent_pre = jnp.dot(normed, latent_weight, preferred_element_type=jnp.float32)
    latent = (latent_pre * lax.rsqrt(lax.optimization_barrier(jnp.mean(latent_pre * latent_pre, axis=-1, keepdims=True)) + eps_norm) * latent_gain).astype(jnp.bfloat16)
    return (normed, latent)

def attend_block(query_block, first_row, group_keys, group_values):
    query_positions = first_row + jnp.arange(query_block.shape[0], dtype=jnp.int32)
    key_positions = jnp.arange(group_keys.shape[0], dtype=jnp.int32)
    scores = jnp.einsum('qhd,khd->hqk', query_block, group_keys, precision=highest_precision) * DH ** (-0.5)
    allowed = key_positions[None, :] <= query_positions[:, None]
    peak = lax.optimization_barrier(jnp.max(jnp.where(allowed, scores, -jnp.inf), axis=-1, keepdims=True))
    weights = jnp.where(allowed, jnp.exp(scores - peak), 0.0)
    totals = lax.optimization_barrier(jnp.sum(weights, axis=-1))
    mixed = jnp.einsum('hqk,khd->qhd', rounded(weights).astype(jnp.float32), group_values, precision=highest_precision)
    return (mixed / jnp.transpose(totals)[:, :, None]).astype(jnp.bfloat16)

def reference(kda_inputs, gate_log, beta, conv_weight, kda_out_weight, residual, norm_gain, latent_weight, latent_gain, query_weight, up_weight):
    activated = [short_conv(kda_inputs[branch], conv_weight[branch]) for branch in range(3)]
    kda_query = rounded(unit_heads(activated[0]) * DK ** (-0.5)).astype(jnp.float32)
    kda_key = rounded(unit_heads(activated[1])).astype(jnp.float32)
    kda_value = rounded(activated[2]).astype(jnp.float32)
    decays = jnp.exp(gate_log)

    def advance(recurrent_state, inputs_row):
        current_query_row, current_key_row, value_row, decay_row, rate_row = inputs_row
        decayed_state = decay_row[:, :, None] * recurrent_state
        predicted_value = jnp.einsum('sa,sau->su', current_key_row, decayed_state, precision=highest_precision)
        recurrent_state = decayed_state + rate_row[:, None, None] * current_key_row[:, :, None] * (value_row - predicted_value)[:, None, :]
        return (recurrent_state, jnp.einsum('sa,sau->su', current_query_row, recurrent_state, precision=highest_precision))

    def split_heads(values):
        return values.reshape(SEQUENCE_TOKENS, HK, DK)
    _, core_rows = lax.scan(advance, jnp.zeros((HK, DK, DK), jnp.float32), (split_heads(kda_query), split_heads(kda_key), split_heads(kda_value), split_heads(decays), beta))
    kda_core = core_rows.reshape(SEQUENCE_TOKENS, HK * DK).astype(jnp.bfloat16)
    kda_proj = jnp.dot(kda_core, kda_out_weight, preferred_element_type=jnp.float32)
    stream_out = (residual.astype(jnp.float32) + kda_proj).astype(jnp.bfloat16)
    normed, latent = prepare(stream_out, norm_gain, latent_weight, latent_gain)
    mla_query = rounded(jnp.dot(normed, query_weight, preferred_element_type=jnp.float32)).astype(jnp.float32).reshape(SEQUENCE_TOKENS, HM, DH)
    paired = rounded(jnp.dot(latent, up_weight.reshape(LAT, 2 * HM * DH), preferred_element_type=jnp.float32)).astype(jnp.float32).reshape(SEQUENCE_TOKENS, 2, HM, DH)
    keys_all = paired[:, 0]
    values_all = paired[:, 1]
    block_rows = math.gcd(SEQUENCE_TOKENS, 256)
    block_count = SEQUENCE_TOKENS // block_rows
    group_count = math.gcd(block_count, 8)
    per_group = block_count // group_count
    query_blocks = mla_query.reshape(block_count, block_rows, HM, DH)
    results = []
    for group_index in range(group_count):
        first_block = group_index * per_group
        key_end = (first_block + per_group) * block_rows
        group_keys = keys_all[:key_end]
        group_values = values_all[:key_end]
        starts = (first_block + jnp.arange(per_group, dtype=jnp.int32)) * block_rows
        group_out = lax.map(lambda item_pair: attend_block(item_pair[1], item_pair[0], group_keys, group_values), (starts, query_blocks[first_block:first_block + per_group]))
        results.append(group_out.reshape(per_group * block_rows, HM * DH))
    attention_out = jnp.concatenate(results, axis=0)
    return (stream_out, attention_out)
```

```python
import functools

import jax
import jax.numpy as jnp
from jax import lax
from jax.experimental import pallas as pl
from jax.experimental.pallas import tpu as pltpu
from jax.sharding import PartitionSpec as P

DK = 128
CONV = 4
DH = 128
BETA_ROWS = 16
MIB = 1 << 20

eps_norm = 1e-06
bf16 = jnp.bfloat16
f32 = jnp.float32
VMEM = pl.BlockSpec(memory_space=pltpu.VMEM)
SMEM = pl.BlockSpec(memory_space=pltpu.SMEM)


def mm(left, right):
    return jnp.dot(left.astype(bf16), right.astype(bf16), preferred_element_type=f32)


def mm_nt(left, right):
    return lax.dot_general(
        left.astype(bf16), right.astype(bf16), (((1,), (1,)), ((), ())), preferred_element_type=f32
    )


def mm_tn(left, right):
    return lax.dot_general(
        left.astype(bf16), right.astype(bf16), (((0,), (0,)), ((), ())), preferred_element_type=f32
    )


def call(kernel, outs, args, scratch=(), limit=32):
    return pl.pallas_call(
        kernel,
        out_shape=[jax.ShapeDtypeStruct(shape, dtype) for shape, dtype in outs],
        in_specs=[SMEM if a.dtype == jnp.int32 else VMEM for a in args],
        out_specs=[VMEM for _ in outs],
        scratch_shapes=[pltpu.VMEM(shape, dtype) for shape, dtype in scratch],
        compiler_params=pltpu.CompilerParams(vmem_limit_bytes=limit * MIB),
    )(*args)


def partner(index, step, size):
    return index ^ step if size & (size - 1) == 0 else (size + step - index) % size


def trade(block, axis, step, size):
    route = []
    for i in range(lax.axis_size(axis)):
        base = i // size * size
        route.append((i, base + partner(i - base, step, size)))
    return lax.ppermute(block, axis, route)


def passed_along(block, axis, distance):
    devices = range(lax.axis_size(axis))
    route = [(i - distance, i) for i in devices if i - distance in devices]
    return lax.ppermute(block, axis, route)


def lanes(block_index, width=128):
    return pl.ds(pl.multiple_of(block_index * width, width), width)


def pack_kernel(heads, place, inputs, gate, beta, *packed):
    length = gate.shape[0]
    me = place[0]
    eye = (
        lax.broadcasted_iota(jnp.int32, (length, length), 0)
        == lax.broadcasted_iota(jnp.int32, (length, length), 1)
    ).astype(f32)
    head_lane = lax.broadcasted_iota(jnp.int32, (1, heads), 1)
    for step in range(heads):
        head = partner(me, step, heads)
        out = packed[step]
        for part in range(3):
            out[part * length : (part + 1) * length, :] = inputs[part, :, lanes(head)]
        out[3 * length : 4 * length, :] = gate[:, lanes(head)].astype(bf16)
        column = jnp.sum(jnp.where(head_lane == head, beta[...], 0.0), axis=1, keepdims=True)
        row = jnp.sum(column * eye, axis=0, keepdims=True)
        out[4 * length :, :] = jnp.broadcast_to(row, (BETA_ROWS, length)).astype(bf16)


def delta_kernel(heads, length, grouped, *refs):
    place, taps = refs[:2]
    blocks = refs[2 : 2 + heads]
    rest = refs[2 + heads :]
    if grouped:
        halo, start, rest = rest[0], rest[1], rest[2:]
    cores = rest[:heads]
    rest = rest[heads:]
    if grouped:
        final, rest = rest[0], rest[1:]
    wide, gates, rates, outputs = rest
    me = place[0]
    pad = 8
    for part in range(3):
        if grouped:
            wide[part, :pad, :] = halo[part]
        else:
            wide[part, :pad, :] = jnp.zeros((pad, DK), f32)
    for step in range(heads):
        where = partner(me, step, heads)
        block = blocks[step]
        at = pl.multiple_of(where * length, length)
        for part in range(3):
            wide[part, pl.ds(pl.multiple_of(at + pad, pad), length), :] = block[
                part * length : (part + 1) * length, :
            ].astype(f32)
        gates[pl.ds(at, length), :] = block[3 * length : 4 * length, :]
        rates[where] = block[4 * length :, :]

    rows = lax.broadcasted_iota(jnp.int32, (length, length), 0)
    cols = lax.broadcasted_iota(jnp.int32, (length, length), 1)
    tril = (rows >= cols).astype(bf16)
    half = length // 2
    spread = jnp.full((BETA_ROWS, DK), 1.0 / BETA_ROWS, bf16)
    chunks = range(heads)

    def convolved(part, i):
        total = jnp.zeros((length, DK), f32)
        for tap in range(CONV):
            first = i * length + pad - (CONV - 1) + tap
            total = total + taps[part, tap : tap + 1, :] * wide[part, first : first + length, :]
        return total / (1.0 + jnp.exp(-total))

    def unit(value):
        return value * lax.rsqrt(jnp.sum(value * value, axis=-1, keepdims=True) + eps_norm)

    coupling, mixing, right, finals, queries_grown, decay = [], [], [], [], [], []
    for i in chunks:
        query = (unit(convolved(0, i)) * DK ** (-0.5)).astype(bf16).astype(f32)
        key = unit(convolved(1, i)).astype(bf16).astype(f32)
        value = convolved(2, i).astype(bf16)
        log = jnp.dot(tril, gates[i * length : (i + 1) * length, :], preferred_element_type=f32)
        rate_row = rates[i][:1].astype(f32)
        rate_column = mm_tn(rates[i], spread)
        last = log[length - 1 :]
        kept, mixed = [], []
        for b in range(2):
            own = slice(b * half, (b + 1) * half)
            middle = log[b * half + half // 2 : b * half + half // 2 + 1]
            row_scale = jnp.exp(log[own] - middle)
            shrunk = key * jnp.exp(jnp.minimum(middle - log, 75.0))
            both = jnp.concatenate([query[own] * row_scale, key[own] * row_scale], axis=0)
            product = mm_nt(both, shrunk)
            mixed.append(product[:half])
            kept.append(product[half:])
        coupling.append(
            jnp.where(rows > cols, jnp.concatenate(kept, axis=0) * rate_row, 0.0).astype(bf16)
        )
        mixing.append(
            jnp.where(rows >= cols, jnp.concatenate(mixed, axis=0) * rate_row, 0.0).astype(bf16)
        )
        growth = jnp.exp(log)
        queries_grown.append(query * growth)
        right.append(jnp.concatenate([value, (key * growth).astype(bf16)], axis=1))
        finals.append((key * jnp.exp(last - log) * rate_column).astype(bf16))
        decay.append(jnp.exp(last))

    size = 1
    inverse = None
    while size < length:
        corner = (
            (rows // (2 * size) == cols // (2 * size))
            & ((rows // size) % 2 == 1)
            & ((cols // size) % 2 == 0)
        )
        corners = [jnp.where(corner, coupling[i], jnp.zeros_like(coupling[i])) for i in chunks]
        if inverse is None:
            unit_matrix = (rows == cols).astype(f32)
            inverse = [unit_matrix - corners[i].astype(f32) for i in chunks]
        else:
            short = [inverse[i].astype(bf16) for i in chunks]
            below = [mm(corners[i], short[i]) for i in chunks]
            inverse = [inverse[i] - mm(short[i], below[i]) for i in chunks]
        size *= 2

    short = [inverse[i].astype(bf16) for i in chunks]
    first = [mm(short[i], right[i]).astype(bf16) for i in chunks]
    left = [right[i].astype(f32) - first[i].astype(f32) - mm(coupling[i], first[i]) for i in chunks]
    solved = [(first[i].astype(f32) + mm(short[i], left[i])).astype(bf16) for i in chunks]

    moves = [mm_tn(solved[i], finals[i]) for i in chunks]
    mixes = [mm(mixing[i], solved[i]) for i in chunks]
    reads = [(queries_grown[i] - mixes[i][:, DK:]).astype(bf16) for i in chunks]
    state = start[...] if grouped else jnp.zeros((DK, DK), f32)
    for i in chunks:
        held = state.astype(bf16)
        outputs[i] = (mixes[i][:, :DK] + mm_nt(reads[i], held)).astype(bf16)
        state = state * decay[i] - mm(held, moves[i][DK:]) + moves[i][:DK]
    if grouped:
        final[...] = state
    for step in range(heads):
        cores[step][...] = outputs[partner(me, step, heads)]


def project_kernel(heads, parts, *refs):
    place, residual, weight = refs[:3]
    cores = refs[3 : 3 + heads]
    outs = refs[3 + heads : 3 + heads + parts]
    whole, summed = refs[3 + heads + parts :]
    me, head_me = place[0], place[1]
    for step in range(heads):
        whole[:, lanes(partner(me, step, heads))] = cores[step][...]
    summed[...] = jnp.dot(whole[...], weight[...], preferred_element_type=f32)
    share = summed.shape[0] // parts
    for step in range(parts):
        at = pl.ds(pl.multiple_of(partner(head_me, step, parts) * share, share), share)
        if step == 0:
            outs[0][...] = summed[at, :] + residual[at, :].astype(f32)
        else:
            outs[step][...] = summed[at, :].astype(bf16)


def normalized(values, gain):
    return values * lax.rsqrt(jnp.mean(values * values, axis=-1, keepdims=True) + eps_norm) * gain


def latent_kernel(parts, *refs):
    gain, latent_weight, latent_gain = refs[:3]
    partials = refs[3 : 3 + parts]
    stream, latent = refs[3 + parts :]
    total = partials[0][...]
    for step in range(1, parts):
        total = total + partials[step][...].astype(f32)
    short = total.astype(bf16)
    stream[...] = short
    normed = normalized(short.astype(f32), gain[...]).astype(bf16)
    before = jnp.dot(normed, latent_weight[...], preferred_element_type=f32)
    latent[...] = normalized(before, latent_gain[...]).astype(bf16)


def join_kernel(parts, *refs):
    place = refs[0]
    pieces = refs[1 : 1 + parts]
    out = refs[1 + parts]
    share = out.shape[0] // parts
    for step in range(parts):
        at = pl.ds(pl.multiple_of(partner(place[1], step, parts) * share, share), share)
        out[at, :] = pieces[step][...]


def query_kernel(parts, *refs):
    place, gain, query_weight, up = refs[:4]
    pieces = refs[4 : 4 + parts]
    stream, absorbed = refs[4 + parts :]
    length = stream.shape[0]
    share = length // parts
    for step in range(parts):
        at = pl.ds(pl.multiple_of(partner(place[1], step, parts) * share, share), share)
        stream[at, :] = pieces[step][...]
    normed = normalized(stream[...].astype(f32), gain[...]).astype(bf16)
    query = jnp.dot(normed, query_weight[...], preferred_element_type=f32).astype(bf16)
    for head in range(query.shape[1] // DH):
        own = slice(head * DH, (head + 1) * DH)
        absorbed[head * length : (head + 1) * length, :] = (
            mm_nt(query[:, own], up[:, own]) * DH ** (-0.5)
        ).astype(bf16)


def attend_kernel(count, *refs):
    place, absorbed, up = refs[:3]
    latents = refs[3 : 3 + count]
    out, scores, mixed = refs[3 + count :]
    length = latents[0].shape[0]
    heads = absorbed.shape[0] // length
    me = place[2]
    rows = lax.broadcasted_iota(jnp.int32, (length, length), 0)
    cols = lax.broadcasted_iota(jnp.int32, (length, length), 1)
    causal = jnp.concatenate([rows >= cols] * heads, axis=0)
    peak = None
    for step in range(count):
        part = mm_nt(absorbed[...], latents[step][...])
        if step == 0:
            part = jnp.where(causal, part, -1e30)
        else:
            part = jnp.where(step <= me, part, -1e30)
        scores[:, step * length : (step + 1) * length] = part
        top = jnp.max(part, axis=-1, keepdims=True)
        peak = top if peak is None else jnp.maximum(peak, top)
    total = None
    for step in range(count):
        weights = jnp.exp(scores[:, step * length : (step + 1) * length] - peak)
        added = jnp.sum(weights, axis=-1, keepdims=True)
        share = mm(weights, latents[step][...])
        if total is None:
            total = added
            mixed[...] = share
        else:
            total = total + added
            mixed[...] += share
    for head in range(heads):
        own = slice(head * length, (head + 1) * length)
        value = slice((heads + head) * DH, (heads + head + 1) * DH)
        spread = (mixed[own, :] / total[own, :]).astype(bf16)
        out[:, head * DH : (head + 1) * DH] = jnp.dot(
            spread, up[:, value], preferred_element_type=f32
        ).astype(bf16)


def per_device(
    kda_inputs,
    gate_log,
    beta,
    conv_weight,
    kda_out_weight,
    residual,
    norm_gain,
    latent_weight,
    latent_gain,
    query_weight,
    up_weight,
):
    length, width = residual.shape
    heads = beta.shape[1]
    count, parts = lax.axis_size("ctx"), lax.axis_size("head")
    groups = count // heads
    ctx_me = lax.axis_index("ctx").astype(jnp.int32)
    place = jnp.stack([ctx_me % heads, lax.axis_index("head").astype(jnp.int32), ctx_me])

    message = (4 * length + BETA_ROWS, DK)
    packed = call(
        functools.partial(pack_kernel, heads),
        [(message, bf16)] * heads,
        [place, kda_inputs, gate_log, beta],
    )
    blocks = [packed[0]] + [trade(packed[k], "ctx", k, heads) for k in range(1, heads)]
    taps = lax.dynamic_slice_in_dim(conv_weight, place[0] * DK, DK, axis=2)
    core_outs = [((length, DK), bf16)] * heads
    scratch = [
        ((3, heads * length + 8, DK), f32),
        ((heads * length, DK), bf16),
        ((heads, BETA_ROWS, length), bf16),
        ((heads, length, DK), bf16),
    ]
    if groups == 1:
        cores = call(
            functools.partial(delta_kernel, heads, length, False),
            core_outs,
            [place, taps] + blocks,
            scratch,
        )
    else:
        tails = jnp.stack([b[: 3 * length].reshape(3, length, DK)[:, length - 8 :] for b in blocks])
        order = jnp.stack([partner(heads - 1, k, heads) == place[0] for k in range(heads)])
        tail = jnp.sum(jnp.where(order[:, None, None, None], tails, 0).astype(f32), axis=0)
        halo = passed_along(tail, "ctx", heads)

        def run(start):
            return call(
                functools.partial(delta_kernel, heads, length, True),
                core_outs + [((DK, DK), f32)],
                [place, taps] + blocks + [halo, start],
                scratch,
            )

        def relay(step_index, start):
            return passed_along(run(start)[heads], "ctx", heads)

        start = lax.fori_loop(0, groups - 1, relay, jnp.zeros((DK, DK), f32))
        cores = run(start)[:heads]

    cores = [cores[0]] + [trade(cores[k], "ctx", k, heads) for k in range(1, heads)]
    share = length // parts
    partials = call(
        functools.partial(project_kernel, heads, parts),
        [((share, width), f32)] + [((share, width), bf16)] * (parts - 1),
        [place, residual, kda_out_weight] + list(cores),
        [((length, heads * DK), bf16), ((length, width), f32)],
    )
    partials = [partials[0]] + [trade(partials[k], "head", k, parts) for k in range(1, parts)]
    stream_rows, latent_rows = call(
        functools.partial(latent_kernel, parts),
        [((share, width), bf16), ((share, latent_weight.shape[1]), bf16)],
        [norm_gain[None], latent_weight, latent_gain[None]] + partials,
    )
    latent_parts = [latent_rows] + [trade(latent_rows, "head", k, parts) for k in range(1, parts)]
    stream_parts = [stream_rows] + [trade(stream_rows, "head", k, parts) for k in range(1, parts)]
    latent = call(
        functools.partial(join_kernel, parts),
        [((length, latent_weight.shape[1]), bf16)],
        [place] + latent_parts,
    )[0]
    latents = [latent] + [passed_along(latent, "ctx", k) for k in range(1, count)]
    up = up_weight.reshape(up_weight.shape[0], -1)
    heads_mla = query_weight.shape[1] // DH
    stream_out, absorbed = call(
        functools.partial(query_kernel, parts),
        [((length, width), bf16), ((heads_mla * length, up.shape[0]), bf16)],
        [place, norm_gain[None], query_weight, up] + stream_parts,
    )
    attention_out = call(
        functools.partial(attend_kernel, count),
        [((length, heads_mla * DH), bf16)],
        [place, absorbed, up] + latents,
        [
            ((heads_mla * length, count * length), f32),
            ((heads_mla * length, up.shape[0]), f32),
        ],
        48,
    )[0]
    return (stream_out, attention_out)


def solution(mesh):
    in_specs = (
        P(None, "ctx", "head"),
        P("ctx", "head"),
        P("ctx", "head"),
        P(None, None, "head"),
        P("head", None),
        P("ctx", None),
        P(),
        P(),
        P(),
        P(None, "head"),
        P(None, None, "head"),
    )
    out_specs = (P("ctx", None), P("ctx", "head"))
    return jax.shard_map(
        per_device, mesh=mesh, in_specs=in_specs, out_specs=out_specs, check_vma=False
    )
```

```python
import functools

import jax
import jax.numpy as jnp
from jax import lax
from jax.experimental import pallas as pl
from jax.experimental.pallas import tpu as pltpu
from jax.sharding import PartitionSpec as P

DK = 128
CONV = 4
DH = 128
HALO = 16
EXTRA = 16
MIB = 1 << 20

eps_norm = 1e-06
bf16 = jnp.bfloat16
f32 = jnp.float32
VMEM = pl.BlockSpec(memory_space=pltpu.VMEM)
SMEM = pl.BlockSpec(memory_space=pltpu.SMEM)
HBM = pl.BlockSpec(memory_space=pltpu.HBM)


def mm(left, right):
    return jnp.dot(left.astype(bf16), right.astype(bf16), preferred_element_type=f32)


def mm_nt(left, right):
    return lax.dot_general(
        left.astype(bf16), right.astype(bf16), (((1,), (1,)), ((), ())), preferred_element_type=f32
    )


def mm_tn(left, right):
    return lax.dot_general(
        left.astype(bf16), right.astype(bf16), (((0,), (0,)), ((), ())), preferred_element_type=f32
    )


def call(kernel, outs, args, scratch=(), limit=32, stored=(), copies=0, cost=1.0):
    scratch_shapes = [pltpu.VMEM(shape, dtype) for shape, dtype in scratch]
    if copies:
        scratch_shapes.append(pltpu.SemaphoreType.DMA((copies,)))
    return pl.pallas_call(
        kernel,
        out_shape=[jax.ShapeDtypeStruct(shape, dtype) for shape, dtype in outs],
        in_specs=[
            HBM if i in stored else SMEM if a.dtype == jnp.int32 else VMEM
            for i, a in enumerate(args)
        ],
        out_specs=[VMEM for _ in outs],
        scratch_shapes=scratch_shapes,
        compiler_params=pltpu.CompilerParams(vmem_limit_bytes=limit * MIB),
        cost_estimate=pl.CostEstimate(flops=int(cost * 1e9), bytes_accessed=0, transcendentals=0),
    )(*args)


def partner(index, step, size):
    return index ^ step if size & (size - 1) == 0 else (size + step - index) % size


def trade(block, axis, step, size):
    route = []
    for i in range(lax.axis_size(axis)):
        base = i // size * size
        route.append((i, base + partner(i - base, step, size)))
    return lax.ppermute(block, axis, route)


def passed_along(block, axis, distance):
    count = lax.axis_size(axis)
    return lax.ppermute(block, axis, [(i, (i + distance) % count) for i in range(count)])


def lanes(block_index, width=128):
    return pl.ds(pl.multiple_of(block_index * width, width), width)


def split_cores(place):
    return place[0] // 2, place[0] % 2


def load_kernel(stored_inputs, stored_gate, stored_taps, inputs, log, taps, gate, sems):
    moves = [
        pltpu.make_async_copy(stored_gate, gate, sems.at[0]),
        pltpu.make_async_copy(stored_inputs, inputs, sems.at[1]),
        pltpu.make_async_copy(stored_taps, taps, sems.at[2]),
    ]
    for move in moves:
        move.start()
    length = gate.shape[0]
    rows = lax.broadcasted_iota(jnp.int32, (length, length), 0)
    cols = lax.broadcasted_iota(jnp.int32, (length, length), 1)
    tril = (rows >= cols).astype(bf16)
    moves[0].wait()
    high = gate[...].astype(bf16)
    low = gate[...] - high.astype(f32)
    log[...] = mm(tril, high) + mm(tril, low)
    moves[1].wait()
    moves[2].wait()


def local_kernel(heads, *refs):
    place, inputs, halo, logs, beta, taps = refs[:6]
    kept, sent, reads, intra = refs[6:10]
    wide, maps = refs[10:]
    length = logs.shape[0]
    pad = wide.shape[1] - length
    before = halo[:, halo.shape[1] - pad :, :].astype(f32)
    wide[:, :pad, :] = jnp.where(place[2] == 0, 0.0, before)
    wide[:, pad:, :] = inputs[...].astype(f32)

    rows = lax.broadcasted_iota(jnp.int32, (length, length), 0)
    cols = lax.broadcasted_iota(jnp.int32, (length, length), 1)
    eye = (rows == cols).astype(f32)
    half = length // 2
    chunks = range(heads)

    def convolved(part, i):
        own = slice(i * DK, (i + 1) * DK)
        total = jnp.zeros((length, DK), f32)
        for tap in range(CONV):
            first = pad - (CONV - 1) + tap
            total = total + taps[part, tap : tap + 1, own] * wide[part, first : first + length, own]
        return total / (1.0 + jnp.exp(-total))

    def unit(value):
        return value * lax.rsqrt(jnp.sum(value * value, axis=-1, keepdims=True) + eps_norm)

    coupling, mixing, right, finals, queries_grown, decay = [], [], [], [], [], []
    for i in chunks:
        own_head = slice(i * DK, (i + 1) * DK)
        query = (unit(convolved(0, i)) * DK ** (-0.5)).astype(bf16).astype(f32)
        key = unit(convolved(1, i)).astype(bf16).astype(f32)
        value = convolved(2, i).astype(bf16)
        log = logs[:, own_head]
        rate_row = beta[i : i + 1, :]
        rate_column = jnp.sum(rate_row * eye, axis=1, keepdims=True)
        last = log[length - 1 :]
        kept_parts, mixed_parts = [], []
        for b in range(2):
            own = slice(b * half, (b + 1) * half)
            middle = log[b * half + half // 2 : b * half + half // 2 + 1]
            row_scale = jnp.exp(log[own] - middle)
            shrunk = key * jnp.exp(jnp.minimum(middle - log, 75.0))
            both = jnp.concatenate([query[own] * row_scale, key[own] * row_scale], axis=0)
            product = mm_nt(both, shrunk)
            mixed_parts.append(product[:half])
            kept_parts.append(product[half:])
        coupling.append(
            jnp.where(rows > cols, jnp.concatenate(kept_parts, axis=0) * rate_row, 0.0).astype(bf16)
        )
        mixing.append(
            jnp.where(rows >= cols, jnp.concatenate(mixed_parts, axis=0) * rate_row, 0.0).astype(
                bf16
            )
        )
        growth = jnp.exp(log)
        queries_grown.append(query * growth)
        right.append(jnp.concatenate([value, (key * growth).astype(bf16)], axis=1))
        finals.append((key * jnp.exp(last - log) * rate_column).astype(bf16))
        decay.append(jnp.exp(last))

    size = 1
    inverse = None
    while size < length:
        corner = (
            (rows // (2 * size) == cols // (2 * size))
            & ((rows // size) % 2 == 1)
            & ((cols // size) % 2 == 0)
        )
        corners = [jnp.where(corner, coupling[i], jnp.zeros_like(coupling[i])) for i in chunks]
        if inverse is None:
            inverse = [eye - corners[i].astype(f32) for i in chunks]
        else:
            short = [inverse[i].astype(bf16) for i in chunks]
            below = [mm(corners[i], short[i]) for i in chunks]
            inverse = [inverse[i] - mm(short[i], below[i]) for i in chunks]
        size *= 2

    short = [inverse[i].astype(bf16) for i in chunks]
    first = [mm(short[i], right[i]).astype(bf16) for i in chunks]
    left = [right[i].astype(f32) - first[i].astype(f32) - mm(coupling[i], first[i]) for i in chunks]
    solved = [(first[i].astype(f32) + mm(short[i], left[i])).astype(bf16) for i in chunks]

    for i in chunks:
        own_head = slice(i * DK, (i + 1) * DK)
        maps[i, : 2 * DK, :] = mm_tn(solved[i], finals[i]).astype(bf16)
        high = decay[i].astype(bf16)
        low = (decay[i] - high.astype(f32)).astype(bf16)
        maps[i, 2 * DK :, :] = jnp.concatenate(
            [jnp.broadcast_to(high, (EXTRA // 2, DK)), jnp.broadcast_to(low, (EXTRA // 2, DK))],
            axis=0,
        )
        mixes = mm(mixing[i], solved[i])
        intra[:, own_head] = mixes[:, :DK]
        reads[:, own_head] = (queries_grown[i] - mixes[:, DK:]).astype(bf16)
    _, core = split_cores(place)
    for pair in range(heads // 2):
        kept[pair] = maps[2 * pair + core]
        sent[pair] = maps[2 * pair + 1 - core]


def parts_of(state_map):
    extra = state_map[2 * DK :].astype(f32)
    decay = extra[:1] + extra[EXTRA // 2 : EXTRA // 2 + 1]
    return state_map[:DK], state_map[DK : 2 * DK], decay


def compose_kernel(pairs, place, kept, got, *refs):
    outs, (maps,) = refs[:pairs], refs[pairs:]
    chip, core = split_cores(place)
    eye = (
        lax.broadcasted_iota(jnp.int32, (DK, DK), 0) == lax.broadcasted_iota(jnp.int32, (DK, DK), 1)
    ).astype(f32)
    for pair in range(pairs):
        mine, other = kept[pair], got[pair]
        offset_a, move_a, decay_a = parts_of(jnp.where(core == 0, mine, other))
        offset_b, move_b, decay_b = parts_of(jnp.where(core == 0, other, mine))
        product = mm(jnp.concatenate([offset_a, move_a], axis=0), move_b)
        column = jnp.sum(eye * decay_a, axis=1, keepdims=True)
        maps[pair, :DK, :] = (
            offset_a.astype(f32) * decay_b - product[:DK] + offset_b.astype(f32)
        ).astype(bf16)
        maps[pair, DK : 2 * DK, :] = (
            move_a.astype(f32) * decay_b + column * move_b.astype(f32) - product[DK:]
        ).astype(bf16)
        decay = decay_a * decay_b
        high = decay.astype(bf16)
        low = (decay - high.astype(f32)).astype(bf16)
        maps[pair, 2 * DK :, :] = jnp.concatenate(
            [jnp.broadcast_to(high, (EXTRA // 2, DK)), jnp.broadcast_to(low, (EXTRA // 2, DK))],
            axis=0,
        )
    for step in range(pairs):
        outs[step][...] = maps[partner(chip, step, pairs)]


def apply_map(state, state_map):
    offset, move, decay = parts_of(state_map)
    return state.astype(f32) * decay - mm(state, move) + offset.astype(f32)


def scan_kernel(pairs, grouped, *refs):
    place, blocks, rest = refs[0], refs[1 : 1 + pairs], refs[1 + pairs :]
    if grouped:
        start, rest = rest[0], rest[1:]
    outs, rest = rest[:pairs], rest[pairs:]
    if grouped:
        final, rest = rest[0], rest[1:]
    maps, starts = rest
    chip, _ = split_cores(place)
    for step in range(pairs):
        maps[partner(chip, step, pairs)] = blocks[step][...]
    state = start[...] if grouped else jnp.zeros((DK, DK), f32)
    for i in range(pairs):
        starts[i] = state.astype(bf16)
        if i < pairs - 1 or grouped:
            if i == 0 and not grouped:
                state = maps[i, :DK, :].astype(f32)
            else:
                state = apply_map(state, maps[i])
    if grouped:
        final[...] = state
    for step in range(pairs):
        outs[step][...] = starts[partner(chip, step, pairs)]


def share_kernel(pairs, place, kept, got, *refs):
    starts, (mine, other) = refs[:pairs], refs[pairs:]
    chip, core = split_cores(place)
    for step in range(pairs):
        pair = partner(chip, step, pairs)
        state = starts[step][...]
        later = apply_map(state, jnp.where(core == 0, kept[pair], got[pair])).astype(bf16)
        mine[pair] = jnp.where(core == 0, state, later)
        other[pair] = jnp.where(core == 0, later, state)


def project_kernel(parts, *refs):
    place, residual, weight, reads, intra, mine, other = refs[:7]
    outs = refs[7 : 7 + parts]
    whole, summed = refs[7 + parts :]
    _, core = split_cores(place)
    head_me = place[1]
    for pair in range(mine.shape[0]):
        for states, head in ((mine, 2 * pair + core), (other, 2 * pair + 1 - core)):
            own = lanes(head)
            whole[:, own] = (intra[:, own] + mm_nt(reads[:, own], states[pair])).astype(bf16)
    summed[...] = jnp.dot(whole[...], weight[...], preferred_element_type=f32)
    share = summed.shape[0] // parts
    for step in range(parts):
        at = pl.ds(pl.multiple_of(partner(head_me, step, parts) * share, share), share)
        if step == 0:
            outs[0][...] = summed[at, :] + residual[at, :].astype(f32)
        else:
            outs[step][...] = summed[at, :].astype(bf16)


def normalized(values, gain):
    return values * lax.rsqrt(jnp.mean(values * values, axis=-1, keepdims=True) + eps_norm) * gain


def latent_kernel(parts, *refs):
    gain, latent_weight, latent_gain = refs[:3]
    partials = refs[3 : 3 + parts]
    stream, latent = refs[3 + parts :]
    total = partials[0][...]
    for step in range(1, parts):
        total = total + partials[step][...].astype(f32)
    short = total.astype(bf16)
    stream[...] = short
    normed = normalized(short.astype(f32), gain[...]).astype(bf16)
    before = jnp.dot(normed, latent_weight[...], preferred_element_type=f32)
    latent[...] = normalized(before, latent_gain[...]).astype(bf16)


def join_kernel(parts, *refs):
    place = refs[0]
    pieces = refs[1 : 1 + parts]
    out = refs[1 + parts]
    share = out.shape[0] // parts
    for step in range(parts):
        at = pl.ds(pl.multiple_of(partner(place[1], step, parts) * share, share), share)
        out[at, :] = pieces[step][...]


def query_kernel(parts, *refs):
    place, gain, query_weight, up = refs[:4]
    pieces = refs[4 : 4 + parts]
    stream, absorbed = refs[4 + parts :]
    length = stream.shape[0]
    share = length // parts
    for step in range(parts):
        at = pl.ds(pl.multiple_of(partner(place[1], step, parts) * share, share), share)
        stream[at, :] = pieces[step][...]
    normed = normalized(stream[...].astype(f32), gain[...]).astype(bf16)
    query = jnp.dot(normed, query_weight[...], preferred_element_type=f32).astype(bf16)
    for head in range(query.shape[1] // DH):
        own = slice(head * DH, (head + 1) * DH)
        absorbed[head * length : (head + 1) * length, :] = (
            mm_nt(query[:, own], up[:, own]) * DH ** (-0.5)
        ).astype(bf16)


def attend_kernel(order, *refs):
    place, absorbed, up = refs[:3]
    latents = refs[3 : 3 + len(order)]
    out, scores, mixed = refs[3 + len(order) :]
    length = latents[0].shape[0]
    heads = absorbed.shape[0] // length
    me = place[2]
    rows = lax.broadcasted_iota(jnp.int32, (length, length), 0)
    cols = lax.broadcasted_iota(jnp.int32, (length, length), 1)
    causal = jnp.concatenate([rows >= cols] * heads, axis=0)
    peak = None
    for place_in, distance in enumerate(order):
        part = mm_nt(absorbed[...], latents[place_in][...])
        allowed = causal if distance == 0 else (me ^ distance) < me
        part = jnp.where(allowed, part, -1e30)
        scores[:, place_in * length : (place_in + 1) * length] = part
        top = jnp.max(part, axis=-1, keepdims=True)
        peak = top if peak is None else jnp.maximum(peak, top)
    total = None
    for place_in in range(len(order)):
        weights = jnp.exp(scores[:, place_in * length : (place_in + 1) * length] - peak)
        added = jnp.sum(weights, axis=-1, keepdims=True)
        share = mm(weights, latents[place_in][...])
        if total is None:
            total = added
            mixed[...] = share
        else:
            total = total + added
            mixed[...] += share
    for head in range(heads):
        own = slice(head * length, (head + 1) * length)
        value = slice((heads + head) * DH, (heads + head + 1) * DH)
        spread = (mixed[own, :] / total[own, :]).astype(bf16)
        out[:, head * DH : (head + 1) * DH] = jnp.dot(
            spread, up[:, value], preferred_element_type=f32
        ).astype(bf16)


def far_first(count):
    return sorted(range(1, count), key=lambda step: (-bin(step).count("1"), -step))


def per_device(
    kda_inputs,
    gate_log,
    beta,
    conv_weight,
    kda_out_weight,
    residual,
    norm_gain,
    latent_weight,
    latent_gain,
    query_weight,
    up_weight,
):
    length, width = residual.shape
    heads = beta.shape[1]
    pairs = heads // 2
    count, parts = lax.axis_size("ctx"), lax.axis_size("head")
    groups = count // heads
    ctx_me = lax.axis_index("ctx").astype(jnp.int32)
    place = jnp.stack([ctx_me % heads, lax.axis_index("head").astype(jnp.int32), ctx_me])

    halo = passed_along(kda_inputs[:, length - HALO :, :], "ctx", 1)
    inputs, logs, taps = call(
        load_kernel,
        [(kda_inputs.shape, bf16), (gate_log.shape, f32), (conv_weight.shape, f32)],
        [kda_inputs, gate_log, conv_weight],
        [(gate_log.shape, f32)],
        24,
        stored=(0, 1, 2),
        copies=3,
    )
    map_shape = (2 * DK + EXTRA, DK)
    kept, sent, reads, intra = call(
        functools.partial(local_kernel, heads),
        [
            ((pairs,) + map_shape, bf16),
            ((pairs,) + map_shape, bf16),
            ((length, heads * DK), bf16),
            ((length, heads * DK), f32),
        ],
        [place, inputs, halo, logs, beta.T, taps],
        [((3, length + 8, heads * DK), f32), ((heads,) + map_shape, bf16)],
        16,
        cost=6.0,
    )

    got = trade(sent, "ctx", 1, heads)
    chip_maps = call(
        functools.partial(compose_kernel, pairs),
        [(map_shape, bf16)] * pairs,
        [place, kept, got],
        [((pairs,) + map_shape, bf16)],
        8,
    )

    def across_chips(pieces):
        moved = {step: trade(pieces[step], "ctx", 2 * step, heads) for step in far_first(pairs)}
        return [pieces[0]] + [moved[step] for step in range(1, pairs)]

    chip_maps = across_chips(chip_maps)
    state_outs = [((DK, DK), bf16)] * pairs
    scratch = [((pairs,) + map_shape, bf16), ((pairs, DK, DK), bf16)]
    if groups == 1:
        starts = call(
            functools.partial(scan_kernel, pairs, False), state_outs, [place] + chip_maps, scratch, 8
        )
    else:

        def run(start):
            return call(
                functools.partial(scan_kernel, pairs, True),
                state_outs + [((DK, DK), f32)],
                [place] + chip_maps + [start],
                scratch,
                8,
            )

        def relay(step_index, start):
            arrived = passed_along(run(start)[pairs], "ctx", heads)
            return jnp.where(ctx_me < heads, 0.0, arrived)

        start = lax.fori_loop(0, groups - 1, relay, jnp.zeros((DK, DK), f32))
        starts = run(start)[:pairs]
    starts = across_chips(starts)
    mine, other = call(
        functools.partial(share_kernel, pairs),
        [((pairs, DK, DK), bf16)] * 2,
        [place, kept, got] + starts,
        limit=8,
    )
    other = trade(other, "ctx", 1, heads)

    share = length // parts
    partials = call(
        functools.partial(project_kernel, parts),
        [((share, width), f32)] + [((share, width), bf16)] * (parts - 1),
        [place, residual, kda_out_weight, reads, intra, mine, other],
        [((length, heads * DK), bf16), ((length, width), f32)],
        16,
    )

    def across_heads(pieces):
        moved = {step: trade(pieces[step], "head", step, parts) for step in far_first(parts)}
        return [pieces[0]] + [moved[step] for step in range(1, parts)]

    partials = across_heads(partials)
    stream_rows, latent_rows = call(
        functools.partial(latent_kernel, parts),
        [((share, width), bf16), ((share, latent_weight.shape[1]), bf16)],
        [norm_gain[None], latent_weight, latent_gain[None]] + partials,
        limit=16,
    )
    latent_parts = across_heads([latent_rows] * parts)
    stream_parts = across_heads([stream_rows] * parts)
    latent = call(
        functools.partial(join_kernel, parts),
        [((length, latent_weight.shape[1]), bf16)],
        [place] + latent_parts,
        limit=8,
    )[0]

    order, latents = [0], [latent]
    for step in far_first(count // 2):
        order.append(2 * step)
        latents.append(trade(latent, "ctx", 2 * step, count))
    for position in range(len(order)):
        order.append(order[position] + 1)
        latents.append(trade(latents[position], "ctx", 1, 2))
    up = up_weight.reshape(up_weight.shape[0], -1)
    heads_mla = query_weight.shape[1] // DH
    stream_out, absorbed = call(
        functools.partial(query_kernel, parts),
        [((length, width), bf16), ((heads_mla * length, up.shape[0]), bf16)],
        [place, norm_gain[None], query_weight, up] + stream_parts,
        limit=16,
    )
    attention_out = call(
        functools.partial(attend_kernel, tuple(order)),
        [((length, heads_mla * DH), bf16)],
        [place, absorbed, up] + latents,
        [
            ((heads_mla * length, count * length), f32),
            ((heads_mla * length, up.shape[0]), f32),
        ],
        12 + count * length * heads_mla * length * 8 // MIB,
    )[0]
    return (stream_out, attention_out)


def solution(mesh):
    in_specs = (
        P(None, "ctx", "head"),
        P("ctx", "head"),
        P("ctx", "head"),
        P(None, None, "head"),
        P("head", None),
        P("ctx", None),
        P(),
        P(),
        P(),
        P(None, "head"),
        P(None, None, "head"),
    )
    out_specs = (P("ctx", None), P("ctx", "head"))
    return jax.shard_map(
        per_device, mesh=mesh, in_specs=in_specs, out_specs=out_specs, check_vma=False
    )
```

```python
import functools

import jax
import jax.numpy as jnp
from jax import lax
from jax.experimental import pallas as pl
from jax.experimental.pallas import tpu as pltpu
from jax.sharding import PartitionSpec as P

DK = 128
CONV = 4
DH = 128
HALO = 16
EXTRA = 16
MIB = 1 << 20

eps_norm = 1e-06
bf16 = jnp.bfloat16
f32 = jnp.float32
VMEM = pl.BlockSpec(memory_space=pltpu.VMEM)
SMEM = pl.BlockSpec(memory_space=pltpu.SMEM)
HBM = pl.BlockSpec(memory_space=pltpu.HBM)


def mm(left, right):
    return jnp.dot(left.astype(bf16), right.astype(bf16), preferred_element_type=f32)


def mm_nt(left, right):
    return lax.dot_general(
        left.astype(bf16), right.astype(bf16), (((1,), (1,)), ((), ())), preferred_element_type=f32
    )


def mm_tn(left, right):
    return lax.dot_general(
        left.astype(bf16), right.astype(bf16), (((0,), (0,)), ((), ())), preferred_element_type=f32
    )


def call(kernel, outs, args, scratch=(), limit=32, stored=(), copies=0, cost=1.0):
    scratch_shapes = [pltpu.VMEM(shape, dtype) for shape, dtype in scratch]
    if copies:
        scratch_shapes.append(pltpu.SemaphoreType.DMA((copies,)))
    return pl.pallas_call(
        kernel,
        out_shape=[jax.ShapeDtypeStruct(shape, dtype) for shape, dtype in outs],
        in_specs=[
            HBM if i in stored else SMEM if a.dtype == jnp.int32 else VMEM
            for i, a in enumerate(args)
        ],
        out_specs=[VMEM for _ in outs],
        scratch_shapes=scratch_shapes,
        compiler_params=pltpu.CompilerParams(vmem_limit_bytes=limit * MIB),
        cost_estimate=pl.CostEstimate(flops=int(cost * 1e9), bytes_accessed=0, transcendentals=0),
    )(*args)


def partner(index, step, size):
    return index ^ step if size & (size - 1) == 0 else (size + step - index) % size


def trade(block, axis, step, size):
    route = []
    for i in range(lax.axis_size(axis)):
        base = i // size * size
        route.append((i, base + partner(i - base, step, size)))
    return lax.ppermute(block, axis, route)


def passed_along(block, axis, distance):
    count = lax.axis_size(axis)
    return lax.ppermute(block, axis, [(i, (i + distance) % count) for i in range(count)])


def lanes(block_index, width=128):
    return pl.ds(pl.multiple_of(block_index * width, width), width)


def split_cores(place):
    return place[0] // 2, place[0] % 2


def load_kernel(stored_inputs, stored_gate, stored_taps, inputs, log, taps, gate, sems):
    moves = [
        pltpu.make_async_copy(stored_gate, gate, sems.at[0]),
        pltpu.make_async_copy(stored_inputs, inputs, sems.at[1]),
        pltpu.make_async_copy(stored_taps, taps, sems.at[2]),
    ]
    for move in moves:
        move.start()
    length = gate.shape[0]
    rows = lax.broadcasted_iota(jnp.int32, (length, length), 0)
    cols = lax.broadcasted_iota(jnp.int32, (length, length), 1)
    tril = (rows >= cols).astype(bf16)
    moves[0].wait()
    high = gate[...].astype(bf16)
    low = gate[...] - high.astype(f32)
    log[...] = mm(tril, high) + mm(tril, low)
    moves[1].wait()
    moves[2].wait()


def put_wide(wide, place, inputs, halo, own, part):
    pad = wide.shape[0] - inputs.shape[1]
    before = halo[part, halo.shape[1] - pad :, own].astype(f32)
    wide[:pad, :] = jnp.where(place[2] == 0, 0.0, before)
    wide[pad:, :] = inputs[part, :, own].astype(f32)


def convolved(wide, taps, own, part):
    length = wide.shape[0] - 8
    total = jnp.zeros((length, DK), f32)
    for tap in range(CONV):
        first = 8 - (CONV - 1) + tap
        total = total + taps[part, tap : tap + 1, own] * wide[first : first + length, :]
    return total / (1.0 + jnp.exp(-total))


def unit(value):
    return value * lax.rsqrt(jnp.sum(value * value, axis=-1, keepdims=True) + eps_norm)


def spans(log):
    half = log.shape[0] // 2
    for b in range(2):
        middle = log[b * half + half // 2 : b * half + half // 2 + 1]
        yield b, slice(b * half, (b + 1) * half), middle


def side_heads(place, pairs):
    _, core = split_cores(place)
    return [2 * i + core for i in range(pairs)] + [2 * i + 1 - core for i in range(pairs)]


def map_kernel(place, inputs, halo, logs, beta, taps, kept, sent, solutions, shrunk, wide):
    length = logs.shape[0]
    pairs = kept.shape[0]
    chunks = range(2 * pairs)
    heads = side_heads(place, pairs)
    lane = [lanes(head) for head in heads]
    rows = lax.broadcasted_iota(jnp.int32, (length, length), 0)
    cols = lax.broadcasted_iota(jnp.int32, (length, length), 1)
    eye = (rows == cols).astype(f32)
    for i in chunks:
        for part in (1, 2):
            put_wide(wide.at[i, part - 1], place, inputs, halo, lane[i], part)

    coupling, right, finals, decay = [], [], [], []
    for i in chunks:
        key = unit(convolved(wide.at[i, 0], taps, lane[i], 1)).astype(bf16).astype(f32)
        value = convolved(wide.at[i, 1], taps, lane[i], 2).astype(bf16)
        log = logs[:, lane[i]]
        rate_row = beta[pl.ds(heads[i], 1), :]
        rate_column = jnp.sum(rate_row * eye, axis=1, keepdims=True)
        last = log[length - 1 :]
        products = []
        for b, own, middle in spans(log):
            shrunk[i, b] = (key * jnp.exp(jnp.minimum(middle - log, 75.0))).astype(bf16)
            products.append(mm_nt(key[own] * jnp.exp(log[own] - middle), shrunk[i, b]))
        coupling.append(
            jnp.where(rows > cols, jnp.concatenate(products, axis=0) * rate_row, 0.0).astype(bf16)
        )
        right.append(jnp.concatenate([value, (key * jnp.exp(log)).astype(bf16)], axis=1))
        finals.append((key * jnp.exp(last - log) * rate_column).astype(bf16))
        decay.append(jnp.exp(last))

    size = 1
    inverse = None
    while size < length:
        corner = (
            (rows // (2 * size) == cols // (2 * size))
            & ((rows // size) % 2 == 1)
            & ((cols // size) % 2 == 0)
        )
        corners = [jnp.where(corner, coupling[i], jnp.zeros_like(coupling[i])) for i in chunks]
        if inverse is None:
            inverse = [eye - corners[i].astype(f32) for i in chunks]
        else:
            short = [inverse[i].astype(bf16) for i in chunks]
            below = [mm(corners[i], short[i]) for i in chunks]
            inverse = [inverse[i] - mm(short[i], below[i]) for i in chunks]
        size *= 2

    short = [inverse[i].astype(bf16) for i in chunks]
    first = [mm(short[i], right[i]).astype(bf16) for i in chunks]
    left = [right[i].astype(f32) - first[i].astype(f32) - mm(coupling[i], first[i]) for i in chunks]
    solved = [(first[i].astype(f32) + mm(short[i], left[i])).astype(bf16) for i in chunks]
    for i in chunks:
        solutions[i] = solved[i]
        maps = kept if i < pairs else sent
        put_map(maps, i % pairs, mm_tn(solved[i], finals[i]), decay[i])


def put_map(maps, i, offset_and_move, decay):
    maps[i, : 2 * DK, :] = offset_and_move.astype(bf16)
    high = decay.astype(bf16)
    low = (decay - high.astype(f32)).astype(bf16)
    maps[i, 2 * DK :, :] = jnp.concatenate(
        [jnp.broadcast_to(high, (EXTRA // 2, DK)), jnp.broadcast_to(low, (EXTRA // 2, DK))],
        axis=0,
    )


def read_kernel(place, inputs, halo, logs, beta, taps, solutions, shrunk, reads, intra, wide):
    length = logs.shape[0]
    rows = lax.broadcasted_iota(jnp.int32, (length, length), 0)
    cols = lax.broadcasted_iota(jnp.int32, (length, length), 1)
    for i, head in enumerate(side_heads(place, solutions.shape[0] // 2)):
        lane = lanes(head)
        put_wide(wide.at[i], place, inputs, halo, lane, 0)
        query = unit(convolved(wide.at[i], taps, lane, 0)) * DK ** (-0.5)
        query = query.astype(bf16).astype(f32)
        log = logs[:, lane]
        products = [
            mm_nt(query[own] * jnp.exp(log[own] - middle), shrunk[i, b])
            for b, own, middle in spans(log)
        ]
        rate_row = beta[pl.ds(head, 1), :]
        mixing = jnp.where(rows >= cols, jnp.concatenate(products, axis=0) * rate_row, 0.0)
        mixes = mm(mixing, solutions[i])
        intra[:, lane] = mixes[:, :DK]
        reads[:, lane] = (query * jnp.exp(log) - mixes[:, DK:]).astype(bf16)


def parts_of(state_map):
    extra = state_map[2 * DK :].astype(f32)
    decay = extra[:1] + extra[EXTRA // 2 : EXTRA // 2 + 1]
    return state_map[:DK], state_map[DK : 2 * DK], decay


def compose_kernel(pairs, place, kept, got, *refs):
    outs, (maps,) = refs[:pairs], refs[pairs:]
    chip, core = split_cores(place)
    eye = (
        lax.broadcasted_iota(jnp.int32, (DK, DK), 0) == lax.broadcasted_iota(jnp.int32, (DK, DK), 1)
    ).astype(f32)
    for pair in range(pairs):
        mine, other = kept[pair], got[pair]
        offset_a, move_a, decay_a = parts_of(jnp.where(core == 0, mine, other))
        offset_b, move_b, decay_b = parts_of(jnp.where(core == 0, other, mine))
        product = mm(jnp.concatenate([offset_a, move_a], axis=0), move_b)
        column = jnp.sum(eye * decay_a, axis=1, keepdims=True)
        offset = offset_a.astype(f32) * decay_b - product[:DK] + offset_b.astype(f32)
        move = move_a.astype(f32) * decay_b + column * move_b.astype(f32) - product[DK:]
        put_map(maps, pair, jnp.concatenate([offset, move], axis=0), decay_a * decay_b)
    for step in range(pairs):
        outs[step][...] = maps[partner(chip, step, pairs)]


def apply_map(state, state_map):
    offset, move, decay = parts_of(state_map)
    return state.astype(f32) * decay - mm(state, move) + offset.astype(f32)


def scan_kernel(pairs, grouped, *refs):
    place, blocks, rest = refs[0], refs[1 : 1 + pairs], refs[1 + pairs :]
    if grouped:
        start, rest = rest[0], rest[1:]
    outs, rest = rest[:pairs], rest[pairs:]
    if grouped:
        final, rest = rest[0], rest[1:]
    maps, starts = rest
    chip, _ = split_cores(place)
    for step in range(pairs):
        maps[partner(chip, step, pairs)] = blocks[step][...]
    state = start[...] if grouped else jnp.zeros((DK, DK), f32)
    for i in range(pairs):
        starts[i] = state.astype(bf16)
        if i < pairs - 1 or grouped:
            if i == 0 and not grouped:
                state = maps[i, :DK, :].astype(f32)
            else:
                state = apply_map(state, maps[i])
    if grouped:
        final[...] = state
    for step in range(pairs):
        outs[step][...] = starts[partner(chip, step, pairs)]


def project_kernel(parts, *refs):
    place, residual, weight, reads, intra, stay, go = refs[:7]
    refs = refs[7:]
    pairs = stay.shape[0]
    mine, other, refs = refs[:pairs], refs[pairs : 2 * pairs], refs[2 * pairs :]
    outs, (whole, summed) = refs[:parts], refs[parts:]
    chip, core = split_cores(place)
    head_me = place[1]
    for step in range(pairs):
        pair = partner(chip, step, pairs)
        for states, maps, side in ((mine, stay, core), (other, go, 1 - core)):
            own = lanes(2 * pair + side)
            state = states[step][...]
            state = jnp.where(core == 0, state, apply_map(state, maps[pair]).astype(bf16))
            whole[:, own] = (intra[:, own] + mm_nt(reads[:, own], state)).astype(bf16)
    summed[...] = jnp.dot(whole[...], weight[...], preferred_element_type=f32)
    share = summed.shape[0] // parts
    for step in range(parts):
        at = pl.ds(pl.multiple_of(partner(head_me, step, parts) * share, share), share)
        if step == 0:
            outs[0][...] = summed[at, :] + residual[at, :].astype(f32)
        else:
            outs[step][...] = summed[at, :].astype(bf16)


def normalized(values, gain):
    return values * lax.rsqrt(jnp.mean(values * values, axis=-1, keepdims=True) + eps_norm) * gain


def latent_kernel(parts, *refs):
    gain, latent_weight, latent_gain = refs[:3]
    partials = refs[3 : 3 + parts]
    stream, latent, together = refs[3 + parts :]
    width = stream.shape[1]
    total = partials[0][...]
    for step in range(1, parts):
        total = total + partials[step][...].astype(f32)
    short = total.astype(bf16)
    stream[...] = short
    together[:, :width] = short
    normed = normalized(short.astype(f32), gain[...]).astype(bf16)
    before = jnp.dot(normed, latent_weight[...], preferred_element_type=f32)
    rows = normalized(before, latent_gain[...]).astype(bf16)
    latent[...] = rows
    together[:, width:] = rows


def join_kernel(parts, *refs):
    place = refs[0]
    pieces = refs[1 : 1 + parts]
    out = refs[1 + parts]
    share = out.shape[0] // parts
    for step in range(parts):
        at = pl.ds(pl.multiple_of(partner(place[1], step, parts) * share, share), share)
        out[at, :] = pieces[step][:, pieces[step].shape[1] - out.shape[1] :]


def query_kernel(parts, *refs):
    place, gain, query_weight, up = refs[:4]
    pieces = refs[4 : 4 + parts]
    stream, absorbed = refs[4 + parts :]
    length = stream.shape[0]
    share = length // parts
    for step in range(parts):
        at = pl.ds(pl.multiple_of(partner(place[1], step, parts) * share, share), share)
        stream[at, :] = pieces[step][:, : stream.shape[1]]
    normed = normalized(stream[...].astype(f32), gain[...]).astype(bf16)
    query = jnp.dot(normed, query_weight[...], preferred_element_type=f32).astype(bf16)
    for head in range(query.shape[1] // DH):
        own = slice(head * DH, (head + 1) * DH)
        absorbed[head * length : (head + 1) * length, :] = (
            mm_nt(query[:, own], up[:, own]) * DH ** (-0.5)
        ).astype(bf16)


def attend_kernel(order, *refs):
    place, absorbed, up = refs[:3]
    blocks = refs[3 : 3 + len(order)]
    out, latents = refs[3 + len(order) :]
    length = blocks[0].shape[0]
    heads = absorbed.shape[0] // length
    me = place[2]
    for position in range(len(order)):
        latents[position * length : (position + 1) * length, :] = blocks[position][...]
    group = 2 if heads % 2 == 0 else 1
    rows = lax.broadcasted_iota(jnp.int32, (group * length, length), 0) % length
    cols = lax.broadcasted_iota(jnp.int32, (group * length, length), 1)
    allowed = [rows >= cols] + [(me ^ distance) < me for distance in order[1:]]
    for first in range(0, heads, group):
        own = slice(first * length, (first + group) * length)
        scores = mm_nt(absorbed[own, :], latents[...])
        parts = [
            jnp.where(allowed[p], scores[:, p * length : (p + 1) * length], -1e30)
            for p in range(len(order))
        ]
        peak = jnp.max(functools.reduce(jnp.maximum, parts), axis=-1, keepdims=True)
        weights = [jnp.exp(part - peak) for part in parts]
        total = jnp.sum(functools.reduce(jnp.add, weights), axis=-1, keepdims=True)
        mixed = mm(jnp.concatenate([w.astype(bf16) for w in weights], axis=1), latents[...])
        spread = (mixed / total).astype(bf16)
        for i in range(group):
            head = first + i
            value = slice((heads + head) * DH, (heads + head + 1) * DH)
            out[:, head * DH : (head + 1) * DH] = jnp.dot(
                spread[i * length : (i + 1) * length], up[:, value], preferred_element_type=f32
            ).astype(bf16)


def far_first(count):
    return sorted(range(1, count), key=lambda step: (-bin(step).count("1"), -step))


def per_device(
    kda_inputs,
    gate_log,
    beta,
    conv_weight,
    kda_out_weight,
    residual,
    norm_gain,
    latent_weight,
    latent_gain,
    query_weight,
    up_weight,
):
    length, width = residual.shape
    heads = beta.shape[1]
    pairs = heads // 2
    count, parts = lax.axis_size("ctx"), lax.axis_size("head")
    groups = count // heads
    ctx_me = lax.axis_index("ctx").astype(jnp.int32)
    place = jnp.stack([ctx_me % heads, lax.axis_index("head").astype(jnp.int32), ctx_me])

    halo = passed_along(kda_inputs[:, length - HALO :, :], "ctx", 1)
    inputs, logs, taps = call(
        load_kernel,
        [(kda_inputs.shape, bf16), (gate_log.shape, f32), (conv_weight.shape, f32)],
        [kda_inputs, gate_log, conv_weight],
        [(gate_log.shape, f32)],
        24,
        stored=(0, 1, 2),
        copies=3,
    )
    map_shape = (2 * DK + EXTRA, DK)
    arguments = [place, inputs, halo, logs, beta.T, taps]
    kept, sent, solutions, shrunk = call(
        map_kernel,
        [
            ((pairs,) + map_shape, bf16),
            ((pairs,) + map_shape, bf16),
            ((heads, length, 2 * DK), bf16),
            ((heads, 2, length, DK), bf16),
        ],
        arguments,
        [((heads, 2, length + 8, DK), f32)],
        16,
        cost=5.0,
    )

    got = trade(sent, "ctx", 1, heads)
    got_kept = trade(kept, "ctx", 1, heads)
    reads, intra = call(
        read_kernel,
        [((length, heads * DK), bf16), ((length, heads * DK), f32)],
        arguments + [solutions, shrunk],
        [((heads, length + 8, DK), f32)],
        16,
        cost=2.0,
    )
    chip_maps = call(
        functools.partial(compose_kernel, pairs),
        [(map_shape, bf16)] * pairs,
        [place, kept, got],
        [((pairs,) + map_shape, bf16)],
        8,
    )

    def across_chips(pieces):
        moved = {step: trade(pieces[step], "ctx", 2 * step, heads) for step in far_first(pairs)}
        return [pieces[0]] + [moved[step] for step in range(1, pairs)]

    chip_maps, reads, intra = lax.optimization_barrier((across_chips(chip_maps), reads, intra))
    state_outs = [((DK, DK), bf16)] * pairs
    scratch = [((pairs,) + map_shape, bf16), ((pairs, DK, DK), bf16)]
    if groups == 1:
        starts = call(
            functools.partial(scan_kernel, pairs, False), state_outs, [place] + chip_maps, scratch, 8
        )
    else:

        def run(start):
            return call(
                functools.partial(scan_kernel, pairs, True),
                state_outs + [((DK, DK), f32)],
                [place] + chip_maps + [start],
                scratch,
                8,
            )

        def relay(step_index, start):
            arrived = passed_along(run(start)[pairs], "ctx", heads)
            return jnp.where(ctx_me < heads, 0.0, arrived)

        start = lax.fori_loop(0, groups - 1, relay, jnp.zeros((DK, DK), f32))
        starts = run(start)[:pairs]
    starts = across_chips(starts)
    others = [trade(state, "ctx", 1, heads) for state in starts]

    share = length // parts
    partials = call(
        functools.partial(project_kernel, parts),
        [((share, width), f32)] + [((share, width), bf16)] * (parts - 1),
        [place, residual, kda_out_weight, reads, intra, got, got_kept] + starts + others,
        [((length, heads * DK), bf16), ((length, width), f32)],
        16,
    )

    def across_heads(pieces):
        moved = {step: trade(pieces[step], "head", step, parts) for step in far_first(parts)}
        return [pieces[0]] + [moved[step] for step in range(1, parts)]

    partials = across_heads(partials)
    latent_width = latent_weight.shape[1]
    stream_rows, latent_rows, together = call(
        functools.partial(latent_kernel, parts),
        [
            ((share, width), bf16),
            ((share, latent_width), bf16),
            ((share, width + latent_width), bf16),
        ],
        [norm_gain[None], latent_weight, latent_gain[None]] + partials,
        limit=16,
    )
    latent_parts = across_heads([latent_rows, together] + [latent_rows] * (parts - 2))
    far_parts = [trade(stream_rows, "head", step, parts) for step in range(2, parts)]
    stream_parts = [stream_rows, latent_parts[1]] + far_parts
    latent = call(
        functools.partial(join_kernel, parts),
        [((length, latent_width), bf16)],
        [place] + latent_parts,
        limit=8,
    )[0]

    order, latents = [0], [latent]
    for step in far_first(count // 2):
        order.append(2 * step)
        latents.append(trade(latent, "ctx", 2 * step, count))
    up = up_weight.reshape(up_weight.shape[0], -1)
    heads_mla = query_weight.shape[1] // DH
    stream_out, absorbed = call(
        functools.partial(query_kernel, parts),
        [((length, width), bf16), ((heads_mla * length, up.shape[0]), bf16)],
        [place, norm_gain[None], query_weight, up] + stream_parts,
        limit=16,
    )
    latents, absorbed = lax.optimization_barrier((latents, absorbed))
    for position in range(len(order)):
        order.append(order[position] + 1)
        latents.append(trade(latents[position], "ctx", 1, 2))
    attention_out = call(
        functools.partial(attend_kernel, tuple(order)),
        [((length, heads_mla * DH), bf16)],
        [place, absorbed, up] + latents,
        [((count * length, up.shape[0]), bf16)],
        12 + count * length * length * 24 // MIB,
        cost=4.0,
    )[0]
    return (stream_out, attention_out)


def solution(mesh):
    in_specs = (
        P(None, "ctx", "head"),
        P("ctx", "head"),
        P("ctx", "head"),
        P(None, None, "head"),
        P("head", None),
        P("ctx", None),
        P(),
        P(),
        P(),
        P(None, "head"),
        P(None, None, "head"),
    )
    out_specs = (P("ctx", None), P("ctx", "head"))
    return jax.shard_map(
        per_device, mesh=mesh, in_specs=in_specs, out_specs=out_specs, check_vma=False
    )
```

```python
import functools

import jax
import jax.numpy as jnp
from jax import lax
from jax.experimental import pallas as pl
from jax.experimental.pallas import tpu as pltpu
from jax.sharding import PartitionSpec as P

DK = 128
CONV = 4
DH = 128
HALO = 16
EXTRA = 16
MIB = 1 << 20

eps_norm = 1e-06
bf16 = jnp.bfloat16
f32 = jnp.float32
VMEM = pl.BlockSpec(memory_space=pltpu.VMEM)
SMEM = pl.BlockSpec(memory_space=pltpu.SMEM)
HBM = pl.BlockSpec(memory_space=pltpu.HBM)


def mm(left, right):
    return jnp.dot(left.astype(bf16), right.astype(bf16), preferred_element_type=f32)


def mm_nt(left, right):
    return lax.dot_general(
        left.astype(bf16), right.astype(bf16), (((1,), (1,)), ((), ())), preferred_element_type=f32
    )


def mm_tn(left, right):
    return lax.dot_general(
        left.astype(bf16), right.astype(bf16), (((0,), (0,)), ((), ())), preferred_element_type=f32
    )


def call(kernel, outs, args, scratch=(), limit=32, stored=(), copies=0, cost=1.0):
    scratch_shapes = [pltpu.VMEM(shape, dtype) for shape, dtype in scratch]
    if copies:
        scratch_shapes.append(pltpu.SemaphoreType.DMA((copies,)))
    return pl.pallas_call(
        kernel,
        out_shape=[jax.ShapeDtypeStruct(shape, dtype) for shape, dtype in outs],
        in_specs=[
            HBM if i in stored else SMEM if a.dtype == jnp.int32 else VMEM
            for i, a in enumerate(args)
        ],
        out_specs=[VMEM for _ in outs],
        scratch_shapes=scratch_shapes,
        compiler_params=pltpu.CompilerParams(vmem_limit_bytes=limit * MIB),
        cost_estimate=pl.CostEstimate(flops=int(cost * 1e9), bytes_accessed=0, transcendentals=0),
    )(*args)


def partner(index, step, size):
    return index ^ step if size & (size - 1) == 0 else (size + step - index) % size


def trade(block, axis, step, size):
    route = []
    for i in range(lax.axis_size(axis)):
        base = i // size * size
        route.append((i, base + partner(i - base, step, size)))
    return lax.ppermute(block, axis, route)


def passed_along(block, axis, distance):
    count = lax.axis_size(axis)
    return lax.ppermute(block, axis, [(i, (i + distance) % count) for i in range(count)])


def lanes(block_index, width=128):
    return pl.ds(pl.multiple_of(block_index * width, width), width)


def split_cores(place):
    return place[0] // 2, place[0] % 2


def load_kernel(stored_inputs, stored_gate, stored_taps, inputs, log, taps, gate, sems):
    moves = [
        pltpu.make_async_copy(stored_gate, gate, sems.at[0]),
        pltpu.make_async_copy(stored_inputs, inputs, sems.at[1]),
        pltpu.make_async_copy(stored_taps, taps, sems.at[2]),
    ]
    for move in moves:
        move.start()
    length = gate.shape[0]
    rows = lax.broadcasted_iota(jnp.int32, (length, length), 0)
    cols = lax.broadcasted_iota(jnp.int32, (length, length), 1)
    tril = (rows >= cols).astype(bf16)
    moves[0].wait()
    high = gate[...].astype(bf16)
    low = gate[...] - high.astype(f32)
    log[...] = mm(tril, high) + mm(tril, low)
    moves[1].wait()
    moves[2].wait()


def put_wide(wide, place, inputs, halo, own, part):
    pad = wide.shape[0] - inputs.shape[1]
    before = halo[part, halo.shape[1] - pad :, own].astype(f32)
    wide[:pad, :] = jnp.where(place[2] == 0, 0.0, before)
    wide[pad:, :] = inputs[part, :, own].astype(f32)


def convolved(wide, taps, own, part):
    length = wide.shape[0] - 8
    total = jnp.zeros((length, DK), f32)
    for tap in range(CONV):
        first = 8 - (CONV - 1) + tap
        total = total + taps[part, tap : tap + 1, own] * wide[first : first + length, :]
    return total / (1.0 + jnp.exp(-total))


def unit(value):
    return value * lax.rsqrt(jnp.sum(value * value, axis=-1, keepdims=True) + eps_norm)


def spans(log):
    half = log.shape[0] // 2
    for b in range(2):
        middle = log[b * half + half // 2 : b * half + half // 2 + 1]
        yield b, slice(b * half, (b + 1) * half), middle


def side_heads(place, pairs):
    _, core = split_cores(place)
    return [2 * i + core for i in range(pairs)] + [2 * i + 1 - core for i in range(pairs)]


def map_kernel(place, inputs, halo, logs, beta, taps, kept, sent, solutions, shrunk, wide):
    length = logs.shape[0]
    pairs = kept.shape[0]
    chunks = range(2 * pairs)
    heads = side_heads(place, pairs)
    lane = [lanes(head) for head in heads]
    rows = lax.broadcasted_iota(jnp.int32, (length, length), 0)
    cols = lax.broadcasted_iota(jnp.int32, (length, length), 1)
    eye = (rows == cols).astype(f32)
    for i in chunks:
        for part in (1, 2):
            put_wide(wide.at[i, part - 1], place, inputs, halo, lane[i], part)

    coupling, right, finals, decay = [], [], [], []
    for i in chunks:
        key = unit(convolved(wide.at[i, 0], taps, lane[i], 1)).astype(bf16).astype(f32)
        value = convolved(wide.at[i, 1], taps, lane[i], 2).astype(bf16)
        log = logs[:, lane[i]]
        rate_row = beta[pl.ds(heads[i], 1), :]
        rate_column = jnp.sum(rate_row * eye, axis=1, keepdims=True)
        last = log[length - 1 :]
        products = []
        for b, own, middle in spans(log):
            shrunk[i, b] = (key * jnp.exp(jnp.minimum(middle - log, 75.0))).astype(bf16)
            products.append(mm_nt(key[own] * jnp.exp(log[own] - middle), shrunk[i, b]))
        coupling.append(
            jnp.where(rows > cols, jnp.concatenate(products, axis=0) * rate_row, 0.0).astype(bf16)
        )
        right.append(jnp.concatenate([value, (key * jnp.exp(log)).astype(bf16)], axis=1))
        finals.append((key * jnp.exp(last - log) * rate_column).astype(bf16))
        decay.append(jnp.exp(last))

    size = 1
    inverse = None
    while size < length:
        corner = (
            (rows // (2 * size) == cols // (2 * size))
            & ((rows // size) % 2 == 1)
            & ((cols // size) % 2 == 0)
        )
        corners = [jnp.where(corner, coupling[i], jnp.zeros_like(coupling[i])) for i in chunks]
        if inverse is None:
            inverse = [eye - corners[i].astype(f32) for i in chunks]
        else:
            short = [inverse[i].astype(bf16) for i in chunks]
            below = [mm(corners[i], short[i]) for i in chunks]
            inverse = [inverse[i] - mm(short[i], below[i]) for i in chunks]
        size *= 2

    short = [inverse[i].astype(bf16) for i in chunks]
    first = [mm(short[i], right[i]).astype(bf16) for i in chunks]
    left = [right[i].astype(f32) - first[i].astype(f32) - mm(coupling[i], first[i]) for i in chunks]
    solved = [(first[i].astype(f32) + mm(short[i], left[i])).astype(bf16) for i in chunks]
    for i in chunks:
        solutions[i] = solved[i]
        maps = kept if i < pairs else sent
        put_map(maps, i % pairs, mm_tn(solved[i], finals[i]), decay[i])


def put_map(maps, i, offset_and_move, decay):
    maps[i, : 2 * DK, :] = offset_and_move.astype(bf16)
    high = decay.astype(bf16)
    low = (decay - high.astype(f32)).astype(bf16)
    maps[i, 2 * DK :, :] = jnp.concatenate(
        [jnp.broadcast_to(high, (EXTRA // 2, DK)), jnp.broadcast_to(low, (EXTRA // 2, DK))],
        axis=0,
    )


def read_kernel(
    place, inputs, halo, logs, beta, taps, solutions, shrunk, stay, go, reads, intra, wide
):
    length = logs.shape[0]
    pairs = stay.shape[0]
    _, core = split_cores(place)
    rows = lax.broadcasted_iota(jnp.int32, (length, length), 0)
    cols = lax.broadcasted_iota(jnp.int32, (length, length), 1)
    for i, head in enumerate(side_heads(place, pairs)):
        lane = lanes(head)
        put_wide(wide.at[i], place, inputs, halo, lane, 0)
        query = unit(convolved(wide.at[i], taps, lane, 0)) * DK ** (-0.5)
        query = query.astype(bf16).astype(f32)
        log = logs[:, lane]
        products = [
            mm_nt(query[own] * jnp.exp(log[own] - middle), shrunk[i, b])
            for b, own, middle in spans(log)
        ]
        rate_row = beta[pl.ds(head, 1), :]
        mixing = jnp.where(rows >= cols, jnp.concatenate(products, axis=0) * rate_row, 0.0)
        mixes = mm(mixing, solutions[i])
        read = query * jnp.exp(log) - mixes[:, DK:]
        offset, move, decay = parts_of((stay if i < pairs else go)[i % pairs])
        both = mm_nt(read, jnp.concatenate([offset, move], axis=0))
        second = core == 1
        intra[:, lane] = mixes[:, :DK] + jnp.where(second, both[:, :DK], 0.0)
        reads[:, lane] = jnp.where(second, read * decay - both[:, DK:], read).astype(bf16)


def parts_of(state_map):
    extra = state_map[2 * DK :].astype(f32)
    decay = extra[:1] + extra[EXTRA // 2 : EXTRA // 2 + 1]
    return state_map[:DK], state_map[DK : 2 * DK], decay


def compose_kernel(pairs, place, kept, got, *refs):
    outs, (maps,) = refs[:pairs], refs[pairs:]
    chip, core = split_cores(place)
    eye = (
        lax.broadcasted_iota(jnp.int32, (DK, DK), 0) == lax.broadcasted_iota(jnp.int32, (DK, DK), 1)
    ).astype(f32)
    for pair in range(pairs):
        mine, other = kept[pair], got[pair]
        offset_a, move_a, decay_a = parts_of(jnp.where(core == 0, mine, other))
        offset_b, move_b, decay_b = parts_of(jnp.where(core == 0, other, mine))
        product = mm(jnp.concatenate([offset_a, move_a], axis=0), move_b)
        column = jnp.sum(eye * decay_a, axis=1, keepdims=True)
        offset = offset_a.astype(f32) * decay_b - product[:DK] + offset_b.astype(f32)
        move = move_a.astype(f32) * decay_b + column * move_b.astype(f32) - product[DK:]
        put_map(maps, pair, jnp.concatenate([offset, move], axis=0), decay_a * decay_b)
    for step in range(pairs):
        outs[step][...] = maps[partner(chip, step, pairs)]


def apply_map(state, state_map):
    offset, move, decay = parts_of(state_map)
    return state.astype(f32) * decay - mm(state, move) + offset.astype(f32)


def scan_kernel(pairs, grouped, *refs):
    place, blocks, rest = refs[0], refs[1 : 1 + pairs], refs[1 + pairs :]
    if grouped:
        start, rest = rest[0], rest[1:]
    outs, rest = rest[:pairs], rest[pairs:]
    if grouped:
        final, rest = rest[0], rest[1:]
    maps, starts = rest
    chip, _ = split_cores(place)
    for step in range(pairs):
        maps[partner(chip, step, pairs)] = blocks[step][...]
    state = start[...] if grouped else jnp.zeros((DK, DK), f32)
    for i in range(pairs):
        starts[i] = state.astype(bf16)
        if i < pairs - 1 or grouped:
            if i == 0 and not grouped:
                state = maps[i, :DK, :].astype(f32)
            else:
                state = apply_map(state, maps[i])
    if grouped:
        final[...] = state
    for step in range(pairs):
        outs[step][...] = starts[partner(chip, step, pairs)]


def project_kernel(parts, *refs):
    place, residual, weight, reads, intra = refs[:5]
    refs = refs[5:]
    pairs = reads.shape[1] // DK // 2
    mine, other, refs = refs[:pairs], refs[pairs : 2 * pairs], refs[2 * pairs :]
    outs, (whole, summed) = refs[:parts], refs[parts:]
    chip, core = split_cores(place)
    head_me = place[1]
    for step in range(pairs):
        pair = partner(chip, step, pairs)
        for states, side in ((mine, core), (other, 1 - core)):
            own = lanes(2 * pair + side)
            whole[:, own] = (intra[:, own] + mm_nt(reads[:, own], states[step][...])).astype(bf16)
    summed[...] = jnp.dot(whole[...], weight[...], preferred_element_type=f32)
    share = summed.shape[0] // parts
    for step in range(parts):
        at = pl.ds(pl.multiple_of(partner(head_me, step, parts) * share, share), share)
        if step == 0:
            outs[0][...] = summed[at, :] + residual[at, :].astype(f32)
        else:
            outs[step][...] = summed[at, :].astype(bf16)


def normalized(values, gain):
    return values * lax.rsqrt(jnp.mean(values * values, axis=-1, keepdims=True) + eps_norm) * gain


def latent_kernel(parts, *refs):
    gain, latent_weight, latent_gain = refs[:3]
    partials = refs[3 : 3 + parts]
    stream, latent, together = refs[3 + parts :]
    width = stream.shape[1]
    total = partials[0][...]
    for step in range(1, parts):
        total = total + partials[step][...].astype(f32)
    short = total.astype(bf16)
    stream[...] = short
    together[:, :width] = short
    normed = normalized(short.astype(f32), gain[...]).astype(bf16)
    before = jnp.dot(normed, latent_weight[...], preferred_element_type=f32)
    rows = normalized(before, latent_gain[...]).astype(bf16)
    latent[...] = rows
    together[:, width:] = rows


def join_kernel(parts, *refs):
    place = refs[0]
    pieces = refs[1 : 1 + parts]
    out = refs[1 + parts]
    share = out.shape[0] // parts
    for step in range(parts):
        at = pl.ds(pl.multiple_of(partner(place[1], step, parts) * share, share), share)
        out[at, :] = pieces[step][:, pieces[step].shape[1] - out.shape[1] :]


def query_kernel(parts, *refs):
    place, gain, query_weight, up = refs[:4]
    pieces = refs[4 : 4 + parts]
    stream, absorbed = refs[4 + parts :]
    length = stream.shape[0]
    share = length // parts
    for step in range(parts):
        at = pl.ds(pl.multiple_of(partner(place[1], step, parts) * share, share), share)
        stream[at, :] = pieces[step][:, : stream.shape[1]]
    normed = normalized(stream[...].astype(f32), gain[...]).astype(bf16)
    query = jnp.dot(normed, query_weight[...], preferred_element_type=f32).astype(bf16)
    for head in range(query.shape[1] // DH):
        own = slice(head * DH, (head + 1) * DH)
        absorbed[head * length : (head + 1) * length, :] = (
            mm_nt(query[:, own], up[:, own]) * DH ** (-0.5)
        ).astype(bf16)


def attend_kernel(order, *refs):
    place, absorbed, up = refs[:3]
    blocks = refs[3 : 3 + len(order)]
    out, latents = refs[3 + len(order) :]
    length = blocks[0].shape[0]
    heads = absorbed.shape[0] // length
    me = place[2]
    for position in range(len(order)):
        latents[position * length : (position + 1) * length, :] = blocks[position][...]
    group = heads
    rows = lax.broadcasted_iota(jnp.int32, (group * length, length), 0) % length
    cols = lax.broadcasted_iota(jnp.int32, (group * length, length), 1)
    allowed = [rows >= cols] + [(me ^ distance) < me for distance in order[1:]]
    for first in range(0, heads, group):
        own = slice(first * length, (first + group) * length)
        scores = mm_nt(absorbed[own, :], latents[...])
        parts = [
            jnp.where(allowed[p], scores[:, p * length : (p + 1) * length], -1e30)
            for p in range(len(order))
        ]
        peak = jnp.max(functools.reduce(jnp.maximum, parts), axis=-1, keepdims=True)
        weights = [jnp.exp(part - peak) for part in parts]
        total = jnp.sum(functools.reduce(jnp.add, weights), axis=-1, keepdims=True)
        mixed = mm(jnp.concatenate([w.astype(bf16) for w in weights], axis=1), latents[...])
        spread = (mixed / total).astype(bf16)
        for i in range(group):
            head = first + i
            value = slice((heads + head) * DH, (heads + head + 1) * DH)
            out[:, head * DH : (head + 1) * DH] = jnp.dot(
                spread[i * length : (i + 1) * length], up[:, value], preferred_element_type=f32
            ).astype(bf16)


def far_first(count):
    return sorted(range(1, count), key=lambda step: (-bin(step).count("1"), -step))


def per_device(
    kda_inputs,
    gate_log,
    beta,
    conv_weight,
    kda_out_weight,
    residual,
    norm_gain,
    latent_weight,
    latent_gain,
    query_weight,
    up_weight,
):
    length, width = residual.shape
    heads = beta.shape[1]
    pairs = heads // 2
    count, parts = lax.axis_size("ctx"), lax.axis_size("head")
    groups = count // heads
    ctx_me = lax.axis_index("ctx").astype(jnp.int32)
    place = jnp.stack([ctx_me % heads, lax.axis_index("head").astype(jnp.int32), ctx_me])

    halo = passed_along(kda_inputs[:, length - HALO :, :], "ctx", 1)
    inputs, logs, taps = call(
        load_kernel,
        [(kda_inputs.shape, bf16), (gate_log.shape, f32), (conv_weight.shape, f32)],
        [kda_inputs, gate_log, conv_weight],
        [(gate_log.shape, f32)],
        24,
        stored=(0, 1, 2),
        copies=3,
    )
    map_shape = (2 * DK + EXTRA, DK)
    arguments = [place, inputs, halo, logs, beta.T, taps]
    kept, sent, solutions, shrunk = call(
        map_kernel,
        [
            ((pairs,) + map_shape, bf16),
            ((pairs,) + map_shape, bf16),
            ((heads, length, 2 * DK), bf16),
            ((heads, 2, length, DK), bf16),
        ],
        arguments,
        [((heads, 2, length + 8, DK), f32)],
        16,
        cost=5.0,
    )

    got = trade(sent, "ctx", 1, heads)
    got_kept = trade(kept, "ctx", 1, heads)
    reads, intra = call(
        read_kernel,
        [((length, heads * DK), bf16), ((length, heads * DK), f32)],
        arguments + [solutions, shrunk, got, got_kept],
        [((heads, length + 8, DK), f32)],
        16,
        cost=2.5,
    )
    chip_maps = call(
        functools.partial(compose_kernel, pairs),
        [(map_shape, bf16)] * pairs,
        [place, kept, got],
        [((pairs,) + map_shape, bf16)],
        8,
    )

    def across_chips(pieces):
        moved = {step: trade(pieces[step], "ctx", 2 * step, heads) for step in far_first(pairs)}
        return [pieces[0]] + [moved[step] for step in range(1, pairs)]

    chip_maps, reads, intra = lax.optimization_barrier((across_chips(chip_maps), reads, intra))
    state_outs = [((DK, DK), bf16)] * pairs
    scratch = [((pairs,) + map_shape, bf16), ((pairs, DK, DK), bf16)]
    if groups == 1:
        starts = call(
            functools.partial(scan_kernel, pairs, False), state_outs, [place] + chip_maps, scratch, 8
        )
    else:

        def run(start):
            return call(
                functools.partial(scan_kernel, pairs, True),
                state_outs + [((DK, DK), f32)],
                [place] + chip_maps + [start],
                scratch,
                8,
            )

        def relay(step_index, start):
            arrived = passed_along(run(start)[pairs], "ctx", heads)
            return jnp.where(ctx_me < heads, 0.0, arrived)

        start = lax.fori_loop(0, groups - 1, relay, jnp.zeros((DK, DK), f32))
        starts = run(start)[:pairs]
    starts = across_chips(starts)
    others = [trade(state, "ctx", 1, heads) for state in starts]

    share = length // parts
    partials = call(
        functools.partial(project_kernel, parts),
        [((share, width), f32)] + [((share, width), bf16)] * (parts - 1),
        [place, residual, kda_out_weight, reads, intra] + starts + others,
        [((length, heads * DK), bf16), ((length, width), f32)],
        16,
    )

    def across_heads(pieces):
        moved = {step: trade(pieces[step], "head", step, parts) for step in far_first(parts)}
        return [pieces[0]] + [moved[step] for step in range(1, parts)]

    partials = across_heads(partials)
    latent_width = latent_weight.shape[1]
    stream_rows, latent_rows, together = call(
        functools.partial(latent_kernel, parts),
        [
            ((share, width), bf16),
            ((share, latent_width), bf16),
            ((share, width + latent_width), bf16),
        ],
        [norm_gain[None], latent_weight, latent_gain[None]] + partials,
        limit=16,
    )
    latent_parts = across_heads([latent_rows, together] + [latent_rows] * (parts - 2))
    far_parts = []
    for step in range(2, parts, 2):
        far_parts.append(trade(stream_rows, "head", step, parts))
        far_parts.append(trade(far_parts[-1], "head", 1, parts))
    stream_parts = [stream_rows, latent_parts[1]] + far_parts
    latent = call(
        functools.partial(join_kernel, parts),
        [((length, latent_width), bf16)],
        [place] + latent_parts,
        limit=8,
    )[0]

    order, latents = [0], [latent]
    for step in far_first(count // 2):
        order.append(2 * step)
        latents.append(trade(latent, "ctx", 2 * step, count))
    for position in range(len(order)):
        order.append(order[position] + 1)
        latents.append(trade(latents[position], "ctx", 1, 2))
    up = up_weight.reshape(up_weight.shape[0], -1)
    heads_mla = query_weight.shape[1] // DH
    stream_out, absorbed = call(
        functools.partial(query_kernel, parts),
        [((length, width), bf16), ((heads_mla * length, up.shape[0]), bf16)],
        [place, norm_gain[None], query_weight, up] + stream_parts,
        limit=16,
    )
    attention_out = call(
        functools.partial(attend_kernel, tuple(order)),
        [((length, heads_mla * DH), bf16)],
        [place, absorbed, up] + latents,
        [((count * length, up.shape[0]), bf16)],
        12 + count * length * length * 24 // MIB,
        cost=4.0,
    )[0]
    return (stream_out, attention_out)


def solution(mesh):
    in_specs = (
        P(None, "ctx", "head"),
        P("ctx", "head"),
        P("ctx", "head"),
        P(None, None, "head"),
        P("head", None),
        P("ctx", None),
        P(),
        P(),
        P(),
        P(None, "head"),
        P(None, None, "head"),
    )
    out_specs = (P("ctx", None), P("ctx", "head"))
    return jax.shard_map(
        per_device, mesh=mesh, in_specs=in_specs, out_specs=out_specs, check_vma=False
    )
```

```python
import functools

import jax
import jax.numpy as jnp
from jax import lax
from jax.experimental import pallas as pl
from jax.experimental.pallas import tpu as pltpu
from jax.sharding import PartitionSpec as P

DK = 128
CONV = 4
DH = 128
HALO = 16
EXTRA = 16
MIB = 1 << 20

eps_norm = 1e-06
bf16 = jnp.bfloat16
f32 = jnp.float32
VMEM = pl.BlockSpec(memory_space=pltpu.VMEM)
SMEM = pl.BlockSpec(memory_space=pltpu.SMEM)
HBM = pl.BlockSpec(memory_space=pltpu.HBM)


def mm(left, right):
    return jnp.dot(left.astype(bf16), right.astype(bf16), preferred_element_type=f32)


def mm_nt(left, right):
    return lax.dot_general(
        left.astype(bf16), right.astype(bf16), (((1,), (1,)), ((), ())), preferred_element_type=f32
    )


def mm_tn(left, right):
    return lax.dot_general(
        left.astype(bf16), right.astype(bf16), (((0,), (0,)), ((), ())), preferred_element_type=f32
    )


def call(kernel, outs, args, scratch=(), limit=32, stored=(), copies=0, cost=1.0):
    scratch_shapes = [pltpu.VMEM(shape, dtype) for shape, dtype in scratch]
    if copies:
        scratch_shapes.append(pltpu.SemaphoreType.DMA((copies,)))
    return pl.pallas_call(
        kernel,
        out_shape=[jax.ShapeDtypeStruct(shape, dtype) for shape, dtype in outs],
        in_specs=[
            HBM if i in stored else SMEM if a.dtype == jnp.int32 else VMEM
            for i, a in enumerate(args)
        ],
        out_specs=[VMEM for _ in outs],
        scratch_shapes=scratch_shapes,
        compiler_params=pltpu.CompilerParams(vmem_limit_bytes=limit * MIB),
        cost_estimate=pl.CostEstimate(flops=int(cost * 1e9), bytes_accessed=0, transcendentals=0),
    )(*args)


def partner(index, step, size):
    return index ^ step if size & (size - 1) == 0 else (size + step - index) % size


def trade(block, axis, step, size):
    route = []
    for i in range(lax.axis_size(axis)):
        base = i // size * size
        route.append((i, base + partner(i - base, step, size)))
    return lax.ppermute(block, axis, route)


def passed_along(block, axis, distance):
    count = lax.axis_size(axis)
    return lax.ppermute(block, axis, [(i, (i + distance) % count) for i in range(count)])


def lanes(block_index, width=128):
    return pl.ds(pl.multiple_of(block_index * width, width), width)


def split_cores(place):
    return place[0] // 2, place[0] % 2


def convolved(wide, taps, part, count):
    total = None
    for tap in range(CONV):
        first = 8 - (CONV - 1) + tap
        term = taps[part, tap : tap + 1, :] * wide[first : first + count, :]
        total = term if total is None else total + term
    return total / (1.0 + jnp.exp(-total))


def finished(activated, part):
    if part == 2:
        return activated.astype(bf16)
    heads = []
    for first in range(0, activated.shape[1], DK):
        head = activated[:, first : first + DK]
        head = head * lax.rsqrt(jnp.sum(head * head, axis=-1, keepdims=True) + eps_norm)
        heads.append((head * DK ** (-0.5) if part == 0 else head).astype(bf16))
    return jnp.concatenate(heads, axis=1)


def load_kernel(stored_inputs, stored_gate, stored_taps, done, log, taps, gate, inputs, wide, sems):
    moves = [
        pltpu.make_async_copy(stored_gate, gate, sems.at[0]),
        pltpu.make_async_copy(stored_taps, taps, sems.at[1]),
        pltpu.make_async_copy(stored_inputs, inputs, sems.at[2]),
    ]
    for move in moves:
        move.start()
    length = gate.shape[0]
    rows = lax.broadcasted_iota(jnp.int32, (length, length), 0)
    cols = lax.broadcasted_iota(jnp.int32, (length, length), 1)
    tril = (rows >= cols).astype(bf16)
    moves[0].wait()
    high = gate[...].astype(bf16)
    low = gate[...] - high.astype(f32)
    log[...] = mm(tril, high) + mm(tril, low)
    moves[1].wait()
    moves[2].wait()
    for part in range(3):
        wide[:8, :] = jnp.zeros((8, wide.shape[1]), f32)
        wide[8:, :] = inputs[part].astype(f32)
        done[part] = finished(convolved(wide, taps, part, length), part)


def first_rows(place, halo, inputs, taps, part, wide):
    count = halo.shape[1]
    before = halo[part, count - 8 :, :].astype(f32)
    wide[:8, :] = jnp.where(place[2] == 0, 0.0, before)
    wide[8:, :] = inputs[part].astype(f32)
    return finished(convolved(wide, taps, part, count), part)


def whole_head(first, done, part, lane):
    return jnp.concatenate([first[:, lane], done[part, first.shape[0] :, lane]], axis=0)


def spans(log):
    half = log.shape[0] // 2
    for b in range(2):
        middle = log[b * half + half // 2 : b * half + half // 2 + 1]
        yield b, slice(b * half, (b + 1) * half), middle


def side_heads(place, pairs):
    _, core = split_cores(place)
    return [2 * i + core for i in range(pairs)] + [2 * i + 1 - core for i in range(pairs)]


def map_kernel(
    place, done, head_rows, halo, logs, beta, taps, kept, sent, solutions, shrunk, first, wide
):
    length = logs.shape[0]
    pairs = kept.shape[0]
    chunks = range(2 * pairs)
    heads = side_heads(place, pairs)
    lane = [lanes(head) for head in heads]
    rows = lax.broadcasted_iota(jnp.int32, (length, length), 0)
    cols = lax.broadcasted_iota(jnp.int32, (length, length), 1)
    eye = (rows == cols).astype(f32)
    for part in (1, 2):
        first[part - 1] = first_rows(place, halo, head_rows, taps, part, wide)

    coupling, right, finals, decay = [], [], [], []
    for i in chunks:
        key = whole_head(first.at[0], done, 1, lane[i]).astype(f32)
        value = whole_head(first.at[1], done, 2, lane[i])
        log = logs[:, lane[i]]
        rate_row = beta[pl.ds(heads[i], 1), :]
        rate_column = jnp.sum(rate_row * eye, axis=1, keepdims=True)
        last = log[length - 1 :]
        products = []
        for b, own, middle in spans(log):
            shrunk[i, b] = (key * jnp.exp(jnp.minimum(middle - log, 75.0))).astype(bf16)
            products.append(mm_nt(key[own] * jnp.exp(log[own] - middle), shrunk[i, b]))
        coupling.append(
            jnp.where(rows > cols, jnp.concatenate(products, axis=0) * rate_row, 0.0).astype(bf16)
        )
        right.append(jnp.concatenate([value, (key * jnp.exp(log)).astype(bf16)], axis=1))
        finals.append((key * jnp.exp(last - log) * rate_column).astype(bf16))
        decay.append(jnp.exp(last))

    size = 1
    inverse = None
    while size < length:
        corner = (
            (rows // (2 * size) == cols // (2 * size))
            & ((rows // size) % 2 == 1)
            & ((cols // size) % 2 == 0)
        )
        corners = [jnp.where(corner, coupling[i], jnp.zeros_like(coupling[i])) for i in chunks]
        if inverse is None:
            inverse = [eye - corners[i].astype(f32) for i in chunks]
        else:
            short = [inverse[i].astype(bf16) for i in chunks]
            below = [mm(corners[i], short[i]) for i in chunks]
            inverse = [inverse[i] - mm(short[i], below[i]) for i in chunks]
        size *= 2

    short = [inverse[i].astype(bf16) for i in chunks]
    near = [mm(short[i], right[i]).astype(bf16) for i in chunks]
    left = [right[i].astype(f32) - near[i].astype(f32) - mm(coupling[i], near[i]) for i in chunks]
    solved = [(near[i].astype(f32) + mm(short[i], left[i])).astype(bf16) for i in chunks]
    for i in chunks:
        solutions[i] = solved[i]
        maps = kept if i < pairs else sent
        put_map(maps, i % pairs, mm_tn(solved[i], finals[i]), decay[i])


def put_map(maps, i, offset_and_move, decay):
    maps[i, : 2 * DK, :] = offset_and_move.astype(bf16)
    high = decay.astype(bf16)
    low = (decay - high.astype(f32)).astype(bf16)
    maps[i, 2 * DK :, :] = jnp.concatenate(
        [jnp.broadcast_to(high, (EXTRA // 2, DK)), jnp.broadcast_to(low, (EXTRA // 2, DK))],
        axis=0,
    )


def read_kernel(place, done, head_rows, halo, logs, beta, taps, *refs):
    solutions, shrunk, stay, go, reads, intra, first, wide = refs
    length = logs.shape[0]
    pairs = stay.shape[0]
    _, core = split_cores(place)
    first[...] = first_rows(place, halo, head_rows, taps, 0, wide)
    rows = lax.broadcasted_iota(jnp.int32, (length, length), 0)
    cols = lax.broadcasted_iota(jnp.int32, (length, length), 1)
    for i, head in enumerate(side_heads(place, pairs)):
        lane = lanes(head)
        query = whole_head(first, done, 0, lane).astype(f32)
        log = logs[:, lane]
        products = [
            mm_nt(query[own] * jnp.exp(log[own] - middle), shrunk[i, b])
            for b, own, middle in spans(log)
        ]
        rate_row = beta[pl.ds(head, 1), :]
        mixing = jnp.where(rows >= cols, jnp.concatenate(products, axis=0) * rate_row, 0.0)
        high = mixing.astype(bf16)
        mixes = mm(high, solutions[i]) + mm(mixing - high.astype(f32), solutions[i])
        read = query * jnp.exp(log) - mixes[:, DK:]
        offset, move, decay = parts_of((stay if i < pairs else go)[i % pairs])
        both = mm_nt(read, jnp.concatenate([offset, move], axis=0))
        second = core == 1
        intra[:, lane] = mixes[:, :DK] + jnp.where(second, both[:, :DK], 0.0)
        reads[:, lane] = jnp.where(second, read * decay - both[:, DK:], read).astype(bf16)


def parts_of(state_map):
    extra = state_map[2 * DK :].astype(f32)
    decay = extra[:1] + extra[EXTRA // 2 : EXTRA // 2 + 1]
    return state_map[:DK], state_map[DK : 2 * DK], decay


def compose_kernel(pairs, place, kept, got, *refs):
    outs, (maps,) = refs[:pairs], refs[pairs:]
    chip, core = split_cores(place)
    eye = (
        lax.broadcasted_iota(jnp.int32, (DK, DK), 0) == lax.broadcasted_iota(jnp.int32, (DK, DK), 1)
    ).astype(f32)
    for pair in range(pairs):
        mine, other = kept[pair], got[pair]
        offset_a, move_a, decay_a = parts_of(jnp.where(core == 0, mine, other))
        offset_b, move_b, decay_b = parts_of(jnp.where(core == 0, other, mine))
        product = mm(jnp.concatenate([offset_a, move_a], axis=0), move_b)
        column = jnp.sum(eye * decay_a, axis=1, keepdims=True)
        offset = offset_a.astype(f32) * decay_b - product[:DK] + offset_b.astype(f32)
        move = move_a.astype(f32) * decay_b + column * move_b.astype(f32) - product[DK:]
        put_map(maps, pair, jnp.concatenate([offset, move], axis=0), decay_a * decay_b)
    for step in range(pairs):
        outs[step][...] = maps[partner(chip, step, pairs)]


def apply_map(state, state_map):
    offset, move, decay = parts_of(state_map)
    return state.astype(f32) * decay - mm(state, move) + offset.astype(f32)


def scan_kernel(pairs, grouped, *refs):
    place, blocks, rest = refs[0], refs[1 : 1 + pairs], refs[1 + pairs :]
    if grouped:
        start, rest = rest[0], rest[1:]
    outs, rest = rest[:pairs], rest[pairs:]
    if grouped:
        final, rest = rest[0], rest[1:]
    maps, starts = rest
    chip, _ = split_cores(place)
    for step in range(pairs):
        maps[partner(chip, step, pairs)] = blocks[step][...]
    state = start[...] if grouped else jnp.zeros((DK, DK), f32)
    for i in range(pairs):
        starts[i] = state.astype(bf16)
        if i < pairs - 1 or grouped:
            if i == 0 and not grouped:
                state = maps[i, :DK, :].astype(f32)
            else:
                state = apply_map(state, maps[i])
    if grouped:
        final[...] = state
    for step in range(pairs):
        outs[step][...] = starts[partner(chip, step, pairs)]


def project_kernel(parts, *refs):
    place, residual, weight, reads, intra = refs[:5]
    refs = refs[5:]
    pairs = reads.shape[1] // DK // 2
    mine, other, refs = refs[:pairs], refs[pairs : 2 * pairs], refs[2 * pairs :]
    outs, (whole, summed) = refs[:parts], refs[parts:]
    chip, core = split_cores(place)
    head_me = place[1]
    for step in range(pairs):
        pair = partner(chip, step, pairs)
        for states, side in ((mine, core), (other, 1 - core)):
            own = lanes(2 * pair + side)
            whole[:, own] = (intra[:, own] + mm_nt(reads[:, own], states[step][...])).astype(bf16)
    summed[...] = jnp.dot(whole[...], weight[...], preferred_element_type=f32)
    share = summed.shape[0] // parts
    for step in range(parts):
        at = pl.ds(pl.multiple_of(partner(head_me, step, parts) * share, share), share)
        if step == 0:
            outs[0][...] = summed[at, :] + residual[at, :].astype(f32)
        else:
            outs[step][...] = summed[at, :].astype(bf16)


def normalized(values, gain):
    return values * lax.rsqrt(jnp.mean(values * values, axis=-1, keepdims=True) + eps_norm) * gain


def latent_kernel(parts, *refs):
    gain, latent_weight, latent_gain = refs[:3]
    partials = refs[3 : 3 + parts]
    stream, latent, together = refs[3 + parts :]
    width = stream.shape[1]
    total = partials[0][...]
    for step in range(1, parts):
        total = total + partials[step][...].astype(f32)
    short = total.astype(bf16)
    stream[...] = short
    together[:, :width] = short
    normed = normalized(short.astype(f32), gain[...]).astype(bf16)
    before = jnp.dot(normed, latent_weight[...], preferred_element_type=f32)
    rows = normalized(before, latent_gain[...]).astype(bf16)
    latent[...] = rows
    together[:, width:] = rows


def join_kernel(parts, *refs):
    place = refs[0]
    pieces = refs[1 : 1 + parts]
    out = refs[1 + parts]
    share = out.shape[0] // parts
    for step in range(parts):
        at = pl.ds(pl.multiple_of(partner(place[1], step, parts) * share, share), share)
        out[at, :] = pieces[step][:, pieces[step].shape[1] - out.shape[1] :]


def attend_kernel(parts, order, *refs):
    place, gain, query_weight, up = refs[:4]
    pieces, refs = refs[4 : 4 + parts], refs[4 + parts :]
    blocks, refs = refs[: len(order)], refs[len(order) :]
    stream, out, absorbed, latents, scores, weights, totals = refs
    length = stream.shape[0]
    heads = absorbed.shape[0] // length
    me = place[2]
    share = length // parts
    for step in range(parts):
        at = pl.ds(pl.multiple_of(partner(place[1], step, parts) * share, share), share)
        stream[at, :] = pieces[step][:, : stream.shape[1]]
    for position in range(len(order)):
        latents[position * length : (position + 1) * length, :] = blocks[position][...]
    normed = normalized(stream[...].astype(f32), gain[...]).astype(bf16)
    query = jnp.dot(normed, query_weight[...], preferred_element_type=f32).astype(bf16)
    for head in range(heads):
        own = slice(head * DH, (head + 1) * DH)
        absorbed[head * length : (head + 1) * length, :] = (
            mm_nt(query[:, own], up[:, own]) * DH ** (-0.5)
        ).astype(bf16)
    scores[...] = mm_nt(absorbed[...], latents[...])
    group = min(length, 32)
    for first in range(0, heads * length, group):
        own = slice(first, first + group)
        rows = lax.broadcasted_iota(jnp.int32, (group, length), 0) + first % length
        cols = lax.broadcasted_iota(jnp.int32, (group, length), 1)
        allowed = [rows >= cols] + [(me ^ distance) < me for distance in order[1:]]
        masked = [
            jnp.where(allowed[p], scores[own, p * length : (p + 1) * length], -1e30)
            for p in range(len(order))
        ]
        peak = jnp.max(functools.reduce(jnp.maximum, masked), axis=-1, keepdims=True)
        shares = [jnp.exp(part - peak) for part in masked]
        total = jnp.sum(functools.reduce(jnp.add, shares), axis=-1, keepdims=True)
        totals[own, :] = jnp.broadcast_to(total, (group, totals.shape[1]))
        for p in range(len(order)):
            weights[own, p * length : (p + 1) * length] = shares[p].astype(bf16)
    mixed = jnp.dot(weights[...], latents[...], preferred_element_type=f32)
    for head in range(heads):
        own = slice(head * length, (head + 1) * length)
        value = slice((heads + head) * DH, (heads + head + 1) * DH)
        outcome = mm(mixed[own], up[:, value])
        out[:, head * DH : (head + 1) * DH] = (outcome / totals[own, :]).astype(bf16)


def far_first(count):
    return sorted(range(1, count), key=lambda step: (-bin(step).count("1"), -step))


def per_device(
    kda_inputs,
    gate_log,
    beta,
    conv_weight,
    kda_out_weight,
    residual,
    norm_gain,
    latent_weight,
    latent_gain,
    query_weight,
    up_weight,
):
    length, width = residual.shape
    heads = beta.shape[1]
    pairs = heads // 2
    count, parts = lax.axis_size("ctx"), lax.axis_size("head")
    groups = count // heads
    ctx_me = lax.axis_index("ctx").astype(jnp.int32)
    place = jnp.stack([ctx_me % heads, lax.axis_index("head").astype(jnp.int32), ctx_me])

    halo = passed_along(kda_inputs[:, length - HALO :, :], "ctx", 1)
    stored = [
        pltpu.with_memory_space_constraint(a, pltpu.HBM) for a in (kda_inputs, gate_log, conv_weight)
    ]
    done, logs, taps = call(
        load_kernel,
        [(kda_inputs.shape, bf16), (gate_log.shape, f32), (conv_weight.shape, f32)],
        stored,
        [
            (gate_log.shape, f32),
            (kda_inputs.shape, bf16),
            ((length + 8, heads * DK), f32),
        ],
        24,
        stored=(0, 1, 2),
        copies=3,
        cost=2.0,
    )
    map_shape = (2 * DK + EXTRA, DK)
    head_rows = kda_inputs[:, :HALO, :]
    arguments = [place, done, head_rows, halo, logs, beta.T, taps]
    kept, sent, solutions, shrunk = call(
        map_kernel,
        [
            ((pairs,) + map_shape, bf16),
            ((pairs,) + map_shape, bf16),
            ((heads, length, 2 * DK), bf16),
            ((heads, 2, length, DK), bf16),
        ],
        arguments,
        [((2, HALO, heads * DK), bf16), ((HALO + 8, heads * DK), f32)],
        16,
        cost=5.0,
    )

    got = trade(sent, "ctx", 1, heads)
    got_kept = trade(kept, "ctx", 1, heads)
    reads, intra = call(
        read_kernel,
        [((length, heads * DK), bf16), ((length, heads * DK), f32)],
        arguments + [solutions, shrunk, got, got_kept],
        [((HALO, heads * DK), bf16), ((HALO + 8, heads * DK), f32)],
        16,
        cost=2.5,
    )
    chip_maps = call(
        functools.partial(compose_kernel, pairs),
        [(map_shape, bf16)] * pairs,
        [place, kept, got],
        [((pairs,) + map_shape, bf16)],
        8,
    )

    def across_chips(pieces):
        moved = {step: trade(pieces[step], "ctx", 2 * step, heads) for step in far_first(pairs)}
        return [pieces[0]] + [moved[step] for step in range(1, pairs)]

    chip_maps, reads, intra = lax.optimization_barrier((across_chips(chip_maps), reads, intra))
    state_outs = [((DK, DK), bf16)] * pairs
    scratch = [((pairs,) + map_shape, bf16), ((pairs, DK, DK), bf16)]
    if groups == 1:
        starts = call(
            functools.partial(scan_kernel, pairs, False), state_outs, [place] + chip_maps, scratch, 8
        )
    else:

        def run(start):
            return call(
                functools.partial(scan_kernel, pairs, True),
                state_outs + [((DK, DK), f32)],
                [place] + chip_maps + [start],
                scratch,
                8,
            )

        def relay(step_index, start):
            arrived = passed_along(run(start)[pairs], "ctx", heads)
            return jnp.where(ctx_me < heads, 0.0, arrived)

        start = lax.fori_loop(0, groups - 1, relay, jnp.zeros((DK, DK), f32))
        starts = run(start)[:pairs]
    starts = across_chips(starts)
    others = [trade(state, "ctx", 1, heads) for state in starts]

    share = length // parts
    partials = call(
        functools.partial(project_kernel, parts),
        [((share, width), f32)] + [((share, width), bf16)] * (parts - 1),
        [place, residual, kda_out_weight, reads, intra] + starts + others,
        [((length, heads * DK), bf16), ((length, width), f32)],
        16,
    )

    def across_heads(pieces):
        moved = {step: trade(pieces[step], "head", step, parts) for step in far_first(parts)}
        return [pieces[0]] + [moved[step] for step in range(1, parts)]

    partials = across_heads(partials)
    latent_width = latent_weight.shape[1]
    stream_rows, latent_rows, together = call(
        functools.partial(latent_kernel, parts),
        [
            ((share, width), bf16),
            ((share, latent_width), bf16),
            ((share, width + latent_width), bf16),
        ],
        [norm_gain[None], latent_weight, latent_gain[None]] + partials,
        limit=16,
    )
    latent_parts = across_heads([latent_rows, together] + [latent_rows] * (parts - 2))
    far_parts = []
    for step in range(2, parts, 2):
        far_parts.append(trade(stream_rows, "head", step, parts))
        far_parts.append(trade(far_parts[-1], "head", 1, parts))
    stream_parts = [stream_rows, latent_parts[1]] + far_parts
    latent = call(
        functools.partial(join_kernel, parts),
        [((length, latent_width), bf16)],
        [place] + latent_parts,
        limit=8,
    )[0]

    order, latents = [0], [latent]
    for step in far_first(count // 2):
        order.append(2 * step)
        latents.append(trade(latent, "ctx", 2 * step, count))
    for position in range(len(order)):
        order.append(order[position] + 1)
        latents.append(trade(latents[position], "ctx", 1, 2))
    up = up_weight.reshape(up_weight.shape[0], -1)
    heads_mla = query_weight.shape[1] // DH
    rows, latent_rows = heads_mla * length, count * length
    stream_out, attention_out = call(
        functools.partial(attend_kernel, parts, tuple(order)),
        [((length, width), bf16), ((length, heads_mla * DH), bf16)],
        [place, norm_gain[None], query_weight, up] + stream_parts + latents,
        [
            ((rows, latent_width), bf16),
            ((latent_rows, latent_width), bf16),
            ((rows, latent_rows), f32),
            ((rows, latent_rows), bf16),
            ((rows, DH), f32),
        ],
        16 + rows * latent_rows * 8 // MIB,
        cost=4.0,
    )
    return (stream_out, attention_out)


def solution(mesh):
    in_specs = (
        P(None, "ctx", "head"),
        P("ctx", "head"),
        P("ctx", "head"),
        P(None, None, "head"),
        P("head", None),
        P("ctx", None),
        P(),
        P(),
        P(),
        P(None, "head"),
        P(None, None, "head"),
    )
    out_specs = (P("ctx", None), P("ctx", "head"))
    return jax.shard_map(
        per_device, mesh=mesh, in_specs=in_specs, out_specs=out_specs, check_vma=False
    )
```

```python
import functools

import jax
import jax.numpy as jnp
from jax import lax
from jax.experimental import pallas as pl
from jax.experimental.pallas import tpu as pltpu
from jax.sharding import PartitionSpec as P

DK = 128
CONV = 4
DH = 128
HALO = 16
EXTRA = 16
MIB = 1 << 20

eps_norm = 1e-06
bf16 = jnp.bfloat16
f32 = jnp.float32
VMEM = pl.BlockSpec(memory_space=pltpu.VMEM)
SMEM = pl.BlockSpec(memory_space=pltpu.SMEM)
HBM = pl.BlockSpec(memory_space=pltpu.HBM)


def mm(left, right):
    return jnp.dot(left.astype(bf16), right.astype(bf16), preferred_element_type=f32)


def mm_nt(left, right):
    return lax.dot_general(
        left.astype(bf16), right.astype(bf16), (((1,), (1,)), ((), ())), preferred_element_type=f32
    )


def mm_tn(left, right):
    return lax.dot_general(
        left.astype(bf16), right.astype(bf16), (((0,), (0,)), ((), ())), preferred_element_type=f32
    )


def call(kernel, outs, args, scratch=(), limit=32, stored=(), copies=0, cost=1.0):
    scratch_shapes = [pltpu.VMEM(shape, dtype) for shape, dtype in scratch]
    if copies:
        scratch_shapes.append(pltpu.SemaphoreType.DMA((copies,)))
    return pl.pallas_call(
        kernel,
        out_shape=[jax.ShapeDtypeStruct(shape, dtype) for shape, dtype in outs],
        in_specs=[
            HBM if i in stored else SMEM if a.dtype == jnp.int32 else VMEM
            for i, a in enumerate(args)
        ],
        out_specs=[VMEM for _ in outs],
        scratch_shapes=scratch_shapes,
        compiler_params=pltpu.CompilerParams(vmem_limit_bytes=limit * MIB),
        cost_estimate=pl.CostEstimate(flops=int(cost * 1e9), bytes_accessed=0, transcendentals=0),
    )(*args)


def partner(index, step, size):
    return index ^ step if size & (size - 1) == 0 else (size + step - index) % size


def trade(block, axis, step, size):
    route = []
    for i in range(lax.axis_size(axis)):
        base = i // size * size
        route.append((i, base + partner(i - base, step, size)))
    return lax.ppermute(block, axis, route)


def passed_along(block, axis, distance):
    count = lax.axis_size(axis)
    return lax.ppermute(block, axis, [(i, (i + distance) % count) for i in range(count)])


def lanes(block_index, width=128):
    return pl.ds(pl.multiple_of(block_index * width, width), width)


def split_cores(place):
    return place[0] // 2, place[0] % 2


def convolved(wide, taps, part, count):
    total = None
    for tap in range(CONV):
        first = 8 - (CONV - 1) + tap
        term = taps[part, tap : tap + 1, :] * wide[first : first + count, :]
        total = term if total is None else total + term
    return total / (1.0 + jnp.exp(-total))


def finished(activated, part):
    if part == 2:
        return activated.astype(bf16)
    heads = []
    for first in range(0, activated.shape[1], DK):
        head = activated[:, first : first + DK]
        head = head * lax.rsqrt(jnp.sum(head * head, axis=-1, keepdims=True) + eps_norm)
        heads.append((head * DK ** (-0.5) if part == 0 else head).astype(bf16))
    return jnp.concatenate(heads, axis=1)


def load_kernel(stored_inputs, stored_gate, stored_taps, done, log, taps, gate, inputs, wide, sems):
    moves = [
        pltpu.make_async_copy(stored_gate, gate, sems.at[0]),
        pltpu.make_async_copy(stored_taps, taps, sems.at[1]),
        pltpu.make_async_copy(stored_inputs, inputs, sems.at[2]),
    ]
    for move in moves:
        move.start()
    length = gate.shape[0]
    rows = lax.broadcasted_iota(jnp.int32, (length, length), 0)
    cols = lax.broadcasted_iota(jnp.int32, (length, length), 1)
    tril = (rows >= cols).astype(bf16)
    moves[0].wait()
    high = gate[...].astype(bf16)
    low = gate[...] - high.astype(f32)
    log[...] = mm(tril, high) + mm(tril, low)
    moves[1].wait()
    moves[2].wait()
    for part in range(3):
        wide[:8, :] = jnp.zeros((8, wide.shape[1]), f32)
        wide[8:, :] = inputs[part].astype(f32)
        done[part] = finished(convolved(wide, taps, part, length), part)


def first_rows(place, halo, inputs, taps, part, wide):
    count = halo.shape[1]
    before = halo[part, count - 8 :, :].astype(f32)
    wide[:8, :] = jnp.where(place[2] == 0, 0.0, before)
    wide[8:, :] = inputs[part].astype(f32)
    return finished(convolved(wide, taps, part, count), part)


def whole_head(first, done, part, lane):
    return jnp.concatenate([first[:, lane], done[part, first.shape[0] :, lane]], axis=0)


def spans(log):
    half = log.shape[0] // 2
    for b in range(2):
        middle = log[b * half + half // 2 : b * half + half // 2 + 1]
        yield b, slice(b * half, (b + 1) * half), middle


def side_heads(place, pairs):
    _, core = split_cores(place)
    return [2 * i + core for i in range(pairs)] + [2 * i + 1 - core for i in range(pairs)]


def map_kernel(
    place, done, head_rows, halo, logs, beta, taps, kept, sent, solutions, shrunk, first, wide
):
    length = logs.shape[0]
    pairs = kept.shape[0]
    chunks = range(2 * pairs)
    heads = side_heads(place, pairs)
    lane = [lanes(head) for head in heads]
    rows = lax.broadcasted_iota(jnp.int32, (length, length), 0)
    cols = lax.broadcasted_iota(jnp.int32, (length, length), 1)
    eye = (rows == cols).astype(f32)
    for part in (1, 2):
        first[part - 1] = first_rows(place, halo, head_rows, taps, part, wide)

    coupling, right, finals, decay = [], [], [], []
    for i in chunks:
        key = whole_head(first.at[0], done, 1, lane[i]).astype(f32)
        value = whole_head(first.at[1], done, 2, lane[i])
        log = logs[:, lane[i]]
        rate_row = beta[pl.ds(heads[i], 1), :]
        rate_column = jnp.sum(rate_row * eye, axis=1, keepdims=True)
        last = log[length - 1 :]
        products = []
        for b, own, middle in spans(log):
            shrunk[i, b] = (key * jnp.exp(jnp.minimum(middle - log, 75.0))).astype(bf16)
            products.append(mm_nt(key[own] * jnp.exp(log[own] - middle), shrunk[i, b]))
        coupling.append(
            jnp.where(rows > cols, jnp.concatenate(products, axis=0) * rate_row, 0.0).astype(bf16)
        )
        right.append(jnp.concatenate([value, (key * jnp.exp(log)).astype(bf16)], axis=1))
        finals.append((key * jnp.exp(last - log) * rate_column).astype(bf16))
        decay.append(jnp.exp(last))

    size = 1
    inverse = None
    while size < length:
        corner = (
            (rows // (2 * size) == cols // (2 * size))
            & ((rows // size) % 2 == 1)
            & ((cols // size) % 2 == 0)
        )
        corners = [jnp.where(corner, coupling[i], jnp.zeros_like(coupling[i])) for i in chunks]
        if inverse is None:
            inverse = [eye - corners[i].astype(f32) for i in chunks]
        else:
            short = [inverse[i].astype(bf16) for i in chunks]
            below = [mm(corners[i], short[i]) for i in chunks]
            inverse = [inverse[i] - mm(short[i], below[i]) for i in chunks]
        size *= 2

    short = [inverse[i].astype(bf16) for i in chunks]
    near = [mm(short[i], right[i]).astype(bf16) for i in chunks]
    left = [right[i].astype(f32) - near[i].astype(f32) - mm(coupling[i], near[i]) for i in chunks]
    solved = [(near[i].astype(f32) + mm(short[i], left[i])).astype(bf16) for i in chunks]
    for i in chunks:
        solutions[i] = solved[i]
        maps = kept if i < pairs else sent
        put_map(maps, i % pairs, mm_tn(solved[i], finals[i]), decay[i])


def put_map(maps, i, offset_and_move, decay):
    maps[i, : 2 * DK, :] = offset_and_move.astype(bf16)
    high = decay.astype(bf16)
    low = (decay - high.astype(f32)).astype(bf16)
    maps[i, 2 * DK :, :] = jnp.concatenate(
        [jnp.broadcast_to(high, (EXTRA // 2, DK)), jnp.broadcast_to(low, (EXTRA // 2, DK))],
        axis=0,
    )


def read_kernel(place, done, head_rows, halo, logs, beta, taps, *refs):
    solutions, shrunk, stay, go, reads, intra, first, wide = refs
    length = logs.shape[0]
    pairs = stay.shape[0]
    _, core = split_cores(place)
    first[...] = first_rows(place, halo, head_rows, taps, 0, wide)
    rows = lax.broadcasted_iota(jnp.int32, (length, length), 0)
    cols = lax.broadcasted_iota(jnp.int32, (length, length), 1)
    for i, head in enumerate(side_heads(place, pairs)):
        lane = lanes(head)
        query = whole_head(first, done, 0, lane).astype(f32)
        log = logs[:, lane]
        products = [
            mm_nt(query[own] * jnp.exp(log[own] - middle), shrunk[i, b])
            for b, own, middle in spans(log)
        ]
        rate_row = beta[pl.ds(head, 1), :]
        mixing = jnp.where(rows >= cols, jnp.concatenate(products, axis=0) * rate_row, 0.0)
        high = mixing.astype(bf16)
        mixes = mm(high, solutions[i]) + mm(mixing - high.astype(f32), solutions[i])
        read = query * jnp.exp(log) - mixes[:, DK:]
        offset, move, decay = parts_of((stay if i < pairs else go)[i % pairs])
        both = mm_nt(read, jnp.concatenate([offset, move], axis=0))
        second = core == 1
        intra[:, lane] = mixes[:, :DK] + jnp.where(second, both[:, :DK], 0.0)
        reads[:, lane] = jnp.where(second, read * decay - both[:, DK:], read).astype(bf16)


def parts_of(state_map):
    extra = state_map[2 * DK :].astype(f32)
    decay = extra[:1] + extra[EXTRA // 2 : EXTRA // 2 + 1]
    return state_map[:DK], state_map[DK : 2 * DK], decay


def compose_kernel(pairs, place, kept, got, *refs):
    outs, (maps,) = refs[:pairs], refs[pairs:]
    chip, core = split_cores(place)
    eye = (
        lax.broadcasted_iota(jnp.int32, (DK, DK), 0) == lax.broadcasted_iota(jnp.int32, (DK, DK), 1)
    ).astype(f32)
    for pair in range(pairs):
        mine, other = kept[pair], got[pair]
        offset_a, move_a, decay_a = parts_of(jnp.where(core == 0, mine, other))
        offset_b, move_b, decay_b = parts_of(jnp.where(core == 0, other, mine))
        product = mm(jnp.concatenate([offset_a, move_a], axis=0), move_b)
        column = jnp.sum(eye * decay_a, axis=1, keepdims=True)
        offset = offset_a.astype(f32) * decay_b - product[:DK] + offset_b.astype(f32)
        move = move_a.astype(f32) * decay_b + column * move_b.astype(f32) - product[DK:]
        put_map(maps, pair, jnp.concatenate([offset, move], axis=0), decay_a * decay_b)
    for step in range(pairs):
        outs[step][...] = maps[partner(chip, step, pairs)]


def apply_map(state, state_map):
    offset, move, decay = parts_of(state_map)
    return state.astype(f32) * decay - mm(state, move) + offset.astype(f32)


def scan_kernel(pairs, grouped, *refs):
    place, refs = refs[0], refs[1:]
    sides, refs = (refs[:pairs], refs[pairs : 2 * pairs]), refs[2 * pairs :]
    if grouped:
        start, refs = refs[0], refs[1:]
    outs, refs = refs[:pairs], refs[pairs:]
    if grouped:
        final, refs = refs[0], refs[1:]
    maps, starts = refs
    chip, _ = split_cores(place)
    for side in range(2):
        for step in range(pairs):
            maps[side, partner(chip, step, pairs)] = sides[side][step][...]
    states = [start[side] if grouped else jnp.zeros((DK, DK), f32) for side in range(2)]
    for i in range(pairs):
        for side in range(2):
            starts[i, side] = states[side].astype(bf16)
            if i == 0 and not grouped:
                states[side] = maps[side, i, :DK, :].astype(f32)
            elif i < pairs - 1 or grouped:
                states[side] = apply_map(states[side], maps[side, i])
    if grouped:
        for side in range(2):
            final[side] = states[side]
    for step in range(pairs):
        outs[step][...] = starts[partner(chip, step, pairs)]


def project_kernel(parts, *refs):
    place, residual, weight, reads, intra = refs[:5]
    refs = refs[5:]
    pairs = reads.shape[1] // DK // 2
    starts, refs = refs[:pairs], refs[pairs:]
    outs, (whole, summed) = refs[:parts], refs[parts:]
    chip, core = split_cores(place)
    head_me = place[1]
    for step in range(pairs):
        pair = partner(chip, step, pairs)
        for side, head in enumerate((2 * pair + core, 2 * pair + 1 - core)):
            own = lanes(head)
            whole[:, own] = (intra[:, own] + mm_nt(reads[:, own], starts[step][side])).astype(bf16)
    summed[...] = jnp.dot(whole[...], weight[...], preferred_element_type=f32)
    share = summed.shape[0] // parts
    for step in range(parts):
        at = pl.ds(pl.multiple_of(partner(head_me, step, parts) * share, share), share)
        if step == 0:
            outs[0][...] = summed[at, :] + residual[at, :].astype(f32)
        else:
            outs[step][...] = summed[at, :].astype(bf16)


def normalized(values, gain):
    return values * lax.rsqrt(jnp.mean(values * values, axis=-1, keepdims=True) + eps_norm) * gain


def latent_kernel(parts, *refs):
    gain, latent_weight, latent_gain = refs[:3]
    partials = refs[3 : 3 + parts]
    stream, latent, together = refs[3 + parts :]
    width = stream.shape[1]
    total = partials[0][...]
    for step in range(1, parts):
        total = total + partials[step][...].astype(f32)
    short = total.astype(bf16)
    stream[...] = short
    together[:, :width] = short
    normed = normalized(short.astype(f32), gain[...]).astype(bf16)
    before = jnp.dot(normed, latent_weight[...], preferred_element_type=f32)
    rows = normalized(before, latent_gain[...]).astype(bf16)
    latent[...] = rows
    together[:, width:] = rows


def join_kernel(parts, *refs):
    place = refs[0]
    pieces = refs[1 : 1 + parts]
    out = refs[1 + parts]
    share = out.shape[0] // parts
    for step in range(parts):
        at = pl.ds(pl.multiple_of(partner(place[1], step, parts) * share, share), share)
        out[at, :] = pieces[step][:, pieces[step].shape[1] - out.shape[1] :]


def attend_kernel(parts, order, *refs):
    place, gain, query_weight, up = refs[:4]
    pieces, refs = refs[4 : 4 + parts], refs[4 + parts :]
    blocks, refs = refs[: len(order)], refs[len(order) :]
    stream, out, absorbed, latents, scores, weights, totals = refs
    length = stream.shape[0]
    heads = absorbed.shape[0] // length
    me = place[2]
    share = length // parts
    for step in range(parts):
        at = pl.ds(pl.multiple_of(partner(place[1], step, parts) * share, share), share)
        stream[at, :] = pieces[step][:, : stream.shape[1]]
    for position in range(len(order)):
        latents[position * length : (position + 1) * length, :] = blocks[position][...]
    normed = normalized(stream[...].astype(f32), gain[...]).astype(bf16)
    query = jnp.dot(normed, query_weight[...], preferred_element_type=f32).astype(bf16)
    for head in range(heads):
        own = slice(head * DH, (head + 1) * DH)
        absorbed[head * length : (head + 1) * length, :] = (
            mm_nt(query[:, own], up[:, own]) * DH ** (-0.5)
        ).astype(bf16)
    scores[...] = mm_nt(absorbed[...], latents[...])
    group = min(length, 32)
    for first in range(0, heads * length, group):
        own = slice(first, first + group)
        rows = lax.broadcasted_iota(jnp.int32, (group, length), 0) + first % length
        cols = lax.broadcasted_iota(jnp.int32, (group, length), 1)
        allowed = [rows >= cols] + [(me ^ distance) < me for distance in order[1:]]
        masked = [
            jnp.where(allowed[p], scores[own, p * length : (p + 1) * length], -1e30)
            for p in range(len(order))
        ]
        peak = jnp.max(functools.reduce(jnp.maximum, masked), axis=-1, keepdims=True)
        shares = [jnp.exp(part - peak) for part in masked]
        total = jnp.sum(functools.reduce(jnp.add, shares), axis=-1, keepdims=True)
        totals[own, :] = jnp.broadcast_to(total, (group, totals.shape[1]))
        for p in range(len(order)):
            weights[own, p * length : (p + 1) * length] = shares[p].astype(bf16)
    mixed = jnp.dot(weights[...], latents[...], preferred_element_type=f32)
    for head in range(heads):
        own = slice(head * length, (head + 1) * length)
        value = slice((heads + head) * DH, (heads + head + 1) * DH)
        outcome = mm(mixed[own], up[:, value])
        out[:, head * DH : (head + 1) * DH] = (outcome / totals[own, :]).astype(bf16)


def far_first(count):
    return sorted(range(1, count), key=lambda step: (-bin(step).count("1"), -step))


def per_device(
    kda_inputs,
    gate_log,
    beta,
    conv_weight,
    kda_out_weight,
    residual,
    norm_gain,
    latent_weight,
    latent_gain,
    query_weight,
    up_weight,
):
    length, width = residual.shape
    heads = beta.shape[1]
    pairs = heads // 2
    count, parts = lax.axis_size("ctx"), lax.axis_size("head")
    groups = count // heads
    ctx_me = lax.axis_index("ctx").astype(jnp.int32)
    place = jnp.stack([ctx_me % heads, lax.axis_index("head").astype(jnp.int32), ctx_me])

    halo = passed_along(kda_inputs[:, length - HALO :, :], "ctx", 1)
    stored = [
        pltpu.with_memory_space_constraint(a, pltpu.HBM) for a in (kda_inputs, gate_log, conv_weight)
    ]
    done, logs, taps = call(
        load_kernel,
        [(kda_inputs.shape, bf16), (gate_log.shape, f32), (conv_weight.shape, f32)],
        stored,
        [
            (gate_log.shape, f32),
            (kda_inputs.shape, bf16),
            ((length + 8, heads * DK), f32),
        ],
        24,
        stored=(0, 1, 2),
        copies=3,
        cost=2.0,
    )
    map_shape = (2 * DK + EXTRA, DK)
    head_rows = kda_inputs[:, :HALO, :]
    arguments = [place, done, head_rows, halo, logs, beta.T, taps]
    kept, sent, solutions, shrunk = call(
        map_kernel,
        [
            ((pairs,) + map_shape, bf16),
            ((pairs,) + map_shape, bf16),
            ((heads, length, 2 * DK), bf16),
            ((heads, 2, length, DK), bf16),
        ],
        arguments,
        [((2, HALO, heads * DK), bf16), ((HALO + 8, heads * DK), f32)],
        16,
        cost=5.0,
    )

    got = trade(sent, "ctx", 1, heads)
    got_kept = trade(kept, "ctx", 1, heads)
    reads, intra = call(
        read_kernel,
        [((length, heads * DK), bf16), ((length, heads * DK), f32)],
        arguments + [solutions, shrunk, got, got_kept],
        [((HALO, heads * DK), bf16), ((HALO + 8, heads * DK), f32)],
        16,
        cost=2.5,
    )
    chip_maps = call(
        functools.partial(compose_kernel, pairs),
        [(map_shape, bf16)] * pairs,
        [place, kept, got],
        [((pairs,) + map_shape, bf16)],
        8,
    )

    def across_chips(pieces):
        moved = {step: trade(pieces[step], "ctx", 2 * step, heads) for step in far_first(pairs)}
        return [pieces[0]] + [moved[step] for step in range(1, pairs)]

    chip_maps, reads, intra = lax.optimization_barrier((across_chips(chip_maps), reads, intra))
    other_maps = [trade(one, "ctx", 1, heads) for one in chip_maps]
    state_outs = [((2, DK, DK), bf16)] * pairs
    scratch = [((2, pairs) + map_shape, bf16), ((pairs, 2, DK, DK), bf16)]

    def run(*start):
        return call(
            functools.partial(scan_kernel, pairs, len(start) > 0),
            state_outs + [((2, DK, DK), f32)] * len(start),
            [place] + chip_maps + other_maps + list(start),
            scratch,
            8,
        )

    if groups == 1:
        starts = run()
    else:

        def relay(step_index, start):
            arrived = passed_along(run(start)[pairs], "ctx", heads)
            return jnp.where(ctx_me < heads, 0.0, arrived)

        start = lax.fori_loop(0, groups - 1, relay, jnp.zeros((2, DK, DK), f32))
        starts = run(start)[:pairs]
    starts = across_chips(starts)

    share = length // parts
    partials = call(
        functools.partial(project_kernel, parts),
        [((share, width), f32)] + [((share, width), bf16)] * (parts - 1),
        [place, residual, kda_out_weight, reads, intra] + starts,
        [((length, heads * DK), bf16), ((length, width), f32)],
        16,
    )

    def across_heads(pieces):
        moved = {step: trade(pieces[step], "head", step, parts) for step in far_first(parts)}
        return [pieces[0]] + [moved[step] for step in range(1, parts)]

    up = up_weight.reshape(up_weight.shape[0], -1)
    partials, up = lax.optimization_barrier((across_heads(partials), up))
    latent_width = latent_weight.shape[1]
    stream_rows, latent_rows, together = call(
        functools.partial(latent_kernel, parts),
        [
            ((share, width), bf16),
            ((share, latent_width), bf16),
            ((share, width + latent_width), bf16),
        ],
        [norm_gain[None], latent_weight, latent_gain[None]] + partials,
        limit=16,
    )
    latent_parts = across_heads([latent_rows, together] + [latent_rows] * (parts - 2))
    far_parts = []
    for step in range(2, parts, 2):
        far_parts.append(trade(stream_rows, "head", step, parts))
        far_parts.append(trade(far_parts[-1], "head", 1, parts))
    stream_parts = [stream_rows, latent_parts[1]] + far_parts
    latent = call(
        functools.partial(join_kernel, parts),
        [((length, latent_width), bf16)],
        [place] + latent_parts,
        limit=8,
    )[0]

    order, latents = [0], [latent]
    for step in far_first(count // 2):
        order.append(2 * step)
        latents.append(trade(latent, "ctx", 2 * step, count))
    for position in range(len(order)):
        order.append(order[position] + 1)
        latents.append(trade(latents[position], "ctx", 1, 2))
    heads_mla = query_weight.shape[1] // DH
    rows, latent_rows = heads_mla * length, count * length
    stream_out, attention_out = call(
        functools.partial(attend_kernel, parts, tuple(order)),
        [((length, width), bf16), ((length, heads_mla * DH), bf16)],
        [place, norm_gain[None], query_weight, up] + stream_parts + latents,
        [
            ((rows, latent_width), bf16),
            ((latent_rows, latent_width), bf16),
            ((rows, latent_rows), f32),
            ((rows, latent_rows), bf16),
            ((rows, DH), f32),
        ],
        16 + rows * latent_rows * 8 // MIB,
        cost=4.0,
    )
    return (stream_out, attention_out)


def solution(mesh):
    in_specs = (
        P(None, "ctx", "head"),
        P("ctx", "head"),
        P("ctx", "head"),
        P(None, None, "head"),
        P("head", None),
        P("ctx", None),
        P(),
        P(),
        P(),
        P(None, "head"),
        P(None, None, "head"),
    )
    out_specs = (P("ctx", None), P("ctx", "head"))
    return jax.shard_map(
        per_device, mesh=mesh, in_specs=in_specs, out_specs=out_specs, check_vma=False
    )
```

```python
import functools

import jax
import jax.numpy as jnp
from jax import lax
from jax.experimental import pallas as pl
from jax.experimental.pallas import tpu as pltpu
from jax.sharding import PartitionSpec as P

DK = 128
CONV = 4
DH = 128
HALO = 16
EXTRA = 16
MIB = 1 << 20

eps_norm = 1e-06
bf16 = jnp.bfloat16
f32 = jnp.float32
VMEM = pl.BlockSpec(memory_space=pltpu.VMEM)
HBM = pl.BlockSpec(memory_space=pltpu.HBM)


def mm(left, right):
    return jnp.dot(left.astype(bf16), right.astype(bf16), preferred_element_type=f32)


def mm_nt(left, right):
    return lax.dot_general(
        left.astype(bf16), right.astype(bf16), (((1,), (1,)), ((), ())), preferred_element_type=f32
    )


def mm_tn(left, right):
    return lax.dot_general(
        left.astype(bf16), right.astype(bf16), (((0,), (0,)), ((), ())), preferred_element_type=f32
    )


def call(kernel, outs, args, scratch=(), limit=32, stored=(), copies=0, cost=1.0):
    scratch_shapes = [pltpu.VMEM(shape, dtype) for shape, dtype in scratch]
    if copies:
        scratch_shapes.append(pltpu.SemaphoreType.DMA((copies,)))
    return pl.pallas_call(
        kernel,
        out_shape=[jax.ShapeDtypeStruct(shape, dtype) for shape, dtype in outs],
        in_specs=[HBM if i in stored else VMEM for i in range(len(args))],
        out_specs=[VMEM for _ in outs],
        scratch_shapes=scratch_shapes,
        compiler_params=pltpu.CompilerParams(vmem_limit_bytes=limit * MIB),
        cost_estimate=pl.CostEstimate(flops=int(cost * 1e9), bytes_accessed=0, transcendentals=0),
    )(*args)


def partner(index, step, size):
    return index ^ step if size & (size - 1) == 0 else (size + step - index) % size


def trade(block, axis, step, size):
    route = []
    for i in range(lax.axis_size(axis)):
        base = i // size * size
        route.append((i, base + partner(i - base, step, size)))
    return lax.ppermute(block, axis, route)


def passed_along(block, axis, distance):
    count = lax.axis_size(axis)
    return lax.ppermute(block, axis, [(i, (i + distance) % count) for i in range(count)])


def lanes(block_index, width=128):
    return pl.ds(pl.multiple_of(block_index * width, width), width)


def here(heads):
    token_index = lax.axis_index("ctx")
    return lax.rem(token_index, heads), lax.axis_index("head"), token_index


def split_cores(place):
    return place[0] // 2, place[0] % 2


def convolved(wide, taps, part, count):
    total = None
    for tap in range(CONV):
        first = 8 - (CONV - 1) + tap
        term = taps[part, tap : tap + 1, :] * wide[first : first + count, :]
        total = term if total is None else total + term
    return total / (1.0 + jnp.exp(-total))


def finished(activated, part):
    if part == 2:
        return activated.astype(bf16)
    heads = []
    for first in range(0, activated.shape[1], DK):
        head = activated[:, first : first + DK]
        head = head * lax.rsqrt(jnp.sum(head * head, axis=-1, keepdims=True) + eps_norm)
        heads.append((head * DK ** (-0.5) if part == 0 else head).astype(bf16))
    return jnp.concatenate(heads, axis=1)


def load_kernel(stored_inputs, stored_gate, stored_taps, done, log, taps, gate, inputs, wide, sems):
    moves = [
        pltpu.make_async_copy(stored_gate, gate, sems.at[0]),
        pltpu.make_async_copy(stored_taps, taps, sems.at[1]),
        pltpu.make_async_copy(stored_inputs, inputs, sems.at[2]),
    ]
    for move in moves:
        move.start()
    length = gate.shape[0]
    rows = lax.broadcasted_iota(jnp.int32, (length, length), 0)
    cols = lax.broadcasted_iota(jnp.int32, (length, length), 1)
    tril = (rows >= cols).astype(bf16)
    moves[0].wait()
    high = gate[...].astype(bf16)
    low = gate[...] - high.astype(f32)
    log[...] = mm(tril, high) + mm(tril, low)
    moves[1].wait()
    moves[2].wait()
    for part in range(3):
        wide[:8, :] = jnp.zeros((8, wide.shape[1]), f32)
        wide[8:, :] = inputs[part].astype(f32)
        done[part] = finished(convolved(wide, taps, part, length), part)


def first_rows(place, halo, inputs, taps, part, wide):
    count = halo.shape[1]
    before = halo[part, count - 8 :, :].astype(f32)
    wide[:8, :] = jnp.where(place[2] == 0, 0.0, before)
    wide[8:, :] = inputs[part].astype(f32)
    return finished(convolved(wide, taps, part, count), part)


def whole_head(first, done, part, lane):
    return jnp.concatenate([first[:, lane], done[part, first.shape[0] :, lane]], axis=0)


def spans(log):
    half = log.shape[0] // 2
    for b in range(2):
        middle = log[b * half + half // 2 : b * half + half // 2 + 1]
        yield b, slice(b * half, (b + 1) * half), middle


def side_heads(place, pairs):
    _, core = split_cores(place)
    return [2 * i + core for i in range(pairs)] + [2 * i + 1 - core for i in range(pairs)]


def map_kernel(
    done, head_rows, halo, logs, beta, taps, kept, sent, solutions, shrunk, first, wide
):
    length = logs.shape[0]
    pairs = kept.shape[0]
    place = here(2 * pairs)
    chunks = range(2 * pairs)
    heads = side_heads(place, pairs)
    lane = [lanes(head) for head in heads]
    rows = lax.broadcasted_iota(jnp.int32, (length, length), 0)
    cols = lax.broadcasted_iota(jnp.int32, (length, length), 1)
    eye = (rows == cols).astype(f32)
    for part in (1, 2):
        first[part - 1] = first_rows(place, halo, head_rows, taps, part, wide)

    coupling, right, finals, decay = [], [], [], []
    for i in chunks:
        key = whole_head(first.at[0], done, 1, lane[i]).astype(f32)
        value = whole_head(first.at[1], done, 2, lane[i])
        log = logs[:, lane[i]]
        rate_row = beta[pl.ds(heads[i], 1), :]
        rate_column = jnp.sum(rate_row * eye, axis=1, keepdims=True)
        last = log[length - 1 :]
        products = []
        for b, own, middle in spans(log):
            shrunk[i, b] = (key * jnp.exp(jnp.minimum(middle - log, 75.0))).astype(bf16)
            products.append(mm_nt(key[own] * jnp.exp(log[own] - middle), shrunk[i, b]))
        coupling.append(
            jnp.where(rows > cols, jnp.concatenate(products, axis=0) * rate_row, 0.0).astype(bf16)
        )
        right.append(jnp.concatenate([value, (key * jnp.exp(log)).astype(bf16)], axis=1))
        finals.append((key * jnp.exp(last - log) * rate_column).astype(bf16))
        decay.append(jnp.exp(last))

    size = 1
    inverse = None
    while size < length:
        corner = (
            (rows // (2 * size) == cols // (2 * size))
            & ((rows // size) % 2 == 1)
            & ((cols // size) % 2 == 0)
        )
        corners = [jnp.where(corner, coupling[i], jnp.zeros_like(coupling[i])) for i in chunks]
        if inverse is None:
            inverse = [eye - corners[i].astype(f32) for i in chunks]
        else:
            short = [inverse[i].astype(bf16) for i in chunks]
            below = [mm(corners[i], short[i]) for i in chunks]
            inverse = [inverse[i] - mm(short[i], below[i]) for i in chunks]
        size *= 2

    short = [inverse[i].astype(bf16) for i in chunks]
    near = [mm(short[i], right[i]).astype(bf16) for i in chunks]
    left = [right[i].astype(f32) - near[i].astype(f32) - mm(coupling[i], near[i]) for i in chunks]
    solved = [(near[i].astype(f32) + mm(short[i], left[i])).astype(bf16) for i in chunks]
    for i in chunks:
        solutions[i] = solved[i]
        maps = kept if i < pairs else sent
        put_map(maps, i % pairs, mm_tn(solved[i], finals[i]), decay[i])


def put_map(maps, i, offset_and_move, decay):
    maps[i, : 2 * DK, :] = offset_and_move.astype(bf16)
    high = decay.astype(bf16)
    low = (decay - high.astype(f32)).astype(bf16)
    maps[i, 2 * DK :, :] = jnp.concatenate(
        [jnp.broadcast_to(high, (EXTRA // 2, DK)), jnp.broadcast_to(low, (EXTRA // 2, DK))],
        axis=0,
    )


def read_kernel(done, head_rows, halo, logs, beta, taps, *refs):
    solutions, shrunk, stay, go, reads, intra, first, wide = refs
    length = logs.shape[0]
    pairs = stay.shape[0]
    place = here(2 * pairs)
    _, core = split_cores(place)
    first[...] = first_rows(place, halo, head_rows, taps, 0, wide)
    rows = lax.broadcasted_iota(jnp.int32, (length, length), 0)
    cols = lax.broadcasted_iota(jnp.int32, (length, length), 1)
    for i, head in enumerate(side_heads(place, pairs)):
        lane = lanes(head)
        query = whole_head(first, done, 0, lane).astype(f32)
        log = logs[:, lane]
        products = [
            mm_nt(query[own] * jnp.exp(log[own] - middle), shrunk[i, b])
            for b, own, middle in spans(log)
        ]
        rate_row = beta[pl.ds(head, 1), :]
        mixing = jnp.where(rows >= cols, jnp.concatenate(products, axis=0) * rate_row, 0.0)
        high = mixing.astype(bf16)
        mixes = mm(high, solutions[i]) + mm(mixing - high.astype(f32), solutions[i])
        read = query * jnp.exp(log) - mixes[:, DK:]
        offset, move, decay = parts_of((stay if i < pairs else go)[i % pairs])
        both = mm_nt(read, jnp.concatenate([offset, move], axis=0))
        second = core == 1
        intra[:, lane] = mixes[:, :DK] + jnp.where(second, both[:, :DK], 0.0)
        reads[:, lane] = jnp.where(second, read * decay - both[:, DK:], read).astype(bf16)


def parts_of(state_map):
    extra = state_map[2 * DK :].astype(f32)
    decay = extra[:1] + extra[EXTRA // 2 : EXTRA // 2 + 1]
    return state_map[:DK], state_map[DK : 2 * DK], decay


def compose_kernel(pairs, kept, got, *refs):
    outs, (maps,) = refs[:pairs], refs[pairs:]
    chip, core = split_cores(here(2 * pairs))
    eye = (
        lax.broadcasted_iota(jnp.int32, (DK, DK), 0) == lax.broadcasted_iota(jnp.int32, (DK, DK), 1)
    ).astype(f32)
    for pair in range(pairs):
        mine, other = kept[pair], got[pair]
        offset_a, move_a, decay_a = parts_of(jnp.where(core == 0, mine, other))
        offset_b, move_b, decay_b = parts_of(jnp.where(core == 0, other, mine))
        product = mm(jnp.concatenate([offset_a, move_a], axis=0), move_b)
        column = jnp.sum(eye * decay_a, axis=1, keepdims=True)
        offset = offset_a.astype(f32) * decay_b - product[:DK] + offset_b.astype(f32)
        move = move_a.astype(f32) * decay_b + column * move_b.astype(f32) - product[DK:]
        put_map(maps, pair, jnp.concatenate([offset, move], axis=0), decay_a * decay_b)
    for step in range(pairs):
        outs[step][...] = maps[partner(chip, step, pairs)]


def apply_map(state, state_map):
    offset, move, decay = parts_of(state_map)
    return state.astype(f32) * decay - mm(state, move) + offset.astype(f32)


def scan_kernel(pairs, grouped, *refs):
    sides, refs = (refs[:pairs], refs[pairs : 2 * pairs]), refs[2 * pairs :]
    if grouped:
        start, refs = refs[0], refs[1:]
    outs, refs = refs[:pairs], refs[pairs:]
    if grouped:
        final, refs = refs[0], refs[1:]
    maps, starts = refs
    chip, _ = split_cores(here(2 * pairs))
    for side in range(2):
        for step in range(pairs):
            maps[side, partner(chip, step, pairs)] = sides[side][step][...]
    states = [start[side] if grouped else jnp.zeros((DK, DK), f32) for side in range(2)]
    for i in range(pairs):
        for side in range(2):
            starts[i, side] = states[side].astype(bf16)
            if i == 0 and not grouped:
                states[side] = maps[side, i, :DK, :].astype(f32)
            elif i < pairs - 1 or grouped:
                states[side] = apply_map(states[side], maps[side, i])
    if grouped:
        for side in range(2):
            final[side] = states[side]
    for step in range(pairs):
        outs[step][...] = starts[partner(chip, step, pairs)]


def project_kernel(parts, *refs):
    residual, weight, reads, intra = refs[:4]
    refs = refs[4:]
    pairs = reads.shape[1] // DK // 2
    place = here(2 * pairs)
    starts, refs = refs[:pairs], refs[pairs:]
    outs, (whole, summed) = refs[:parts], refs[parts:]
    chip, core = split_cores(place)
    head_me = place[1]
    for step in range(pairs):
        pair = partner(chip, step, pairs)
        for side, head in enumerate((2 * pair + core, 2 * pair + 1 - core)):
            own = lanes(head)
            whole[:, own] = (intra[:, own] + mm_nt(reads[:, own], starts[step][side])).astype(bf16)
    summed[...] = jnp.dot(whole[...], weight[...], preferred_element_type=f32)
    share = summed.shape[0] // parts
    for step in range(parts):
        at = pl.ds(pl.multiple_of(partner(head_me, step, parts) * share, share), share)
        if step == 0:
            outs[0][...] = summed[at, :] + residual[at, :].astype(f32)
        else:
            outs[step][...] = summed[at, :].astype(bf16)


def normalized(values, gain):
    return values * lax.rsqrt(jnp.mean(values * values, axis=-1, keepdims=True) + eps_norm) * gain


def latent_kernel(parts, *refs):
    gain, latent_weight, latent_gain = refs[:3]
    partials = refs[3 : 3 + parts]
    stream, latent, together = refs[3 + parts :]
    width = stream.shape[1]
    total = partials[0][...]
    for step in range(1, parts):
        total = total + partials[step][...].astype(f32)
    short = total.astype(bf16)
    stream[...] = short
    together[:, :width] = short
    normed = normalized(short.astype(f32), gain[...]).astype(bf16)
    before = jnp.dot(normed, latent_weight[...], preferred_element_type=f32)
    rows = normalized(before, latent_gain[...]).astype(bf16)
    latent[...] = rows
    together[:, width:] = rows


def join_kernel(parts, *refs):
    pieces = refs[:parts]
    out = refs[parts]
    share = out.shape[0] // parts
    for step in range(parts):
        at = pl.ds(pl.multiple_of(partner(lax.axis_index("head"), step, parts) * share, share), share)
        out[at, :] = pieces[step][:, pieces[step].shape[1] - out.shape[1] :]


def attend_kernel(parts, order, *refs):
    gain, query_weight, up = refs[:3]
    pieces, refs = refs[3 : 3 + parts], refs[3 + parts :]
    blocks, refs = refs[: len(order)], refs[len(order) :]
    stream, out, absorbed, latents, scores, weights, totals = refs
    length = stream.shape[0]
    heads = absorbed.shape[0] // length
    me = lax.axis_index("ctx")
    share = length // parts
    for step in range(parts):
        at = pl.ds(pl.multiple_of(partner(lax.axis_index("head"), step, parts) * share, share), share)
        stream[at, :] = pieces[step][:, : stream.shape[1]]
    for position in range(len(order)):
        latents[position * length : (position + 1) * length, :] = blocks[position][...]
    normed = normalized(stream[...].astype(f32), gain[...]).astype(bf16)
    query = jnp.dot(normed, query_weight[...], preferred_element_type=f32).astype(bf16)
    for head in range(heads):
        own = slice(head * DH, (head + 1) * DH)
        absorbed[head * length : (head + 1) * length, :] = (
            mm_nt(query[:, own], up[:, own]) * DH ** (-0.5)
        ).astype(bf16)
    scores[...] = mm_nt(absorbed[...], latents[...])
    group = min(length, 32)
    for first in range(0, heads * length, group):
        own = slice(first, first + group)
        rows = lax.broadcasted_iota(jnp.int32, (group, length), 0) + first % length
        cols = lax.broadcasted_iota(jnp.int32, (group, length), 1)
        allowed = [rows >= cols] + [(me ^ distance) < me for distance in order[1:]]
        masked = [
            jnp.where(allowed[p], scores[own, p * length : (p + 1) * length], -1e30)
            for p in range(len(order))
        ]
        peak = jnp.max(functools.reduce(jnp.maximum, masked), axis=-1, keepdims=True)
        shares = [jnp.exp(part - peak) for part in masked]
        total = jnp.sum(functools.reduce(jnp.add, shares), axis=-1, keepdims=True)
        totals[own, :] = jnp.broadcast_to(total, (group, totals.shape[1]))
        for p in range(len(order)):
            weights[own, p * length : (p + 1) * length] = shares[p].astype(bf16)
    mixed = jnp.dot(weights[...], latents[...], preferred_element_type=f32)
    for head in range(heads):
        own = slice(head * length, (head + 1) * length)
        value = slice((heads + head) * DH, (heads + head + 1) * DH)
        outcome = mm(mixed[own], up[:, value])
        out[:, head * DH : (head + 1) * DH] = (outcome / totals[own, :]).astype(bf16)


def far_first(count):
    return sorted(range(1, count), key=lambda step: (-bin(step).count("1"), -step))


def per_device(
    kda_inputs,
    gate_log,
    beta,
    conv_weight,
    kda_out_weight,
    residual,
    norm_gain,
    latent_weight,
    latent_gain,
    query_weight,
    up_weight,
):
    length, width = residual.shape
    heads = beta.shape[1]
    pairs = heads // 2
    count, parts = lax.axis_size("ctx"), lax.axis_size("head")
    groups = count // heads

    halo = passed_along(kda_inputs[:, length - HALO :, :], "ctx", 1)
    stored = [
        pltpu.with_memory_space_constraint(a, pltpu.HBM) for a in (kda_inputs, gate_log, conv_weight)
    ]
    done, logs, taps = call(
        load_kernel,
        [(kda_inputs.shape, bf16), (gate_log.shape, f32), (conv_weight.shape, f32)],
        stored,
        [
            (gate_log.shape, f32),
            (kda_inputs.shape, bf16),
            ((length + 8, heads * DK), f32),
        ],
        24,
        stored=(0, 1, 2),
        copies=3,
        cost=2.0,
    )
    map_shape = (2 * DK + EXTRA, DK)
    head_rows = kda_inputs[:, :HALO, :]
    arguments = [done, head_rows, halo, logs, beta.T, taps]
    kept, sent, solutions, shrunk = call(
        map_kernel,
        [
            ((pairs,) + map_shape, bf16),
            ((pairs,) + map_shape, bf16),
            ((heads, length, 2 * DK), bf16),
            ((heads, 2, length, DK), bf16),
        ],
        arguments,
        [((2, HALO, heads * DK), bf16), ((HALO + 8, heads * DK), f32)],
        16,
        cost=5.0,
    )

    got = trade(sent, "ctx", 1, heads)
    got_kept = trade(kept, "ctx", 1, heads)
    reads, intra = call(
        read_kernel,
        [((length, heads * DK), bf16), ((length, heads * DK), f32)],
        arguments + [solutions, shrunk, got, got_kept],
        [((HALO, heads * DK), bf16), ((HALO + 8, heads * DK), f32)],
        16,
        cost=2.5,
    )
    chip_maps = call(
        functools.partial(compose_kernel, pairs),
        [(map_shape, bf16)] * pairs,
        [kept, got],
        [((pairs,) + map_shape, bf16)],
        8,
    )

    def across_chips(pieces):
        moved = {step: trade(pieces[step], "ctx", 2 * step, heads) for step in far_first(pairs)}
        return [pieces[0]] + [moved[step] for step in range(1, pairs)]

    chip_maps, reads, intra = lax.optimization_barrier((across_chips(chip_maps), reads, intra))
    other_maps = [trade(one, "ctx", 1, heads) for one in chip_maps]
    state_outs = [((2, DK, DK), bf16)] * pairs
    scratch = [((2, pairs) + map_shape, bf16), ((pairs, 2, DK, DK), bf16)]

    def run(*start):
        return call(
            functools.partial(scan_kernel, pairs, len(start) > 0),
            state_outs + [((2, DK, DK), f32)] * len(start),
            chip_maps + other_maps + list(start),
            scratch,
            8,
        )

    if groups == 1:
        starts = run()
    else:

        def relay(step_index, start):
            arrived = passed_along(run(start)[pairs], "ctx", heads)
            return jnp.where(lax.axis_index("ctx") < heads, 0.0, arrived)

        start = lax.fori_loop(0, groups - 1, relay, jnp.zeros((2, DK, DK), f32))
        starts = run(start)[:pairs]
    starts = across_chips(starts)

    share = length // parts
    partials = call(
        functools.partial(project_kernel, parts),
        [((share, width), f32)] + [((share, width), bf16)] * (parts - 1),
        [residual, kda_out_weight, reads, intra] + starts,
        [((length, heads * DK), bf16), ((length, width), f32)],
        16,
    )

    def across_heads(pieces):
        moved = {step: trade(pieces[step], "head", step, parts) for step in far_first(parts)}
        return [pieces[0]] + [moved[step] for step in range(1, parts)]

    up = up_weight.reshape(up_weight.shape[0], -1)
    partials, up = lax.optimization_barrier((across_heads(partials), up))
    latent_width = latent_weight.shape[1]
    stream_rows, latent_rows, together = call(
        functools.partial(latent_kernel, parts),
        [
            ((share, width), bf16),
            ((share, latent_width), bf16),
            ((share, width + latent_width), bf16),
        ],
        [norm_gain[None], latent_weight, latent_gain[None]] + partials,
        limit=16,
    )
    latent_parts = across_heads([latent_rows, together] + [latent_rows] * (parts - 2))
    far_parts = []
    for step in range(2, parts, 2):
        far_parts.append(trade(stream_rows, "head", step, parts))
        far_parts.append(trade(far_parts[-1], "head", 1, parts))
    stream_parts = [stream_rows, latent_parts[1]] + far_parts
    latent = call(
        functools.partial(join_kernel, parts),
        [((length, latent_width), bf16)],
        latent_parts,
        limit=8,
    )[0]

    order, latents = [0], [latent]
    for step in far_first(count // 2):
        order.append(2 * step)
        latents.append(trade(latent, "ctx", 2 * step, count))
    for position in range(len(order)):
        order.append(order[position] + 1)
        latents.append(trade(latents[position], "ctx", 1, 2))
    heads_mla = query_weight.shape[1] // DH
    rows, latent_rows = heads_mla * length, count * length
    stream_out, attention_out = call(
        functools.partial(attend_kernel, parts, tuple(order)),
        [((length, width), bf16), ((length, heads_mla * DH), bf16)],
        [norm_gain[None], query_weight, up] + stream_parts + latents,
        [
            ((rows, latent_width), bf16),
            ((latent_rows, latent_width), bf16),
            ((rows, latent_rows), f32),
            ((rows, latent_rows), bf16),
            ((rows, DH), f32),
        ],
        16 + rows * latent_rows * 8 // MIB,
        cost=4.0,
    )
    return (stream_out, attention_out)


def solution(mesh):
    in_specs = (
        P(None, "ctx", "head"),
        P("ctx", "head"),
        P("ctx", "head"),
        P(None, None, "head"),
        P("head", None),
        P("ctx", None),
        P(),
        P(),
        P(),
        P(None, "head"),
        P(None, None, "head"),
    )
    out_specs = (P("ctx", None), P("ctx", "head"))
    return jax.shard_map(
        per_device, mesh=mesh, in_specs=in_specs, out_specs=out_specs, check_vma=False
    )
```

```python
import functools

import jax
import jax.numpy as jnp
from jax import lax
from jax.experimental import pallas as pl
from jax.experimental.pallas import tpu as pltpu
from jax.sharding import PartitionSpec as P

DK = 128
CONV = 4
DH = 128
HALO = 16
EXTRA = 16
MIB = 1 << 20

eps_norm = 1e-06
bf16 = jnp.bfloat16
f32 = jnp.float32
VMEM = pl.BlockSpec(memory_space=pltpu.VMEM)
HBM = pl.BlockSpec(memory_space=pltpu.HBM)


def mm(left, right):
    return jnp.dot(left.astype(bf16), right.astype(bf16), preferred_element_type=f32)


def mm_nt(left, right):
    return lax.dot_general(
        left.astype(bf16), right.astype(bf16), (((1,), (1,)), ((), ())), preferred_element_type=f32
    )


def mm_tn(left, right):
    return lax.dot_general(
        left.astype(bf16), right.astype(bf16), (((0,), (0,)), ((), ())), preferred_element_type=f32
    )


def call(kernel, outs, args, scratch=(), limit=32, stored=(), copies=0, cost=1.0):
    scratch_shapes = [pltpu.VMEM(shape, dtype) for shape, dtype in scratch]
    if copies:
        scratch_shapes.append(pltpu.SemaphoreType.DMA((copies,)))
    return pl.pallas_call(
        kernel,
        out_shape=[jax.ShapeDtypeStruct(shape, dtype) for shape, dtype in outs],
        in_specs=[HBM if i in stored else VMEM for i in range(len(args))],
        out_specs=[VMEM for _ in outs],
        scratch_shapes=scratch_shapes,
        compiler_params=pltpu.CompilerParams(vmem_limit_bytes=limit * MIB),
        cost_estimate=pl.CostEstimate(flops=int(cost * 1e9), bytes_accessed=0, transcendentals=0),
    )(*args)


def partner(index, step, size):
    return index ^ step if size & (size - 1) == 0 else (size + step - index) % size


def trade(block, axis, step, size):
    route = []
    for i in range(lax.axis_size(axis)):
        base = i // size * size
        route.append((i, base + partner(i - base, step, size)))
    return lax.ppermute(block, axis, route)


def passed_along(block, axis, distance):
    count = lax.axis_size(axis)
    return lax.ppermute(block, axis, [(i, (i + distance) % count) for i in range(count)])


def lanes(block_index, width=128):
    return pl.ds(pl.multiple_of(block_index * width, width), width)


def here(heads):
    token_index = lax.axis_index("ctx")
    return lax.rem(token_index, heads), lax.axis_index("head"), token_index


def split_cores(place):
    return place[0] // 2, place[0] % 2


def convolved(wide, taps, part, count):
    total = None
    for tap in range(CONV):
        first = 8 - (CONV - 1) + tap
        term = taps[part, tap : tap + 1, :] * wide[first : first + count, :]
        total = term if total is None else total + term
    return total / (1.0 + jnp.exp(-total))


def finished(activated, part):
    if part == 2:
        return activated.astype(bf16)
    heads = []
    for first in range(0, activated.shape[1], DK):
        head = activated[:, first : first + DK]
        head = head * lax.rsqrt(jnp.sum(head * head, axis=-1, keepdims=True) + eps_norm)
        heads.append((head * DK ** (-0.5) if part == 0 else head).astype(bf16))
    return jnp.concatenate(heads, axis=1)


def last_rows_kernel(stored_inputs, rows, sems):
    length, count = stored_inputs.shape[1], rows.shape[1]
    move = pltpu.make_async_copy(
        stored_inputs.at[:, length - count : length, :], rows, sems.at[0]
    )
    move.start()
    move.wait()


def load_kernel(
    stored_inputs, stored_gate, stored_taps, done, head_rows, log, taps, gate, inputs, wide, sems
):
    moves = [
        pltpu.make_async_copy(stored_gate, gate, sems.at[0]),
        pltpu.make_async_copy(stored_taps, taps, sems.at[1]),
        pltpu.make_async_copy(stored_inputs, inputs, sems.at[2]),
    ]
    for move in moves:
        move.start()
    length = gate.shape[0]
    rows = lax.broadcasted_iota(jnp.int32, (length, length), 0)
    cols = lax.broadcasted_iota(jnp.int32, (length, length), 1)
    tril = (rows >= cols).astype(bf16)
    moves[0].wait()
    high = gate[...].astype(bf16)
    low = gate[...] - high.astype(f32)
    log[...] = mm(tril, high) + mm(tril, low)
    moves[1].wait()
    moves[2].wait()
    head_rows[...] = inputs[:, : head_rows.shape[1], :]
    for part in range(3):
        wide[:8, :] = jnp.zeros((8, wide.shape[1]), f32)
        wide[8:, :] = inputs[part].astype(f32)
        done[part] = finished(convolved(wide, taps, part, length), part)


def first_rows(place, halo, inputs, taps, part, wide):
    count = halo.shape[1]
    before = halo[part, count - 8 :, :].astype(f32)
    wide[:8, :] = jnp.where(place[2] == 0, 0.0, before)
    wide[8:, :] = inputs[part].astype(f32)
    return finished(convolved(wide, taps, part, count), part)


def whole_head(first, done, part, lane):
    return jnp.concatenate([first[:, lane], done[part, first.shape[0] :, lane]], axis=0)


def spans(log):
    half = log.shape[0] // 2
    for b in range(2):
        middle = log[b * half + half // 2 : b * half + half // 2 + 1]
        yield b, slice(b * half, (b + 1) * half), middle


def side_heads(place, pairs):
    _, core = split_cores(place)
    return [2 * i + core for i in range(pairs)] + [2 * i + 1 - core for i in range(pairs)]


def map_kernel(
    done, head_rows, halo, logs, beta, taps, kept, sent, solutions, shrunk, first, wide
):
    length = logs.shape[0]
    pairs = kept.shape[0]
    place = here(2 * pairs)
    chunks = range(2 * pairs)
    heads = side_heads(place, pairs)
    lane = [lanes(head) for head in heads]
    rows = lax.broadcasted_iota(jnp.int32, (length, length), 0)
    cols = lax.broadcasted_iota(jnp.int32, (length, length), 1)
    eye = (rows == cols).astype(f32)
    for part in (1, 2):
        first[part - 1] = first_rows(place, halo, head_rows, taps, part, wide)

    coupling, right, finals, decay = [], [], [], []
    for i in chunks:
        key = whole_head(first.at[0], done, 1, lane[i]).astype(f32)
        value = whole_head(first.at[1], done, 2, lane[i])
        log = logs[:, lane[i]]
        rate_row = beta[pl.ds(heads[i], 1), :]
        rate_column = jnp.sum(rate_row * eye, axis=1, keepdims=True)
        last = log[length - 1 :]
        products = []
        for b, own, middle in spans(log):
            shrunk[i, b] = (key * jnp.exp(jnp.minimum(middle - log, 75.0))).astype(bf16)
            products.append(mm_nt(key[own] * jnp.exp(log[own] - middle), shrunk[i, b]))
        coupling.append(
            jnp.where(rows > cols, jnp.concatenate(products, axis=0) * rate_row, 0.0).astype(bf16)
        )
        right.append(jnp.concatenate([value, (key * jnp.exp(log)).astype(bf16)], axis=1))
        finals.append((key * jnp.exp(last - log) * rate_column).astype(bf16))
        decay.append(jnp.exp(last))

    size = 1
    inverse = None
    while size < length:
        corner = (
            (rows // (2 * size) == cols // (2 * size))
            & ((rows // size) % 2 == 1)
            & ((cols // size) % 2 == 0)
        )
        corners = [jnp.where(corner, coupling[i], jnp.zeros_like(coupling[i])) for i in chunks]
        if inverse is None:
            inverse = [eye - corners[i].astype(f32) for i in chunks]
        else:
            short = [inverse[i].astype(bf16) for i in chunks]
            below = [mm(corners[i], short[i]) for i in chunks]
            inverse = [inverse[i] - mm(short[i], below[i]) for i in chunks]
        size *= 2

    short = [inverse[i].astype(bf16) for i in chunks]
    near = [mm(short[i], right[i]).astype(bf16) for i in chunks]
    left = [right[i].astype(f32) - near[i].astype(f32) - mm(coupling[i], near[i]) for i in chunks]
    solved = [(near[i].astype(f32) + mm(short[i], left[i])).astype(bf16) for i in chunks]
    for i in chunks:
        solutions[i] = solved[i]
        maps = kept if i < pairs else sent
        put_map(maps, i % pairs, mm_tn(solved[i], finals[i]), decay[i])


def put_map(maps, i, offset_and_move, decay):
    maps[i, : 2 * DK, :] = offset_and_move.astype(bf16)
    high = decay.astype(bf16)
    low = (decay - high.astype(f32)).astype(bf16)
    maps[i, 2 * DK :, :] = jnp.concatenate(
        [jnp.broadcast_to(high, (EXTRA // 2, DK)), jnp.broadcast_to(low, (EXTRA // 2, DK))],
        axis=0,
    )


def read_kernel(done, head_rows, halo, logs, beta, taps, *refs):
    solutions, shrunk, stay, go, reads, intra, first, wide = refs
    length = logs.shape[0]
    pairs = stay.shape[0]
    place = here(2 * pairs)
    _, core = split_cores(place)
    first[...] = first_rows(place, halo, head_rows, taps, 0, wide)
    rows = lax.broadcasted_iota(jnp.int32, (length, length), 0)
    cols = lax.broadcasted_iota(jnp.int32, (length, length), 1)
    for i, head in enumerate(side_heads(place, pairs)):
        lane = lanes(head)
        query = whole_head(first, done, 0, lane).astype(f32)
        log = logs[:, lane]
        products = [
            mm_nt(query[own] * jnp.exp(log[own] - middle), shrunk[i, b])
            for b, own, middle in spans(log)
        ]
        rate_row = beta[pl.ds(head, 1), :]
        mixing = jnp.where(rows >= cols, jnp.concatenate(products, axis=0) * rate_row, 0.0)
        high = mixing.astype(bf16)
        mixes = mm(high, solutions[i]) + mm(mixing - high.astype(f32), solutions[i])
        read = query * jnp.exp(log) - mixes[:, DK:]
        offset, move, decay = parts_of((stay if i < pairs else go)[i % pairs])
        both = mm_nt(read, jnp.concatenate([offset, move], axis=0))
        second = core == 1
        intra[:, lane] = mixes[:, :DK] + jnp.where(second, both[:, :DK], 0.0)
        reads[:, lane] = jnp.where(second, read * decay - both[:, DK:], read).astype(bf16)


def parts_of(state_map):
    extra = state_map[2 * DK :].astype(f32)
    decay = extra[:1] + extra[EXTRA // 2 : EXTRA // 2 + 1]
    return state_map[:DK], state_map[DK : 2 * DK], decay


def compose_kernel(pairs, kept, got, *refs):
    outs, (maps,) = refs[:pairs], refs[pairs:]
    chip, core = split_cores(here(2 * pairs))
    eye = (
        lax.broadcasted_iota(jnp.int32, (DK, DK), 0) == lax.broadcasted_iota(jnp.int32, (DK, DK), 1)
    ).astype(f32)
    for pair in range(pairs):
        mine, other = kept[pair], got[pair]
        offset_a, move_a, decay_a = parts_of(jnp.where(core == 0, mine, other))
        offset_b, move_b, decay_b = parts_of(jnp.where(core == 0, other, mine))
        product = mm(jnp.concatenate([offset_a, move_a], axis=0), move_b)
        column = jnp.sum(eye * decay_a, axis=1, keepdims=True)
        offset = offset_a.astype(f32) * decay_b - product[:DK] + offset_b.astype(f32)
        move = move_a.astype(f32) * decay_b + column * move_b.astype(f32) - product[DK:]
        put_map(maps, pair, jnp.concatenate([offset, move], axis=0), decay_a * decay_b)
    for step in range(pairs):
        outs[step][...] = maps[partner(chip, step, pairs)]


def apply_map(state, state_map):
    offset, move, decay = parts_of(state_map)
    return state.astype(f32) * decay - mm(state, move) + offset.astype(f32)


def stack_kernel(pairs, *refs):
    blocks, (maps,) = refs[:pairs], refs[pairs:]
    chip, _ = split_cores(here(2 * pairs))
    for step in range(pairs):
        maps[partner(chip, step, pairs)] = blocks[step][...]


def scan_kernel(pairs, grouped, *refs):
    maps, refs = refs[:2], refs[2:]
    if grouped:
        start, refs = refs[0], refs[1:]
    outs, refs = refs[:pairs], refs[pairs:]
    if grouped:
        final, refs = refs[0], refs[1:]
    starts = refs[0]
    chip, _ = split_cores(here(2 * pairs))
    states = [start[side] if grouped else jnp.zeros((DK, DK), f32) for side in range(2)]
    for i in range(pairs):
        for side in range(2):
            starts[i, side] = states[side].astype(bf16)
            if i == 0 and not grouped:
                states[side] = maps[side][i, :DK, :].astype(f32)
            elif i < pairs - 1 or grouped:
                states[side] = apply_map(states[side], maps[side][i])
    if grouped:
        for side in range(2):
            final[side] = states[side]
    for step in range(pairs):
        outs[step][...] = starts[partner(chip, step, pairs)]


def project_kernel(parts, *refs):
    residual, weight, reads, intra = refs[:4]
    refs = refs[4:]
    pairs = reads.shape[1] // DK // 2
    place = here(2 * pairs)
    starts, refs = refs[:pairs], refs[pairs:]
    outs, (whole, summed) = refs[:parts], refs[parts:]
    chip, core = split_cores(place)
    head_me = place[1]
    for step in range(pairs):
        pair = partner(chip, step, pairs)
        for side, head in enumerate((2 * pair + core, 2 * pair + 1 - core)):
            own = lanes(head)
            whole[:, own] = (intra[:, own] + mm_nt(reads[:, own], starts[step][side])).astype(bf16)
    summed[...] = jnp.dot(whole[...], weight[...], preferred_element_type=f32)
    share = summed.shape[0] // parts
    for step in range(parts):
        at = pl.ds(pl.multiple_of(partner(head_me, step, parts) * share, share), share)
        if step == 0:
            outs[0][...] = summed[at, :] + residual[at, :].astype(f32)
        else:
            outs[step][...] = summed[at, :].astype(bf16)


def normalized(values, gain):
    return values * lax.rsqrt(jnp.mean(values * values, axis=-1, keepdims=True) + eps_norm) * gain


def latent_kernel(parts, *refs):
    gain, latent_weight, latent_gain = refs[:3]
    partials = refs[3 : 3 + parts]
    stream, latent, together = refs[3 + parts :]
    width = stream.shape[1]
    total = partials[0][...]
    for step in range(1, parts):
        total = total + partials[step][...].astype(f32)
    short = total.astype(bf16)
    stream[...] = short
    together[:, :width] = short
    normed = normalized(short.astype(f32), gain[...]).astype(bf16)
    before = jnp.dot(normed, latent_weight[...], preferred_element_type=f32)
    rows = normalized(before, latent_gain[...]).astype(bf16)
    latent[...] = rows
    together[:, width:] = rows


def join_kernel(parts, *refs):
    pieces = refs[:parts]
    out = refs[parts]
    share = out.shape[0] // parts
    for step in range(parts):
        at = pl.ds(pl.multiple_of(partner(lax.axis_index("head"), step, parts) * share, share), share)
        out[at, :] = pieces[step][:, pieces[step].shape[1] - out.shape[1] :]


def attend_kernel(parts, order, *refs):
    gain, query_weight, up = refs[:3]
    pieces, refs = refs[3 : 3 + parts], refs[3 + parts :]
    blocks, refs = refs[: len(order)], refs[len(order) :]
    stream, out, absorbed, latents, scores, weights, totals = refs
    length = stream.shape[0]
    heads = absorbed.shape[0] // length
    me = lax.axis_index("ctx")
    share = length // parts
    for step in range(parts):
        at = pl.ds(pl.multiple_of(partner(lax.axis_index("head"), step, parts) * share, share), share)
        stream[at, :] = pieces[step][:, : stream.shape[1]]
    for position in range(len(order)):
        latents[position * length : (position + 1) * length, :] = blocks[position][...]
    normed = normalized(stream[...].astype(f32), gain[...]).astype(bf16)
    query = jnp.dot(normed, query_weight[...], preferred_element_type=f32).astype(bf16)
    for head in range(heads):
        own = slice(head * DH, (head + 1) * DH)
        absorbed[head * length : (head + 1) * length, :] = (
            mm_nt(query[:, own], up[:, own]) * DH ** (-0.5)
        ).astype(bf16)
    scores[...] = mm_nt(absorbed[...], latents[...])
    group = min(length, 32)
    for first in range(0, heads * length, group):
        own = slice(first, first + group)
        rows = lax.broadcasted_iota(jnp.int32, (group, length), 0) + first % length
        cols = lax.broadcasted_iota(jnp.int32, (group, length), 1)
        allowed = [rows >= cols] + [(me ^ distance) < me for distance in order[1:]]
        masked = [
            jnp.where(allowed[p], scores[own, p * length : (p + 1) * length], -1e30)
            for p in range(len(order))
        ]
        peak = jnp.max(functools.reduce(jnp.maximum, masked), axis=-1, keepdims=True)
        shares = [jnp.exp(part - peak) for part in masked]
        total = jnp.sum(functools.reduce(jnp.add, shares), axis=-1, keepdims=True)
        totals[own, :] = jnp.broadcast_to(total, (group, totals.shape[1]))
        for p in range(len(order)):
            weights[own, p * length : (p + 1) * length] = shares[p].astype(bf16)
    mixed = jnp.dot(weights[...], latents[...], preferred_element_type=f32)
    for head in range(heads):
        own = slice(head * length, (head + 1) * length)
        value = slice((heads + head) * DH, (heads + head + 1) * DH)
        outcome = mm(mixed[own], up[:, value])
        out[:, head * DH : (head + 1) * DH] = (outcome / totals[own, :]).astype(bf16)


def far_first(count):
    return sorted(range(1, count), key=lambda step: (-bin(step).count("1"), -step))


def per_device(
    kda_inputs,
    gate_log,
    beta,
    conv_weight,
    kda_out_weight,
    residual,
    norm_gain,
    latent_weight,
    latent_gain,
    query_weight,
    up_weight,
):
    length, width = residual.shape
    heads = beta.shape[1]
    pairs = heads // 2
    count, parts = lax.axis_size("ctx"), lax.axis_size("head")
    groups = count // heads

    stored = [
        pltpu.with_memory_space_constraint(a, pltpu.HBM) for a in (kda_inputs, gate_log, conv_weight)
    ]
    edge_shape = (kda_inputs.shape[0], HALO, kda_inputs.shape[2])
    last_rows = call(
        last_rows_kernel, [(edge_shape, bf16)], stored[:1], limit=8, stored=(0,), copies=1, cost=0.2
    )[0]
    halo = passed_along(last_rows, "ctx", 1)
    done, head_rows, logs, taps = call(
        load_kernel,
        [
            (kda_inputs.shape, bf16),
            (edge_shape, bf16),
            (gate_log.shape, f32),
            (conv_weight.shape, f32),
        ],
        stored,
        [
            (gate_log.shape, f32),
            (kda_inputs.shape, bf16),
            ((length + 8, heads * DK), f32),
        ],
        24,
        stored=(0, 1, 2),
        copies=3,
        cost=2.0,
    )
    map_shape = (2 * DK + EXTRA, DK)
    arguments = [done, head_rows, halo, logs, beta.T, taps]
    kept, sent, solutions, shrunk = call(
        map_kernel,
        [
            ((pairs,) + map_shape, bf16),
            ((pairs,) + map_shape, bf16),
            ((heads, length, 2 * DK), bf16),
            ((heads, 2, length, DK), bf16),
        ],
        arguments,
        [((2, HALO, heads * DK), bf16), ((HALO + 8, heads * DK), f32)],
        16,
        cost=5.0,
    )

    got = trade(sent, "ctx", 1, heads)
    got_kept = trade(kept, "ctx", 1, heads)
    reads, intra = call(
        read_kernel,
        [((length, heads * DK), bf16), ((length, heads * DK), f32)],
        arguments + [solutions, shrunk, got, got_kept],
        [((HALO, heads * DK), bf16), ((HALO + 8, heads * DK), f32)],
        16,
        cost=2.5,
    )
    chip_maps = call(
        functools.partial(compose_kernel, pairs),
        [(map_shape, bf16)] * pairs,
        [kept, got],
        [((pairs,) + map_shape, bf16)],
        8,
    )

    def across_chips(pieces):
        moved = {step: trade(pieces[step], "ctx", 2 * step, heads) for step in far_first(pairs)}
        return [pieces[0]] + [moved[step] for step in range(1, pairs)]

    chip_maps, reads, intra = lax.optimization_barrier((across_chips(chip_maps), reads, intra))
    chip_maps = call(
        functools.partial(stack_kernel, pairs),
        [((pairs,) + map_shape, bf16)],
        chip_maps,
        limit=8,
        cost=0.2,
    )[0]
    other_maps = trade(chip_maps, "ctx", 1, heads)
    state_outs = [((2, DK, DK), bf16)] * pairs
    scratch = [((pairs, 2, DK, DK), bf16)]

    def run(*start):
        return call(
            functools.partial(scan_kernel, pairs, len(start) > 0),
            state_outs + [((2, DK, DK), f32)] * len(start),
            [chip_maps, other_maps] + list(start),
            scratch,
            8,
        )

    if groups == 1:
        starts = run()
    else:

        def relay(step_index, start):
            arrived = passed_along(run(start)[pairs], "ctx", heads)
            return jnp.where(lax.axis_index("ctx") < heads, 0.0, arrived)

        start = lax.fori_loop(0, groups - 1, relay, jnp.zeros((2, DK, DK), f32))
        starts = run(start)[:pairs]
    starts = across_chips(starts)

    share = length // parts
    partials = call(
        functools.partial(project_kernel, parts),
        [((share, width), f32)] + [((share, width), bf16)] * (parts - 1),
        [residual, kda_out_weight, reads, intra] + starts,
        [((length, heads * DK), bf16), ((length, width), f32)],
        16,
    )

    def across_heads(pieces):
        moved = {step: trade(pieces[step], "head", step, parts) for step in far_first(parts)}
        return [pieces[0]] + [moved[step] for step in range(1, parts)]

    up = up_weight.reshape(up_weight.shape[0], -1)
    partials, up = lax.optimization_barrier((across_heads(partials), up))
    latent_width = latent_weight.shape[1]
    stream_rows, latent_rows, together = call(
        functools.partial(latent_kernel, parts),
        [
            ((share, width), bf16),
            ((share, latent_width), bf16),
            ((share, width + latent_width), bf16),
        ],
        [norm_gain[None], latent_weight, latent_gain[None]] + partials,
        limit=16,
    )
    latent_parts = across_heads([latent_rows, together] + [latent_rows] * (parts - 2))
    far_parts = []
    for step in range(2, parts, 2):
        far_parts.append(trade(stream_rows, "head", step, parts))
        far_parts.append(trade(far_parts[-1], "head", 1, parts))
    stream_parts = [stream_rows, latent_parts[1]] + far_parts
    latent = call(
        functools.partial(join_kernel, parts),
        [((length, latent_width), bf16)],
        latent_parts,
        limit=8,
    )[0]

    order, latents = [0], [latent]
    for step in far_first(count // 2):
        order.append(2 * step)
        latents.append(trade(latent, "ctx", 2 * step, count))
    for position in range(len(order)):
        order.append(order[position] + 1)
        latents.append(trade(latents[position], "ctx", 1, 2))
    heads_mla = query_weight.shape[1] // DH
    rows, latent_rows = heads_mla * length, count * length
    stream_out, attention_out = call(
        functools.partial(attend_kernel, parts, tuple(order)),
        [((length, width), bf16), ((length, heads_mla * DH), bf16)],
        [norm_gain[None], query_weight, up] + stream_parts + latents,
        [
            ((rows, latent_width), bf16),
            ((latent_rows, latent_width), bf16),
            ((rows, latent_rows), f32),
            ((rows, latent_rows), bf16),
            ((rows, DH), f32),
        ],
        16 + rows * latent_rows * 8 // MIB,
        cost=4.0,
    )
    return (stream_out, attention_out)


def solution(mesh):
    in_specs = (
        P(None, "ctx", "head"),
        P("ctx", "head"),
        P("ctx", "head"),
        P(None, None, "head"),
        P("head", None),
        P("ctx", None),
        P(),
        P(),
        P(),
        P(None, "head"),
        P(None, None, "head"),
    )
    out_specs = (P("ctx", None), P("ctx", "head"))
    return jax.shard_map(
        per_device, mesh=mesh, in_specs=in_specs, out_specs=out_specs, check_vma=False
    )
```

```python
import functools

import jax
import jax.numpy as jnp
from jax import lax
from jax.experimental import pallas as pl
from jax.experimental.pallas import tpu as pltpu
from jax.sharding import PartitionSpec as P

DK = 128
CONV = 4
DH = 128
HALO = 16
EXTRA = 16
MIB = 1 << 20

eps_norm = 1e-06
bf16 = jnp.bfloat16
f32 = jnp.float32
VMEM = pl.BlockSpec(memory_space=pltpu.VMEM)
HBM = pl.BlockSpec(memory_space=pltpu.HBM)


def mm(left, right):
    return jnp.dot(left.astype(bf16), right.astype(bf16), preferred_element_type=f32)


def mm_nt(left, right):
    return lax.dot_general(
        left.astype(bf16), right.astype(bf16), (((1,), (1,)), ((), ())), preferred_element_type=f32
    )


def mm_tn(left, right):
    return lax.dot_general(
        left.astype(bf16), right.astype(bf16), (((0,), (0,)), ((), ())), preferred_element_type=f32
    )


def call(kernel, outs, args, scratch=(), limit=32, stored=(), copies=0, cost=1.0):
    scratch_shapes = [pltpu.VMEM(shape, dtype) for shape, dtype in scratch]
    if copies:
        scratch_shapes.append(pltpu.SemaphoreType.DMA((copies,)))
    return pl.pallas_call(
        kernel,
        out_shape=[jax.ShapeDtypeStruct(shape, dtype) for shape, dtype in outs],
        in_specs=[HBM if i in stored else VMEM for i in range(len(args))],
        out_specs=[VMEM for _ in outs],
        scratch_shapes=scratch_shapes,
        compiler_params=pltpu.CompilerParams(vmem_limit_bytes=limit * MIB),
        cost_estimate=pl.CostEstimate(flops=int(cost * 1e9), bytes_accessed=0, transcendentals=0),
    )(*args)


def partner(index, step, size):
    return index ^ step if size & (size - 1) == 0 else (size + step - index) % size


def trade(block, axis, step, size):
    route = []
    for i in range(lax.axis_size(axis)):
        base = i // size * size
        route.append((i, base + partner(i - base, step, size)))
    return lax.ppermute(block, axis, route)


def passed_along(block, axis, distance):
    count = lax.axis_size(axis)
    return lax.ppermute(block, axis, [(i, (i + distance) % count) for i in range(count)])


def lanes(block_index, width=128):
    return pl.ds(pl.multiple_of(block_index * width, width), width)


def here(heads):
    token_index = lax.axis_index("ctx")
    return lax.rem(token_index, heads), lax.axis_index("head"), token_index


def split_cores(place):
    return place[0] // 2, place[0] % 2


def convolved(wide, taps, part, count):
    total = None
    for tap in range(CONV):
        first = 8 - (CONV - 1) + tap
        term = taps[part, tap : tap + 1, :] * wide[first : first + count, :]
        total = term if total is None else total + term
    return total / (1.0 + jnp.exp(-total))


def finished(activated, part):
    if part == 2:
        return activated.astype(bf16)
    heads = []
    for first in range(0, activated.shape[1], DK):
        head = activated[:, first : first + DK]
        head = head * lax.rsqrt(jnp.sum(head * head, axis=-1, keepdims=True) + eps_norm)
        heads.append((head * DK ** (-0.5) if part == 0 else head).astype(bf16))
    return jnp.concatenate(heads, axis=1)


def last_rows_kernel(stored_inputs, packed, rows, sems):
    length, count = stored_inputs.shape[1], rows.shape[1]
    move = pltpu.make_async_copy(
        stored_inputs.at[:, length - count : length, :], rows, sems.at[0]
    )
    move.start()
    move.wait()
    reach = CONV - 1
    last = [rows[part].astype(f32)[count - reach :] for part in range(rows.shape[0])]
    spare = jnp.zeros((packed.shape[0] - reach * len(last), packed.shape[1]), f32)
    packed[...] = jnp.concatenate(last + [spare], axis=0).astype(bf16)


def load_kernel(
    stored_inputs, stored_gate, stored_taps, done, head_rows, log, taps, gate, inputs, wide, sems
):
    moves = [
        pltpu.make_async_copy(stored_gate, gate, sems.at[0]),
        pltpu.make_async_copy(stored_taps, taps, sems.at[1]),
        pltpu.make_async_copy(stored_inputs, inputs, sems.at[2]),
    ]
    for move in moves:
        move.start()
    length = gate.shape[0]
    rows = lax.broadcasted_iota(jnp.int32, (length, length), 0)
    cols = lax.broadcasted_iota(jnp.int32, (length, length), 1)
    tril = (rows >= cols).astype(bf16)
    moves[0].wait()
    high = gate[...].astype(bf16)
    low = gate[...] - high.astype(f32)
    log[...] = mm(tril, high) + mm(tril, low)
    moves[1].wait()
    moves[2].wait()
    head_rows[...] = inputs[:, : head_rows.shape[1], :]
    for part in range(3):
        wide[:8, :] = jnp.zeros((8, wide.shape[1]), f32)
        wide[8:, :] = inputs[part].astype(f32)
        done[part] = finished(convolved(wide, taps, part, length), part)


def first_rows(place, halo, inputs, taps, part, wide):
    count, reach = inputs.shape[1], CONV - 1
    before = halo[...].astype(f32)[part * reach : (part + 1) * reach]
    wide[8 - reach : 8, :] = jnp.where(place[2] == 0, 0.0, before)
    wide[8:, :] = inputs[part].astype(f32)
    return finished(convolved(wide, taps, part, count), part)


def whole_head(first, done, part, lane):
    return jnp.concatenate([first[:, lane], done[part, first.shape[0] :, lane]], axis=0)


def spans(log):
    half = log.shape[0] // 2
    for b in range(2):
        middle = log[b * half + half // 2 : b * half + half // 2 + 1]
        yield b, slice(b * half, (b + 1) * half), middle


def side_heads(place, pairs):
    _, core = split_cores(place)
    return [2 * i + core for i in range(pairs)] + [2 * i + 1 - core for i in range(pairs)]


def map_kernel(
    done, head_rows, halo, logs, beta, taps, kept, sent, solutions, shrunk, first, wide
):
    length = logs.shape[0]
    pairs = kept.shape[0]
    place = here(2 * pairs)
    chunks = range(2 * pairs)
    heads = side_heads(place, pairs)
    lane = [lanes(head) for head in heads]
    rows = lax.broadcasted_iota(jnp.int32, (length, length), 0)
    cols = lax.broadcasted_iota(jnp.int32, (length, length), 1)
    eye = (rows == cols).astype(f32)
    for part in (1, 2):
        first[part - 1] = first_rows(place, halo, head_rows, taps, part, wide)

    coupling, right, finals, decay = [], [], [], []
    for i in chunks:
        key = whole_head(first.at[0], done, 1, lane[i]).astype(f32)
        value = whole_head(first.at[1], done, 2, lane[i])
        log = logs[:, lane[i]]
        rate_row = beta[pl.ds(heads[i], 1), :]
        rate_column = jnp.sum(rate_row * eye, axis=1, keepdims=True)
        last = log[length - 1 :]
        products = []
        for b, own, middle in spans(log):
            shrunk[i, b] = (key * jnp.exp(jnp.minimum(middle - log, 75.0))).astype(bf16)
            products.append(mm_nt(key[own] * jnp.exp(log[own] - middle), shrunk[i, b]))
        coupling.append(
            jnp.where(rows > cols, jnp.concatenate(products, axis=0) * rate_row, 0.0).astype(bf16)
        )
        right.append(jnp.concatenate([value, (key * jnp.exp(log)).astype(bf16)], axis=1))
        finals.append((key * jnp.exp(last - log) * rate_column).astype(bf16))
        decay.append(jnp.exp(last))

    size = 1
    inverse = None
    while size < length:
        corner = (
            (rows // (2 * size) == cols // (2 * size))
            & ((rows // size) % 2 == 1)
            & ((cols // size) % 2 == 0)
        )
        corners = [jnp.where(corner, coupling[i], jnp.zeros_like(coupling[i])) for i in chunks]
        if inverse is None:
            inverse = [eye - corners[i].astype(f32) for i in chunks]
        else:
            short = [inverse[i].astype(bf16) for i in chunks]
            below = [mm(corners[i], short[i]) for i in chunks]
            inverse = [inverse[i] - mm(short[i], below[i]) for i in chunks]
        size *= 2

    short = [inverse[i].astype(bf16) for i in chunks]
    near = [mm(short[i], right[i]).astype(bf16) for i in chunks]
    left = [right[i].astype(f32) - near[i].astype(f32) - mm(coupling[i], near[i]) for i in chunks]
    solved = [(near[i].astype(f32) + mm(short[i], left[i])).astype(bf16) for i in chunks]
    for i in chunks:
        solutions[i] = solved[i]
        maps = kept if i < pairs else sent
        put_map(maps, i % pairs, mm_tn(solved[i], finals[i]), decay[i])


def put_map(maps, i, offset_and_move, decay):
    maps[i, : 2 * DK, :] = offset_and_move.astype(bf16)
    high = decay.astype(bf16)
    low = (decay - high.astype(f32)).astype(bf16)
    maps[i, 2 * DK :, :] = jnp.concatenate(
        [jnp.broadcast_to(high, (EXTRA // 2, DK)), jnp.broadcast_to(low, (EXTRA // 2, DK))],
        axis=0,
    )


def read_kernel(done, head_rows, halo, logs, beta, taps, *refs):
    solutions, shrunk, stay, go, reads, intra, first, wide = refs
    length = logs.shape[0]
    pairs = stay.shape[0]
    place = here(2 * pairs)
    _, core = split_cores(place)
    first[...] = first_rows(place, halo, head_rows, taps, 0, wide)
    rows = lax.broadcasted_iota(jnp.int32, (length, length), 0)
    cols = lax.broadcasted_iota(jnp.int32, (length, length), 1)
    for i, head in enumerate(side_heads(place, pairs)):
        lane = lanes(head)
        query = whole_head(first, done, 0, lane).astype(f32)
        log = logs[:, lane]
        products = [
            mm_nt(query[own] * jnp.exp(log[own] - middle), shrunk[i, b])
            for b, own, middle in spans(log)
        ]
        rate_row = beta[pl.ds(head, 1), :]
        mixing = jnp.where(rows >= cols, jnp.concatenate(products, axis=0) * rate_row, 0.0)
        high = mixing.astype(bf16)
        mixes = mm(high, solutions[i]) + mm(mixing - high.astype(f32), solutions[i])
        read = query * jnp.exp(log) - mixes[:, DK:]
        offset, move, decay = parts_of((stay if i < pairs else go)[i % pairs])
        both = mm_nt(read, jnp.concatenate([offset, move], axis=0))
        second = core == 1
        intra[:, lane] = mixes[:, :DK] + jnp.where(second, both[:, :DK], 0.0)
        reads[:, lane] = jnp.where(second, read * decay - both[:, DK:], read).astype(bf16)


def parts_of(state_map):
    extra = state_map[2 * DK :].astype(f32)
    decay = extra[:1] + extra[EXTRA // 2 : EXTRA // 2 + 1]
    return state_map[:DK], state_map[DK : 2 * DK], decay


def compose_kernel(pairs, kept, got, *refs):
    outs, (maps,) = refs[:pairs], refs[pairs:]
    chip, core = split_cores(here(2 * pairs))
    eye = (
        lax.broadcasted_iota(jnp.int32, (DK, DK), 0) == lax.broadcasted_iota(jnp.int32, (DK, DK), 1)
    ).astype(f32)
    for pair in range(pairs):
        mine, other = kept[pair], got[pair]
        offset_a, move_a, decay_a = parts_of(jnp.where(core == 0, mine, other))
        offset_b, move_b, decay_b = parts_of(jnp.where(core == 0, other, mine))
        product = mm(jnp.concatenate([offset_a, move_a], axis=0), move_b)
        column = jnp.sum(eye * decay_a, axis=1, keepdims=True)
        offset = offset_a.astype(f32) * decay_b - product[:DK] + offset_b.astype(f32)
        move = move_a.astype(f32) * decay_b + column * move_b.astype(f32) - product[DK:]
        put_map(maps, pair, jnp.concatenate([offset, move], axis=0), decay_a * decay_b)
    for step in range(pairs):
        outs[step][...] = maps[partner(chip, step, pairs)]


def apply_map(state, state_map):
    offset, move, decay = parts_of(state_map)
    return state.astype(f32) * decay - mm(state, move) + offset.astype(f32)


def stack_kernel(pairs, *refs):
    blocks, (maps,) = refs[:pairs], refs[pairs:]
    chip, _ = split_cores(here(2 * pairs))
    for step in range(pairs):
        maps[partner(chip, step, pairs)] = blocks[step][...]


def scan_kernel(pairs, grouped, *refs):
    maps, refs = refs[:2], refs[2:]
    if grouped:
        start, refs = refs[0], refs[1:]
    outs, refs = refs[:pairs], refs[pairs:]
    if grouped:
        final, refs = refs[0], refs[1:]
    starts = refs[0]
    chip, _ = split_cores(here(2 * pairs))
    states = [start[side] if grouped else jnp.zeros((DK, DK), f32) for side in range(2)]
    for i in range(pairs):
        for side in range(2):
            starts[i, side] = states[side].astype(bf16)
            if i == 0 and not grouped:
                states[side] = maps[side][i, :DK, :].astype(f32)
            elif i < pairs - 1 or grouped:
                states[side] = apply_map(states[side], maps[side][i])
    if grouped:
        for side in range(2):
            final[side] = states[side]
    for step in range(pairs):
        outs[step][...] = starts[partner(chip, step, pairs)]


def project_kernel(parts, *refs):
    residual, weight, reads, intra = refs[:4]
    refs = refs[4:]
    pairs = reads.shape[1] // DK // 2
    place = here(2 * pairs)
    starts, refs = refs[:pairs], refs[pairs:]
    outs, (whole, summed) = refs[:parts], refs[parts:]
    chip, core = split_cores(place)
    head_me = place[1]
    for step in range(pairs):
        pair = partner(chip, step, pairs)
        for side, head in enumerate((2 * pair + core, 2 * pair + 1 - core)):
            own = lanes(head)
            whole[:, own] = (intra[:, own] + mm_nt(reads[:, own], starts[step][side])).astype(bf16)
    summed[...] = jnp.dot(whole[...], weight[...], preferred_element_type=f32)
    share = summed.shape[0] // parts
    for step in range(parts):
        at = pl.ds(pl.multiple_of(partner(head_me, step, parts) * share, share), share)
        if step == 0:
            outs[0][...] = summed[at, :] + residual[at, :].astype(f32)
        else:
            outs[step][...] = summed[at, :].astype(bf16)


def normalized(values, gain):
    return values * lax.rsqrt(jnp.mean(values * values, axis=-1, keepdims=True) + eps_norm) * gain


def latent_kernel(parts, *refs):
    gain, latent_weight, latent_gain = refs[:3]
    partials = refs[3 : 3 + parts]
    stream, latent, together = refs[3 + parts :]
    width = stream.shape[1]
    total = partials[0][...]
    for step in range(1, parts):
        total = total + partials[step][...].astype(f32)
    short = total.astype(bf16)
    stream[...] = short
    together[:, :width] = short
    normed = normalized(short.astype(f32), gain[...]).astype(bf16)
    before = jnp.dot(normed, latent_weight[...], preferred_element_type=f32)
    rows = normalized(before, latent_gain[...]).astype(bf16)
    latent[...] = rows
    together[:, width:] = rows


def join_kernel(parts, *refs):
    pieces = refs[:parts]
    out = refs[parts]
    share = out.shape[0] // parts
    for step in range(parts):
        at = pl.ds(pl.multiple_of(partner(lax.axis_index("head"), step, parts) * share, share), share)
        out[at, :] = pieces[step][:, pieces[step].shape[1] - out.shape[1] :]


def attend_kernel(parts, order, *refs):
    gain, query_weight, up = refs[:3]
    pieces, refs = refs[3 : 3 + parts], refs[3 + parts :]
    blocks, refs = refs[: len(order)], refs[len(order) :]
    stream, out, absorbed, latents, scores, weights, totals = refs
    length = stream.shape[0]
    heads = absorbed.shape[0] // length
    me = lax.axis_index("ctx")
    share = length // parts
    for step in range(parts):
        at = pl.ds(pl.multiple_of(partner(lax.axis_index("head"), step, parts) * share, share), share)
        stream[at, :] = pieces[step][:, : stream.shape[1]]
    for position in range(len(order)):
        latents[position * length : (position + 1) * length, :] = blocks[position][...]
    normed = normalized(stream[...].astype(f32), gain[...]).astype(bf16)
    query = jnp.dot(normed, query_weight[...], preferred_element_type=f32).astype(bf16)
    for head in range(heads):
        own = slice(head * DH, (head + 1) * DH)
        absorbed[head * length : (head + 1) * length, :] = (
            mm_nt(query[:, own], up[:, own]) * DH ** (-0.5)
        ).astype(bf16)
    scores[...] = mm_nt(absorbed[...], latents[...])
    group = min(length, 32)
    for first in range(0, heads * length, group):
        own = slice(first, first + group)
        rows = lax.broadcasted_iota(jnp.int32, (group, length), 0) + first % length
        cols = lax.broadcasted_iota(jnp.int32, (group, length), 1)
        allowed = [rows >= cols] + [(me ^ distance) < me for distance in order[1:]]
        masked = [
            jnp.where(allowed[p], scores[own, p * length : (p + 1) * length], -1e30)
            for p in range(len(order))
        ]
        peak = jnp.max(functools.reduce(jnp.maximum, masked), axis=-1, keepdims=True)
        shares = [jnp.exp(part - peak) for part in masked]
        total = jnp.sum(functools.reduce(jnp.add, shares), axis=-1, keepdims=True)
        totals[own, :] = jnp.broadcast_to(total, (group, totals.shape[1]))
        for p in range(len(order)):
            weights[own, p * length : (p + 1) * length] = shares[p].astype(bf16)
    mixed = jnp.dot(weights[...], latents[...], preferred_element_type=f32)
    for head in range(heads):
        own = slice(head * length, (head + 1) * length)
        value = slice((heads + head) * DH, (heads + head + 1) * DH)
        outcome = mm(mixed[own], up[:, value])
        out[:, head * DH : (head + 1) * DH] = (outcome / totals[own, :]).astype(bf16)


def far_first(count):
    return sorted(range(1, count), key=lambda step: (-bin(step).count("1"), -step))


def per_device(
    kda_inputs,
    gate_log,
    beta,
    conv_weight,
    kda_out_weight,
    residual,
    norm_gain,
    latent_weight,
    latent_gain,
    query_weight,
    up_weight,
):
    length, width = residual.shape
    heads = beta.shape[1]
    pairs = heads // 2
    count, parts = lax.axis_size("ctx"), lax.axis_size("head")
    groups = count // heads

    stored = [
        pltpu.with_memory_space_constraint(a, pltpu.HBM) for a in (kda_inputs, gate_log, conv_weight)
    ]
    edge_shape = (kda_inputs.shape[0], HALO, kda_inputs.shape[2])
    last_rows = call(
        last_rows_kernel,
        [(edge_shape[1:], bf16)],
        stored[:1],
        [(edge_shape, bf16)],
        8,
        stored=(0,),
        copies=1,
        cost=0.2,
    )[0]
    halo = passed_along(last_rows, "ctx", 1)
    done, head_rows, logs, taps = call(
        load_kernel,
        [
            (kda_inputs.shape, bf16),
            (edge_shape, bf16),
            (gate_log.shape, f32),
            (conv_weight.shape, f32),
        ],
        stored,
        [
            (gate_log.shape, f32),
            (kda_inputs.shape, bf16),
            ((length + 8, heads * DK), f32),
        ],
        24,
        stored=(0, 1, 2),
        copies=3,
        cost=2.0,
    )
    map_shape = (2 * DK + EXTRA, DK)
    arguments = [done, head_rows, halo, logs, beta.T, taps]
    kept, sent, solutions, shrunk = call(
        map_kernel,
        [
            ((pairs,) + map_shape, bf16),
            ((pairs,) + map_shape, bf16),
            ((heads, length, 2 * DK), bf16),
            ((heads, 2, length, DK), bf16),
        ],
        arguments,
        [((2, HALO, heads * DK), bf16), ((HALO + 8, heads * DK), f32)],
        16,
        cost=5.0,
    )

    got = trade(sent, "ctx", 1, heads)
    got_kept = trade(kept, "ctx", 1, heads)
    reads, intra = call(
        read_kernel,
        [((length, heads * DK), bf16), ((length, heads * DK), f32)],
        arguments + [solutions, shrunk, got, got_kept],
        [((HALO, heads * DK), bf16), ((HALO + 8, heads * DK), f32)],
        16,
        cost=2.5,
    )
    chip_maps = call(
        functools.partial(compose_kernel, pairs),
        [(map_shape, bf16)] * pairs,
        [kept, got],
        [((pairs,) + map_shape, bf16)],
        8,
    )

    def across_chips(pieces):
        moved = {step: trade(pieces[step], "ctx", 2 * step, heads) for step in far_first(pairs)}
        return [pieces[0]] + [moved[step] for step in range(1, pairs)]

    chip_maps, reads, intra = lax.optimization_barrier((across_chips(chip_maps), reads, intra))
    chip_maps = call(
        functools.partial(stack_kernel, pairs),
        [((pairs,) + map_shape, bf16)],
        chip_maps,
        limit=8,
        cost=0.2,
    )[0]
    other_maps = trade(chip_maps, "ctx", 1, heads)
    state_outs = [((2, DK, DK), bf16)] * pairs
    scratch = [((pairs, 2, DK, DK), bf16)]

    def run(*start):
        return call(
            functools.partial(scan_kernel, pairs, len(start) > 0),
            state_outs + [((2, DK, DK), f32)] * len(start),
            [chip_maps, other_maps] + list(start),
            scratch,
            8,
        )

    if groups == 1:
        starts = run()
    else:

        def relay(step_index, start):
            arrived = passed_along(run(start)[pairs], "ctx", heads)
            return jnp.where(lax.axis_index("ctx") < heads, 0.0, arrived)

        start = lax.fori_loop(0, groups - 1, relay, jnp.zeros((2, DK, DK), f32))
        starts = run(start)[:pairs]
    starts = across_chips(starts)

    share = length // parts
    partials = call(
        functools.partial(project_kernel, parts),
        [((share, width), f32)] + [((share, width), bf16)] * (parts - 1),
        [residual, kda_out_weight, reads, intra] + starts,
        [((length, heads * DK), bf16), ((length, width), f32)],
        16,
    )

    def across_heads(pieces):
        moved = {step: trade(pieces[step], "head", step, parts) for step in far_first(parts)}
        return [pieces[0]] + [moved[step] for step in range(1, parts)]

    up = up_weight.reshape(up_weight.shape[0], -1)
    partials, up = lax.optimization_barrier((across_heads(partials), up))
    latent_width = latent_weight.shape[1]
    stream_rows, latent_rows, together = call(
        functools.partial(latent_kernel, parts),
        [
            ((share, width), bf16),
            ((share, latent_width), bf16),
            ((share, width + latent_width), bf16),
        ],
        [norm_gain[None], latent_weight, latent_gain[None]] + partials,
        limit=16,
    )
    latent_parts = across_heads([latent_rows, together] + [latent_rows] * (parts - 2))
    far_parts = []
    for step in range(2, parts, 2):
        far_parts.append(trade(stream_rows, "head", step, parts))
        far_parts.append(trade(far_parts[-1], "head", 1, parts))
    stream_parts = [stream_rows, latent_parts[1]] + far_parts
    latent = call(
        functools.partial(join_kernel, parts),
        [((length, latent_width), bf16)],
        latent_parts,
        limit=8,
    )[0]

    order, latents = [0], [latent]
    for step in far_first(count // 2):
        order.append(2 * step)
        latents.append(trade(latent, "ctx", 2 * step, count))
    for position in range(len(order)):
        order.append(order[position] + 1)
        latents.append(trade(latents[position], "ctx", 1, 2))
    heads_mla = query_weight.shape[1] // DH
    rows, latent_rows = heads_mla * length, count * length
    stream_out, attention_out = call(
        functools.partial(attend_kernel, parts, tuple(order)),
        [((length, width), bf16), ((length, heads_mla * DH), bf16)],
        [norm_gain[None], query_weight, up] + stream_parts + latents,
        [
            ((rows, latent_width), bf16),
            ((latent_rows, latent_width), bf16),
            ((rows, latent_rows), f32),
            ((rows, latent_rows), bf16),
            ((rows, DH), f32),
        ],
        16 + rows * latent_rows * 8 // MIB,
        cost=4.0,
    )
    return (stream_out, attention_out)


def solution(mesh):
    in_specs = (
        P(None, "ctx", "head"),
        P("ctx", "head"),
        P("ctx", "head"),
        P(None, None, "head"),
        P("head", None),
        P("ctx", None),
        P(),
        P(),
        P(),
        P(None, "head"),
        P(None, None, "head"),
    )
    out_specs = (P("ctx", None), P("ctx", "head"))
    return jax.shard_map(
        per_device, mesh=mesh, in_specs=in_specs, out_specs=out_specs, check_vma=False
    )
```

```python
import functools

import jax
import jax.numpy as jnp
from jax import lax
from jax.experimental import pallas as pl
from jax.experimental.pallas import tpu as pltpu
from jax.sharding import PartitionSpec as P

DK = 128
CONV = 4
DH = 128
HALO = 16
EXTRA = 16
MIB = 1 << 20

eps_norm = 1e-06
bf16 = jnp.bfloat16
f32 = jnp.float32
VMEM = pl.BlockSpec(memory_space=pltpu.VMEM)
HBM = pl.BlockSpec(memory_space=pltpu.HBM)


def mm(left, right):
    return jnp.dot(left.astype(bf16), right.astype(bf16), preferred_element_type=f32)


def mm_nt(left, right):
    return lax.dot_general(
        left.astype(bf16), right.astype(bf16), (((1,), (1,)), ((), ())), preferred_element_type=f32
    )


def mm_tn(left, right):
    return lax.dot_general(
        left.astype(bf16), right.astype(bf16), (((0,), (0,)), ((), ())), preferred_element_type=f32
    )


def call(kernel, outs, args, scratch=(), limit=32, stored=(), copies=0, cost=1.0):
    scratch_shapes = [pltpu.VMEM(shape, dtype) for shape, dtype in scratch]
    if copies:
        scratch_shapes.append(pltpu.SemaphoreType.DMA((copies,)))
    return pl.pallas_call(
        kernel,
        out_shape=[jax.ShapeDtypeStruct(shape, dtype) for shape, dtype in outs],
        in_specs=[HBM if i in stored else VMEM for i in range(len(args))],
        out_specs=[VMEM for _ in outs],
        scratch_shapes=scratch_shapes,
        compiler_params=pltpu.CompilerParams(vmem_limit_bytes=limit * MIB),
        cost_estimate=pl.CostEstimate(flops=int(cost * 1e9), bytes_accessed=0, transcendentals=0),
    )(*args)


def partner(index, step, size):
    return index ^ step if size & (size - 1) == 0 else (size + step - index) % size


def trade(block, axis, step, size):
    route = []
    for i in range(lax.axis_size(axis)):
        base = i // size * size
        route.append((i, base + partner(i - base, step, size)))
    return lax.ppermute(block, axis, route)


def passed_along(block, axis, distance):
    count = lax.axis_size(axis)
    return lax.ppermute(block, axis, [(i, (i + distance) % count) for i in range(count)])


def lanes(block_index, width=128):
    return pl.ds(pl.multiple_of(block_index * width, width), width)


def here(heads):
    token_index = lax.axis_index("ctx")
    return lax.rem(token_index, heads), lax.axis_index("head"), token_index


def split_cores(place):
    return place[0] // 2, place[0] % 2


def convolved(wide, taps, part, count):
    total = None
    for tap in range(CONV):
        first = 8 - (CONV - 1) + tap
        term = taps[part, tap : tap + 1, :] * wide[first : first + count, :]
        total = term if total is None else total + term
    return total / (1.0 + jnp.exp(-total))


def finished(activated, part):
    if part == 2:
        return activated.astype(bf16)
    heads = []
    for first in range(0, activated.shape[1], DK):
        head = activated[:, first : first + DK]
        head = head * lax.rsqrt(jnp.sum(head * head, axis=-1, keepdims=True) + eps_norm)
        heads.append((head * DK ** (-0.5) if part == 0 else head).astype(bf16))
    return jnp.concatenate(heads, axis=1)


def last_rows_kernel(stored_inputs, packed, rows, sems):
    length, count = stored_inputs.shape[1], rows.shape[1]
    move = pltpu.make_async_copy(
        stored_inputs.at[:, length - count : length, :], rows, sems.at[0]
    )
    move.start()
    move.wait()
    reach = CONV - 1
    last = [rows[part].astype(f32)[count - reach :] for part in range(rows.shape[0])]
    spare = jnp.zeros((packed.shape[0] - reach * len(last), packed.shape[1]), f32)
    packed[...] = jnp.concatenate(last + [spare], axis=0).astype(bf16)


def load_kernel(
    stored_inputs, stored_gate, stored_taps, done, head_rows, log, taps, gate, inputs, wide, sems
):
    moves = [
        pltpu.make_async_copy(stored_gate, gate, sems.at[0]),
        pltpu.make_async_copy(stored_taps, taps, sems.at[1]),
        pltpu.make_async_copy(stored_inputs, inputs, sems.at[2]),
    ]
    for move in moves:
        move.start()
    length = gate.shape[0]
    rows = lax.broadcasted_iota(jnp.int32, (length, length), 0)
    cols = lax.broadcasted_iota(jnp.int32, (length, length), 1)
    tril = (rows >= cols).astype(bf16)
    moves[0].wait()
    high = gate[...].astype(bf16)
    low = gate[...] - high.astype(f32)
    log[...] = mm(tril, high) + mm(tril, low)
    moves[1].wait()
    moves[2].wait()
    head_rows[...] = inputs[:, : head_rows.shape[1], :]
    for part in range(3):
        wide[:8, :] = jnp.zeros((8, wide.shape[1]), f32)
        wide[8:, :] = inputs[part].astype(f32)
        done[part] = finished(convolved(wide, taps, part, length), part)


def first_rows(place, halo, inputs, taps, part, wide):
    count, reach = inputs.shape[1], CONV - 1
    before = halo[...].astype(f32)[part * reach : (part + 1) * reach]
    wide[8 - reach : 8, :] = jnp.where(place[2] == 0, 0.0, before)
    wide[8:, :] = inputs[part].astype(f32)
    return finished(convolved(wide, taps, part, count), part)


def whole_head(first, done, part, lane):
    return jnp.concatenate([first[:, lane], done[part, first.shape[0] :, lane]], axis=0)


def spans(log):
    half = log.shape[0] // 2
    for b in range(2):
        middle = log[b * half + half // 2 : b * half + half // 2 + 1]
        yield b, slice(b * half, (b + 1) * half), middle


def side_heads(place, pairs):
    _, core = split_cores(place)
    return [2 * i + core for i in range(pairs)] + [2 * i + 1 - core for i in range(pairs)]


def map_kernel(
    done, head_rows, halo, logs, beta, taps, kept, sent, solutions, shrunk, first, wide
):
    length = logs.shape[0]
    pairs = kept.shape[0]
    place = here(2 * pairs)
    chunks = range(2 * pairs)
    heads = side_heads(place, pairs)
    lane = [lanes(head) for head in heads]
    rows = lax.broadcasted_iota(jnp.int32, (length, length), 0)
    cols = lax.broadcasted_iota(jnp.int32, (length, length), 1)
    eye = (rows == cols).astype(f32)
    for part in (1, 2):
        first[part - 1] = first_rows(place, halo, head_rows, taps, part, wide)

    coupling, right, finals, decay = [], [], [], []
    for i in chunks:
        key = whole_head(first.at[0], done, 1, lane[i]).astype(f32)
        value = whole_head(first.at[1], done, 2, lane[i])
        log = logs[:, lane[i]]
        rate_row = beta[pl.ds(heads[i], 1), :]
        rate_column = jnp.sum(rate_row * eye, axis=1, keepdims=True)
        last = log[length - 1 :]
        products = []
        for b, own, middle in spans(log):
            shrunk[i, b] = (key * jnp.exp(jnp.minimum(middle - log, 75.0))).astype(bf16)
            products.append(mm_nt(key[own] * jnp.exp(log[own] - middle), shrunk[i, b]))
        coupling.append(
            jnp.where(rows > cols, jnp.concatenate(products, axis=0) * rate_row, 0.0).astype(bf16)
        )
        right.append(jnp.concatenate([value, (key * jnp.exp(log)).astype(bf16)], axis=1))
        finals.append((key * jnp.exp(last - log) * rate_column).astype(bf16))
        decay.append(jnp.exp(last))

    size = 1
    inverse = None
    while size < length:
        corner = (
            (rows // (2 * size) == cols // (2 * size))
            & ((rows // size) % 2 == 1)
            & ((cols // size) % 2 == 0)
        )
        corners = [jnp.where(corner, coupling[i], jnp.zeros_like(coupling[i])) for i in chunks]
        if inverse is None:
            inverse = [eye - corners[i].astype(f32) for i in chunks]
        else:
            short = [inverse[i].astype(bf16) for i in chunks]
            below = [mm(corners[i], short[i]) for i in chunks]
            inverse = [inverse[i] - mm(short[i], below[i]) for i in chunks]
        size *= 2

    short = [inverse[i].astype(bf16) for i in chunks]
    near = [mm(short[i], right[i]).astype(bf16) for i in chunks]
    left = [right[i].astype(f32) - near[i].astype(f32) - mm(coupling[i], near[i]) for i in chunks]
    solved = [(near[i].astype(f32) + mm(short[i], left[i])).astype(bf16) for i in chunks]
    for i in chunks:
        solutions[i] = solved[i]
        maps = kept if i < pairs else sent
        put_map(maps, i % pairs, mm_tn(solved[i], finals[i]), decay[i])


def put_map(maps, i, offset_and_move, decay):
    maps[i, : 2 * DK, :] = offset_and_move.astype(bf16)
    high = decay.astype(bf16)
    low = (decay - high.astype(f32)).astype(bf16)
    maps[i, 2 * DK :, :] = jnp.concatenate(
        [jnp.broadcast_to(high, (EXTRA // 2, DK)), jnp.broadcast_to(low, (EXTRA // 2, DK))],
        axis=0,
    )


def read_kernel(done, head_rows, halo, logs, beta, taps, *refs):
    solutions, shrunk, stay, go, reads, intra, first, wide = refs
    length = logs.shape[0]
    pairs = stay.shape[0]
    place = here(2 * pairs)
    _, core = split_cores(place)
    first[...] = first_rows(place, halo, head_rows, taps, 0, wide)
    rows = lax.broadcasted_iota(jnp.int32, (length, length), 0)
    cols = lax.broadcasted_iota(jnp.int32, (length, length), 1)
    for i, head in enumerate(side_heads(place, pairs)):
        lane = lanes(head)
        query = whole_head(first, done, 0, lane).astype(f32)
        log = logs[:, lane]
        products = [
            mm_nt(query[own] * jnp.exp(log[own] - middle), shrunk[i, b])
            for b, own, middle in spans(log)
        ]
        rate_row = beta[pl.ds(head, 1), :]
        mixing = jnp.where(rows >= cols, jnp.concatenate(products, axis=0) * rate_row, 0.0)
        high = mixing.astype(bf16)
        mixes = mm(high, solutions[i]) + mm(mixing - high.astype(f32), solutions[i])
        read = query * jnp.exp(log) - mixes[:, DK:]
        offset, move, decay = parts_of((stay if i < pairs else go)[i % pairs])
        both = mm_nt(read, jnp.concatenate([offset, move], axis=0))
        second = core == 1
        intra[:, lane] = mixes[:, :DK] + jnp.where(second, both[:, :DK], 0.0)
        reads[:, lane] = jnp.where(second, read * decay - both[:, DK:], read).astype(bf16)


def parts_of(state_map):
    extra = state_map[2 * DK :].astype(f32)
    decay = extra[:1] + extra[EXTRA // 2 : EXTRA // 2 + 1]
    return state_map[:DK], state_map[DK : 2 * DK], decay


def compose_kernel(pairs, kept, got, *refs):
    outs, (maps,) = refs[:pairs], refs[pairs:]
    chip, core = split_cores(here(2 * pairs))
    eye = (
        lax.broadcasted_iota(jnp.int32, (DK, DK), 0) == lax.broadcasted_iota(jnp.int32, (DK, DK), 1)
    ).astype(f32)
    for pair in range(pairs):
        mine, other = kept[pair], got[pair]
        offset_a, move_a, decay_a = parts_of(jnp.where(core == 0, mine, other))
        offset_b, move_b, decay_b = parts_of(jnp.where(core == 0, other, mine))
        product = mm(jnp.concatenate([offset_a, move_a], axis=0), move_b)
        column = jnp.sum(eye * decay_a, axis=1, keepdims=True)
        offset = offset_a.astype(f32) * decay_b - product[:DK] + offset_b.astype(f32)
        move = move_a.astype(f32) * decay_b + column * move_b.astype(f32) - product[DK:]
        put_map(maps, pair, jnp.concatenate([offset, move], axis=0), decay_a * decay_b)
    for step in range(pairs):
        outs[step][...] = maps[partner(chip, step, pairs)]


def apply_map(state, state_map):
    offset, move, decay = parts_of(state_map)
    return state.astype(f32) * decay - mm(state, move) + offset.astype(f32)


def stack_kernel(pairs, *refs):
    blocks, (maps,) = refs[:pairs], refs[pairs:]
    chip, _ = split_cores(here(2 * pairs))
    for step in range(pairs):
        maps[partner(chip, step, pairs)] = blocks[step][...]


def scan_kernel(pairs, grouped, *refs):
    maps, refs = refs[:2], refs[2:]
    if grouped:
        start, refs = refs[0], refs[1:]
    outs, refs = refs[:pairs], refs[pairs:]
    if grouped:
        final, refs = refs[0], refs[1:]
    starts = refs[0]
    chip, _ = split_cores(here(2 * pairs))
    states = [start[side] if grouped else jnp.zeros((DK, DK), f32) for side in range(2)]
    for i in range(pairs):
        for side in range(2):
            starts[i, side] = states[side].astype(bf16)
            if i == 0 and not grouped:
                states[side] = maps[side][i, :DK, :].astype(f32)
            elif i < pairs - 1 or grouped:
                states[side] = apply_map(states[side], maps[side][i])
    if grouped:
        for side in range(2):
            final[side] = states[side]
    for step in range(pairs):
        outs[step][...] = starts[partner(chip, step, pairs)]


def project_kernel(parts, *refs):
    residual, weight, reads, intra = refs[:4]
    refs = refs[4:]
    pairs = reads.shape[1] // DK // 2
    place = here(2 * pairs)
    starts, refs = refs[:pairs], refs[pairs:]
    outs, (whole, summed) = refs[:parts], refs[parts:]
    chip, core = split_cores(place)
    head_me = place[1]
    for step in range(pairs):
        pair = partner(chip, step, pairs)
        for side, head in enumerate((2 * pair + core, 2 * pair + 1 - core)):
            own = lanes(head)
            whole[:, own] = (intra[:, own] + mm_nt(reads[:, own], starts[step][side])).astype(bf16)
    summed[...] = jnp.dot(whole[...], weight[...], preferred_element_type=f32)
    share = summed.shape[0] // parts
    for step in range(parts):
        at = pl.ds(pl.multiple_of(partner(head_me, step, parts) * share, share), share)
        if step == 0:
            outs[0][...] = summed[at, :] + residual[at, :].astype(f32)
        else:
            outs[step][...] = summed[at, :].astype(bf16)


def normalized(values, gain):
    return values * lax.rsqrt(jnp.mean(values * values, axis=-1, keepdims=True) + eps_norm) * gain


def latent_kernel(parts, *refs):
    gain, latent_weight, latent_gain = refs[:3]
    partials = refs[3 : 3 + parts]
    stream, latent, together = refs[3 + parts :]
    width = stream.shape[1]
    total = partials[0][...]
    for step in range(1, parts):
        total = total + partials[step][...].astype(f32)
    short = total.astype(bf16)
    stream[...] = short
    together[:, :width] = short
    normed = normalized(short.astype(f32), gain[...]).astype(bf16)
    before = jnp.dot(normed, latent_weight[...], preferred_element_type=f32)
    rows = normalized(before, latent_gain[...]).astype(bf16)
    latent[...] = rows
    together[:, width:] = rows


def join_kernel(parts, *refs):
    pieces = refs[:parts]
    out = refs[parts]
    share = out.shape[0] // parts
    for step in range(parts):
        at = pl.ds(pl.multiple_of(partner(lax.axis_index("head"), step, parts) * share, share), share)
        out[at, :] = pieces[step][:, pieces[step].shape[1] - out.shape[1] :]


def attend_kernel(parts, order, *refs):
    gain, query_weight, up = refs[:3]
    pieces, refs = refs[3 : 3 + parts], refs[3 + parts :]
    blocks, refs = refs[: len(order)], refs[len(order) :]
    stream, out, absorbed, latents, scores, weights, totals = refs
    length = stream.shape[0]
    heads = absorbed.shape[0] // length
    me = lax.axis_index("ctx")
    share = length // parts
    for step in range(parts):
        at = pl.ds(pl.multiple_of(partner(lax.axis_index("head"), step, parts) * share, share), share)
        stream[at, :] = pieces[step][:, : stream.shape[1]]
    for position in range(len(order)):
        latents[position * length : (position + 1) * length, :] = blocks[position][...]
    normed = normalized(stream[...].astype(f32), gain[...]).astype(bf16)
    query = jnp.dot(normed, query_weight[...], preferred_element_type=f32).astype(bf16)
    for head in range(heads):
        own = slice(head * DH, (head + 1) * DH)
        absorbed[head * length : (head + 1) * length, :] = (
            mm_nt(query[:, own], up[:, own]) * DH ** (-0.5)
        ).astype(bf16)
    span = min(2, heads) * length
    for first in range(0, heads * length, span):
        scores[first : first + span, :] = mm_nt(absorbed[first : first + span, :], latents[...])
    group = min(length, 16)
    for first in range(0, heads * length, group):
        own = slice(first, first + group)
        rows = lax.broadcasted_iota(jnp.int32, (group, length), 0) + first % length
        cols = lax.broadcasted_iota(jnp.int32, (group, length), 1)
        allowed = [rows >= cols] + [(me ^ distance) < me for distance in order[1:]]
        masked = [
            jnp.where(allowed[p], scores[own, p * length : (p + 1) * length], -1e30)
            for p in range(len(order))
        ]
        peak = jnp.max(functools.reduce(jnp.maximum, masked), axis=-1, keepdims=True)
        shares = [jnp.exp(part - peak) for part in masked]
        total = jnp.sum(functools.reduce(jnp.add, shares), axis=-1, keepdims=True)
        totals[own, :] = jnp.broadcast_to(total, (group, totals.shape[1]))
        for p in range(len(order)):
            weights[own, p * length : (p + 1) * length] = shares[p].astype(bf16)
    mixed = jnp.dot(weights[...], latents[...], preferred_element_type=f32)
    for head in range(heads):
        own = slice(head * length, (head + 1) * length)
        value = slice((heads + head) * DH, (heads + head + 1) * DH)
        outcome = mm(mixed[own], up[:, value])
        out[:, head * DH : (head + 1) * DH] = (outcome / totals[own, :]).astype(bf16)


def far_first(count):
    return sorted(range(1, count), key=lambda step: (-bin(step).count("1"), -step))


def per_device(
    kda_inputs,
    gate_log,
    beta,
    conv_weight,
    kda_out_weight,
    residual,
    norm_gain,
    latent_weight,
    latent_gain,
    query_weight,
    up_weight,
):
    length, width = residual.shape
    heads = beta.shape[1]
    pairs = heads // 2
    count, parts = lax.axis_size("ctx"), lax.axis_size("head")
    groups = count // heads

    stored = [
        pltpu.with_memory_space_constraint(a, pltpu.HBM) for a in (kda_inputs, gate_log, conv_weight)
    ]
    edge_shape = (kda_inputs.shape[0], HALO, kda_inputs.shape[2])
    last_rows = call(
        last_rows_kernel,
        [(edge_shape[1:], bf16)],
        stored[:1],
        [(edge_shape, bf16)],
        8,
        stored=(0,),
        copies=1,
        cost=0.2,
    )[0]
    halo = passed_along(last_rows, "ctx", 1)
    done, head_rows, logs, taps = call(
        load_kernel,
        [
            (kda_inputs.shape, bf16),
            (edge_shape, bf16),
            (gate_log.shape, f32),
            (conv_weight.shape, f32),
        ],
        stored,
        [
            (gate_log.shape, f32),
            (kda_inputs.shape, bf16),
            ((length + 8, heads * DK), f32),
        ],
        24,
        stored=(0, 1, 2),
        copies=3,
        cost=2.0,
    )
    map_shape = (2 * DK + EXTRA, DK)
    arguments = [done, head_rows, halo, logs, beta.T, taps]
    kept, sent, solutions, shrunk = call(
        map_kernel,
        [
            ((pairs,) + map_shape, bf16),
            ((pairs,) + map_shape, bf16),
            ((heads, length, 2 * DK), bf16),
            ((heads, 2, length, DK), bf16),
        ],
        arguments,
        [((2, HALO, heads * DK), bf16), ((HALO + 8, heads * DK), f32)],
        16,
        cost=5.0,
    )

    got = trade(sent, "ctx", 1, heads)
    got_kept = trade(kept, "ctx", 1, heads)
    reads, intra = call(
        read_kernel,
        [((length, heads * DK), bf16), ((length, heads * DK), f32)],
        arguments + [solutions, shrunk, got, got_kept],
        [((HALO, heads * DK), bf16), ((HALO + 8, heads * DK), f32)],
        16,
        cost=2.5,
    )
    chip_maps = call(
        functools.partial(compose_kernel, pairs),
        [(map_shape, bf16)] * pairs,
        [kept, got],
        [((pairs,) + map_shape, bf16)],
        8,
    )

    def across_chips(pieces):
        moved = {step: trade(pieces[step], "ctx", 2 * step, heads) for step in far_first(pairs)}
        return [pieces[0]] + [moved[step] for step in range(1, pairs)]

    chip_maps, reads, intra = lax.optimization_barrier((across_chips(chip_maps), reads, intra))
    chip_maps = call(
        functools.partial(stack_kernel, pairs),
        [((pairs,) + map_shape, bf16)],
        chip_maps,
        limit=8,
        cost=0.2,
    )[0]
    other_maps = trade(chip_maps, "ctx", 1, heads)
    state_outs = [((2, DK, DK), bf16)] * pairs
    scratch = [((pairs, 2, DK, DK), bf16)]

    def run(*start):
        return call(
            functools.partial(scan_kernel, pairs, len(start) > 0),
            state_outs + [((2, DK, DK), f32)] * len(start),
            [chip_maps, other_maps] + list(start),
            scratch,
            8,
        )

    if groups == 1:
        starts = run()
    else:

        def relay(step_index, start):
            arrived = passed_along(run(start)[pairs], "ctx", heads)
            return jnp.where(lax.axis_index("ctx") < heads, 0.0, arrived)

        start = lax.fori_loop(0, groups - 1, relay, jnp.zeros((2, DK, DK), f32))
        starts = run(start)[:pairs]
    starts = across_chips(starts)

    share = length // parts
    partials = call(
        functools.partial(project_kernel, parts),
        [((share, width), f32)] + [((share, width), bf16)] * (parts - 1),
        [residual, kda_out_weight, reads, intra] + starts,
        [((length, heads * DK), bf16), ((length, width), f32)],
        16,
    )

    def across_heads(pieces):
        moved = {step: trade(pieces[step], "head", step, parts) for step in far_first(parts)}
        return [pieces[0]] + [moved[step] for step in range(1, parts)]

    up = up_weight.reshape(up_weight.shape[0], -1)
    partials, up = lax.optimization_barrier((across_heads(partials), up))
    latent_width = latent_weight.shape[1]
    stream_rows, latent_rows, together = call(
        functools.partial(latent_kernel, parts),
        [
            ((share, width), bf16),
            ((share, latent_width), bf16),
            ((share, width + latent_width), bf16),
        ],
        [norm_gain[None], latent_weight, latent_gain[None]] + partials,
        limit=16,
    )
    latent_parts = across_heads([latent_rows, together] + [latent_rows] * (parts - 2))
    far_parts = []
    for step in range(2, parts, 2):
        far_parts.append(trade(stream_rows, "head", step, parts))
        far_parts.append(trade(far_parts[-1], "head", 1, parts))
    stream_parts = [stream_rows, latent_parts[1]] + far_parts
    latent = call(
        functools.partial(join_kernel, parts),
        [((length, latent_width), bf16)],
        latent_parts,
        limit=8,
    )[0]

    order, latents = [0], [latent]
    for step in far_first(count // 2):
        order.append(2 * step)
        latents.append(trade(latent, "ctx", 2 * step, count))
    for position in range(len(order)):
        order.append(order[position] + 1)
        latents.append(trade(latents[position], "ctx", 1, 2))
    heads_mla = query_weight.shape[1] // DH
    rows, latent_rows = heads_mla * length, count * length
    stream_out, attention_out = call(
        functools.partial(attend_kernel, parts, tuple(order)),
        [((length, width), bf16), ((length, heads_mla * DH), bf16)],
        [norm_gain[None], query_weight, up] + stream_parts + latents,
        [
            ((rows, latent_width), bf16),
            ((latent_rows, latent_width), bf16),
            ((rows, latent_rows), f32),
            ((rows, latent_rows), bf16),
            ((rows, DH), f32),
        ],
        16 + rows * latent_rows * 8 // MIB,
        cost=4.0,
    )
    return (stream_out, attention_out)


def solution(mesh):
    in_specs = (
        P(None, "ctx", "head"),
        P("ctx", "head"),
        P("ctx", "head"),
        P(None, None, "head"),
        P("head", None),
        P("ctx", None),
        P(),
        P(),
        P(),
        P(None, "head"),
        P(None, None, "head"),
    )
    out_specs = (P("ctx", None), P("ctx", "head"))
    return jax.shard_map(
        per_device, mesh=mesh, in_specs=in_specs, out_specs=out_specs, check_vma=False
    )
```

```python
import functools

import jax
import jax.numpy as jnp
from jax import lax
from jax.experimental import pallas as pl
from jax.experimental.pallas import tpu as pltpu
from jax.sharding import PartitionSpec as P

DK = 128
CONV = 4
DH = 128
HALO = 16
EXTRA = 16
MIB = 1 << 20

eps_norm = 1e-06
bf16 = jnp.bfloat16
f32 = jnp.float32
VMEM = pl.BlockSpec(memory_space=pltpu.VMEM)
HBM = pl.BlockSpec(memory_space=pltpu.HBM)


def mm(left, right):
    return jnp.dot(left.astype(bf16), right.astype(bf16), preferred_element_type=f32)


def mm_nt(left, right):
    return lax.dot_general(
        left.astype(bf16), right.astype(bf16), (((1,), (1,)), ((), ())), preferred_element_type=f32
    )


def mm_tn(left, right):
    return lax.dot_general(
        left.astype(bf16), right.astype(bf16), (((0,), (0,)), ((), ())), preferred_element_type=f32
    )


def call(kernel, outs, args, scratch=(), limit=32, stored=(), copies=0, cost=1.0, results=False):
    scratch_shapes = [pltpu.VMEM(shape, dtype) for shape, dtype in scratch]
    if copies:
        scratch_shapes.append(pltpu.SemaphoreType.DMA((copies,)))
    return pl.pallas_call(
        kernel,
        out_shape=[jax.ShapeDtypeStruct(shape, dtype) for shape, dtype in outs],
        in_specs=[HBM if i in stored else VMEM for i in range(len(args))],
        out_specs=[HBM if results else VMEM for _ in outs],
        scratch_shapes=scratch_shapes,
        compiler_params=pltpu.CompilerParams(vmem_limit_bytes=limit * MIB),
        cost_estimate=pl.CostEstimate(flops=int(cost * 1e9), bytes_accessed=0, transcendentals=0),
    )(*args)


def partner(index, step, size):
    return index ^ step if size & (size - 1) == 0 else (size + step - index) % size


def trade(block, axis, step, size):
    route = []
    for i in range(lax.axis_size(axis)):
        base = i // size * size
        route.append((i, base + partner(i - base, step, size)))
    return lax.ppermute(block, axis, route)


def passed_along(block, axis, distance):
    count = lax.axis_size(axis)
    return lax.ppermute(block, axis, [(i, (i + distance) % count) for i in range(count)])


def lanes(block_index, width=128):
    return pl.ds(pl.multiple_of(block_index * width, width), width)


def here(heads):
    token_index = lax.axis_index("ctx")
    return lax.rem(token_index, heads), lax.axis_index("head"), token_index


def split_cores(place):
    return place[0] // 2, place[0] % 2


def convolved(wide, taps, part, count):
    total = None
    for tap in range(CONV):
        first = 8 - (CONV - 1) + tap
        term = taps[part, tap : tap + 1, :] * wide[first : first + count, :]
        total = term if total is None else total + term
    return total / (1.0 + jnp.exp(-total))


def finished(activated, part):
    if part == 2:
        return activated.astype(bf16)
    heads = []
    for first in range(0, activated.shape[1], DK):
        head = activated[:, first : first + DK]
        head = head * lax.rsqrt(jnp.sum(head * head, axis=-1, keepdims=True) + eps_norm)
        heads.append((head * DK ** (-0.5) if part == 0 else head).astype(bf16))
    return jnp.concatenate(heads, axis=1)


def last_rows_kernel(stored_inputs, packed, rows, sems):
    length, count = stored_inputs.shape[1], rows.shape[1]
    move = pltpu.make_async_copy(
        stored_inputs.at[:, length - count : length, :], rows, sems.at[0]
    )
    move.start()
    move.wait()
    reach = CONV - 1
    last = [rows[part].astype(f32)[count - reach :] for part in range(rows.shape[0])]
    spare = jnp.zeros((packed.shape[0] - reach * len(last), packed.shape[1]), f32)
    packed[...] = jnp.concatenate(last + [spare], axis=0).astype(bf16)


def load_kernel(
    stored_inputs, stored_gate, stored_taps, done, head_rows, log, taps, gate, inputs, wide, sems
):
    moves = [
        pltpu.make_async_copy(stored_gate, gate, sems.at[0]),
        pltpu.make_async_copy(stored_taps, taps, sems.at[1]),
        pltpu.make_async_copy(stored_inputs, inputs, sems.at[2]),
    ]
    for move in moves:
        move.start()
    length = gate.shape[0]
    rows = lax.broadcasted_iota(jnp.int32, (length, length), 0)
    cols = lax.broadcasted_iota(jnp.int32, (length, length), 1)
    tril = (rows >= cols).astype(bf16)
    moves[0].wait()
    high = gate[...].astype(bf16)
    low = gate[...] - high.astype(f32)
    log[...] = mm(tril, high) + mm(tril, low)
    moves[1].wait()
    moves[2].wait()
    head_rows[...] = inputs[:, : head_rows.shape[1], :]
    for part in range(3):
        wide[:8, :] = jnp.zeros((8, wide.shape[1]), f32)
        wide[8:, :] = inputs[part].astype(f32)
        done[part] = finished(convolved(wide, taps, part, length), part)


def first_rows(place, halo, inputs, taps, part, wide):
    count, reach = inputs.shape[1], CONV - 1
    before = halo[...].astype(f32)[part * reach : (part + 1) * reach]
    wide[8 - reach : 8, :] = jnp.where(place[2] == 0, 0.0, before)
    wide[8:, :] = inputs[part].astype(f32)
    return finished(convolved(wide, taps, part, count), part)


def whole_head(first, done, part, lane):
    return jnp.concatenate([first[:, lane], done[part, first.shape[0] :, lane]], axis=0)


def spans(log):
    half = log.shape[0] // 2
    for b in range(2):
        middle = log[b * half + half // 2 : b * half + half // 2 + 1]
        yield b, slice(b * half, (b + 1) * half), middle


def side_heads(place, pairs):
    _, core = split_cores(place)
    return [2 * i + core for i in range(pairs)] + [2 * i + 1 - core for i in range(pairs)]


def map_kernel(
    done, head_rows, halo, logs, beta, taps, kept, sent, solutions, shrunk, first, wide
):
    length = logs.shape[0]
    pairs = kept.shape[0]
    place = here(2 * pairs)
    chunks = range(2 * pairs)
    heads = side_heads(place, pairs)
    lane = [lanes(head) for head in heads]
    rows = lax.broadcasted_iota(jnp.int32, (length, length), 0)
    cols = lax.broadcasted_iota(jnp.int32, (length, length), 1)
    eye = (rows == cols).astype(f32)
    for part in (1, 2):
        first[part - 1] = first_rows(place, halo, head_rows, taps, part, wide)

    coupling, right, finals, decay = [], [], [], []
    for i in chunks:
        key = whole_head(first.at[0], done, 1, lane[i]).astype(f32)
        value = whole_head(first.at[1], done, 2, lane[i])
        log = logs[:, lane[i]]
        rate_row = beta[pl.ds(heads[i], 1), :]
        rate_column = jnp.sum(rate_row * eye, axis=1, keepdims=True)
        last = log[length - 1 :]
        products = []
        for b, own, middle in spans(log):
            shrunk[i, b] = (key * jnp.exp(jnp.minimum(middle - log, 75.0))).astype(bf16)
            products.append(mm_nt(key[own] * jnp.exp(log[own] - middle), shrunk[i, b]))
        coupling.append(
            jnp.where(rows > cols, jnp.concatenate(products, axis=0) * rate_row, 0.0).astype(bf16)
        )
        right.append(jnp.concatenate([value, (key * jnp.exp(log)).astype(bf16)], axis=1))
        finals.append((key * jnp.exp(last - log) * rate_column).astype(bf16))
        decay.append(jnp.exp(last))

    size = 1
    inverse = None
    while size < length:
        corner = (
            (rows // (2 * size) == cols // (2 * size))
            & ((rows // size) % 2 == 1)
            & ((cols // size) % 2 == 0)
        )
        corners = [jnp.where(corner, coupling[i], jnp.zeros_like(coupling[i])) for i in chunks]
        if inverse is None:
            inverse = [eye - corners[i].astype(f32) for i in chunks]
        else:
            short = [inverse[i].astype(bf16) for i in chunks]
            below = [mm(corners[i], short[i]) for i in chunks]
            inverse = [inverse[i] - mm(short[i], below[i]) for i in chunks]
        size *= 2

    short = [inverse[i].astype(bf16) for i in chunks]
    near = [mm(short[i], right[i]).astype(bf16) for i in chunks]
    left = [right[i].astype(f32) - near[i].astype(f32) - mm(coupling[i], near[i]) for i in chunks]
    solved = [(near[i].astype(f32) + mm(short[i], left[i])).astype(bf16) for i in chunks]
    for i in chunks:
        solutions[i] = solved[i]
        maps = kept if i < pairs else sent
        put_map(maps, i % pairs, mm_tn(solved[i], finals[i]), decay[i])


def put_map(maps, i, offset_and_move, decay):
    maps[i, : 2 * DK, :] = offset_and_move.astype(bf16)
    high = decay.astype(bf16)
    low = (decay - high.astype(f32)).astype(bf16)
    maps[i, 2 * DK :, :] = jnp.concatenate(
        [jnp.broadcast_to(high, (EXTRA // 2, DK)), jnp.broadcast_to(low, (EXTRA // 2, DK))],
        axis=0,
    )


def read_kernel(done, head_rows, halo, logs, beta, taps, *refs):
    solutions, shrunk, stay, go, reads, intra, first, wide = refs
    length = logs.shape[0]
    pairs = stay.shape[0]
    place = here(2 * pairs)
    _, core = split_cores(place)
    first[...] = first_rows(place, halo, head_rows, taps, 0, wide)
    rows = lax.broadcasted_iota(jnp.int32, (length, length), 0)
    cols = lax.broadcasted_iota(jnp.int32, (length, length), 1)
    for i, head in enumerate(side_heads(place, pairs)):
        lane = lanes(head)
        query = whole_head(first, done, 0, lane).astype(f32)
        log = logs[:, lane]
        products = [
            mm_nt(query[own] * jnp.exp(log[own] - middle), shrunk[i, b])
            for b, own, middle in spans(log)
        ]
        rate_row = beta[pl.ds(head, 1), :]
        mixing = jnp.where(rows >= cols, jnp.concatenate(products, axis=0) * rate_row, 0.0)
        high = mixing.astype(bf16)
        mixes = mm(high, solutions[i]) + mm(mixing - high.astype(f32), solutions[i])
        read = query * jnp.exp(log) - mixes[:, DK:]
        offset, move, decay = parts_of((stay if i < pairs else go)[i % pairs])
        both = mm_nt(read, jnp.concatenate([offset, move], axis=0))
        second = core == 1
        intra[:, lane] = mixes[:, :DK] + jnp.where(second, both[:, :DK], 0.0)
        reads[:, lane] = jnp.where(second, read * decay - both[:, DK:], read).astype(bf16)


def parts_of(state_map):
    extra = state_map[2 * DK :].astype(f32)
    decay = extra[:1] + extra[EXTRA // 2 : EXTRA // 2 + 1]
    return state_map[:DK], state_map[DK : 2 * DK], decay


def compose_kernel(pairs, kept, got, *refs):
    outs, (maps,) = refs[:pairs], refs[pairs:]
    chip, core = split_cores(here(2 * pairs))
    eye = (
        lax.broadcasted_iota(jnp.int32, (DK, DK), 0) == lax.broadcasted_iota(jnp.int32, (DK, DK), 1)
    ).astype(f32)
    for pair in range(pairs):
        mine, other = kept[pair], got[pair]
        offset_a, move_a, decay_a = parts_of(jnp.where(core == 0, mine, other))
        offset_b, move_b, decay_b = parts_of(jnp.where(core == 0, other, mine))
        product = mm(jnp.concatenate([offset_a, move_a], axis=0), move_b)
        column = jnp.sum(eye * decay_a, axis=1, keepdims=True)
        offset = offset_a.astype(f32) * decay_b - product[:DK] + offset_b.astype(f32)
        move = move_a.astype(f32) * decay_b + column * move_b.astype(f32) - product[DK:]
        put_map(maps, pair, jnp.concatenate([offset, move], axis=0), decay_a * decay_b)
    for step in range(pairs):
        outs[step][...] = maps[partner(chip, step, pairs)]


def apply_map(state, state_map):
    offset, move, decay = parts_of(state_map)
    return state.astype(f32) * decay - mm(state, move) + offset.astype(f32)


def stack_kernel(pairs, *refs):
    blocks, (maps,) = refs[:pairs], refs[pairs:]
    chip, _ = split_cores(here(2 * pairs))
    for step in range(pairs):
        maps[partner(chip, step, pairs)] = blocks[step][...]


def scan_kernel(pairs, grouped, *refs):
    maps, refs = refs[:2], refs[2:]
    if grouped:
        start, refs = refs[0], refs[1:]
    outs, refs = refs[:pairs], refs[pairs:]
    if grouped:
        final, refs = refs[0], refs[1:]
    starts = refs[0]
    chip, _ = split_cores(here(2 * pairs))
    states = [start[side] if grouped else jnp.zeros((DK, DK), f32) for side in range(2)]
    for i in range(pairs):
        for side in range(2):
            starts[i, side] = states[side].astype(bf16)
            if i == 0 and not grouped:
                states[side] = maps[side][i, :DK, :].astype(f32)
            elif i < pairs - 1 or grouped:
                states[side] = apply_map(states[side], maps[side][i])
    if grouped:
        for side in range(2):
            final[side] = states[side]
    for step in range(pairs):
        outs[step][...] = starts[partner(chip, step, pairs)]


def project_kernel(parts, *refs):
    residual, weight, reads, intra = refs[:4]
    refs = refs[4:]
    pairs = reads.shape[1] // DK // 2
    place = here(2 * pairs)
    starts, refs = refs[:pairs], refs[pairs:]
    outs, (whole, summed) = refs[:parts], refs[parts:]
    chip, core = split_cores(place)
    head_me = place[1]
    for step in range(pairs):
        pair = partner(chip, step, pairs)
        for side, head in enumerate((2 * pair + core, 2 * pair + 1 - core)):
            own = lanes(head)
            whole[:, own] = (intra[:, own] + mm_nt(reads[:, own], starts[step][side])).astype(bf16)
    summed[...] = jnp.dot(whole[...], weight[...], preferred_element_type=f32)
    share = summed.shape[0] // parts
    for step in range(parts):
        at = pl.ds(pl.multiple_of(partner(head_me, step, parts) * share, share), share)
        if step == 0:
            outs[0][...] = summed[at, :] + residual[at, :].astype(f32)
        else:
            outs[step][...] = summed[at, :].astype(bf16)


def normalized(values, gain):
    return values * lax.rsqrt(jnp.mean(values * values, axis=-1, keepdims=True) + eps_norm) * gain


def latent_kernel(parts, *refs):
    gain, latent_weight, latent_gain = refs[:3]
    partials = refs[3 : 3 + parts]
    stream, latent, together = refs[3 + parts :]
    width = stream.shape[1]
    total = partials[0][...]
    for step in range(1, parts):
        total = total + partials[step][...].astype(f32)
    short = total.astype(bf16)
    stream[...] = short
    together[:, :width] = short
    normed = normalized(short.astype(f32), gain[...]).astype(bf16)
    before = jnp.dot(normed, latent_weight[...], preferred_element_type=f32)
    rows = normalized(before, latent_gain[...]).astype(bf16)
    latent[...] = rows
    together[:, width:] = rows


def join_kernel(parts, *refs):
    pieces = refs[:parts]
    out = refs[parts]
    share = out.shape[0] // parts
    for step in range(parts):
        at = pl.ds(pl.multiple_of(partner(lax.axis_index("head"), step, parts) * share, share), share)
        out[at, :] = pieces[step][:, pieces[step].shape[1] - out.shape[1] :]


def attend_kernel(parts, order, *refs):
    gain, query_weight, up = refs[:3]
    pieces, refs = refs[3 : 3 + parts], refs[3 + parts :]
    blocks, refs = refs[: len(order)], refs[len(order) :]
    stored_stream, stored_out, stream, out, absorbed, latents, scores, weights, totals, sems = refs
    save_stream = pltpu.make_async_copy(stream, stored_stream, sems.at[0])
    save_out = pltpu.make_async_copy(out, stored_out, sems.at[1])
    length = stream.shape[0]
    heads = absorbed.shape[0] // length
    me = lax.axis_index("ctx")
    share = length // parts
    for step in range(parts):
        at = pl.ds(pl.multiple_of(partner(lax.axis_index("head"), step, parts) * share, share), share)
        stream[at, :] = pieces[step][:, : stream.shape[1]]
    save_stream.start()
    for position in range(len(order)):
        latents[position * length : (position + 1) * length, :] = blocks[position][...]
    normed = normalized(stream[...].astype(f32), gain[...]).astype(bf16)
    query = jnp.dot(normed, query_weight[...], preferred_element_type=f32).astype(bf16)
    for head in range(heads):
        own = slice(head * DH, (head + 1) * DH)
        absorbed[head * length : (head + 1) * length, :] = (
            mm_nt(query[:, own], up[:, own]) * DH ** (-0.5)
        ).astype(bf16)
    span = min(2, heads) * length
    for first in range(0, heads * length, span):
        scores[first : first + span, :] = mm_nt(absorbed[first : first + span, :], latents[...])
    group = min(length, 16)
    for first in range(0, heads * length, group):
        own = slice(first, first + group)
        rows = lax.broadcasted_iota(jnp.int32, (group, length), 0) + first % length
        cols = lax.broadcasted_iota(jnp.int32, (group, length), 1)
        allowed = [rows >= cols] + [(me ^ distance) < me for distance in order[1:]]
        masked = [
            jnp.where(allowed[p], scores[own, p * length : (p + 1) * length], -1e30)
            for p in range(len(order))
        ]
        peak = jnp.max(functools.reduce(jnp.maximum, masked), axis=-1, keepdims=True)
        shares = [jnp.exp(part - peak) for part in masked]
        total = jnp.sum(functools.reduce(jnp.add, shares), axis=-1, keepdims=True)
        totals[own, :] = jnp.broadcast_to(total, (group, totals.shape[1]))
        for p in range(len(order)):
            weights[own, p * length : (p + 1) * length] = shares[p].astype(bf16)
    mixed = jnp.dot(weights[...], latents[...], preferred_element_type=f32)
    for head in range(heads):
        own = slice(head * length, (head + 1) * length)
        value = slice((heads + head) * DH, (heads + head + 1) * DH)
        outcome = mm(mixed[own], up[:, value])
        out[:, head * DH : (head + 1) * DH] = (outcome / totals[own, :]).astype(bf16)
    save_out.start()
    save_stream.wait()
    save_out.wait()


def far_first(count):
    return sorted(range(1, count), key=lambda step: (-bin(step).count("1"), -step))


def per_device(
    kda_inputs,
    gate_log,
    beta,
    conv_weight,
    kda_out_weight,
    residual,
    norm_gain,
    latent_weight,
    latent_gain,
    query_weight,
    up_weight,
):
    length, width = residual.shape
    heads = beta.shape[1]
    pairs = heads // 2
    count, parts = lax.axis_size("ctx"), lax.axis_size("head")
    groups = count // heads

    stored = [
        pltpu.with_memory_space_constraint(a, pltpu.HBM) for a in (kda_inputs, gate_log, conv_weight)
    ]
    edge_shape = (kda_inputs.shape[0], HALO, kda_inputs.shape[2])
    last_rows = call(
        last_rows_kernel,
        [(edge_shape[1:], bf16)],
        stored[:1],
        [(edge_shape, bf16)],
        8,
        stored=(0,),
        copies=1,
        cost=0.2,
    )[0]
    halo = passed_along(last_rows, "ctx", 1)
    done, head_rows, logs, taps = call(
        load_kernel,
        [
            (kda_inputs.shape, bf16),
            (edge_shape, bf16),
            (gate_log.shape, f32),
            (conv_weight.shape, f32),
        ],
        stored,
        [
            (gate_log.shape, f32),
            (kda_inputs.shape, bf16),
            ((length + 8, heads * DK), f32),
        ],
        24,
        stored=(0, 1, 2),
        copies=3,
        cost=2.0,
    )
    map_shape = (2 * DK + EXTRA, DK)
    arguments = [done, head_rows, halo, logs, beta.T, taps]
    kept, sent, solutions, shrunk = call(
        map_kernel,
        [
            ((pairs,) + map_shape, bf16),
            ((pairs,) + map_shape, bf16),
            ((heads, length, 2 * DK), bf16),
            ((heads, 2, length, DK), bf16),
        ],
        arguments,
        [((2, HALO, heads * DK), bf16), ((HALO + 8, heads * DK), f32)],
        16,
        cost=5.0,
    )

    got = trade(sent, "ctx", 1, heads)
    got_kept = trade(kept, "ctx", 1, heads)
    reads, intra = call(
        read_kernel,
        [((length, heads * DK), bf16), ((length, heads * DK), f32)],
        arguments + [solutions, shrunk, got, got_kept],
        [((HALO, heads * DK), bf16), ((HALO + 8, heads * DK), f32)],
        16,
        cost=2.5,
    )
    chip_maps = call(
        functools.partial(compose_kernel, pairs),
        [(map_shape, bf16)] * pairs,
        [kept, got],
        [((pairs,) + map_shape, bf16)],
        8,
    )

    def across_chips(pieces):
        moved = {step: trade(pieces[step], "ctx", 2 * step, heads) for step in far_first(pairs)}
        return [pieces[0]] + [moved[step] for step in range(1, pairs)]

    chip_maps, reads, intra = lax.optimization_barrier((across_chips(chip_maps), reads, intra))
    chip_maps = call(
        functools.partial(stack_kernel, pairs),
        [((pairs,) + map_shape, bf16)],
        chip_maps,
        limit=8,
        cost=0.2,
    )[0]
    other_maps = trade(chip_maps, "ctx", 1, heads)
    state_outs = [((2, DK, DK), bf16)] * pairs
    scratch = [((pairs, 2, DK, DK), bf16)]

    def run(*start):
        return call(
            functools.partial(scan_kernel, pairs, len(start) > 0),
            state_outs + [((2, DK, DK), f32)] * len(start),
            [chip_maps, other_maps] + list(start),
            scratch,
            8,
        )

    if groups == 1:
        starts = run()
    else:

        def relay(step_index, start):
            arrived = passed_along(run(start)[pairs], "ctx", heads)
            return jnp.where(lax.axis_index("ctx") < heads, 0.0, arrived)

        start = lax.fori_loop(0, groups - 1, relay, jnp.zeros((2, DK, DK), f32))
        starts = run(start)[:pairs]
    starts = across_chips(starts)

    share = length // parts
    partials = call(
        functools.partial(project_kernel, parts),
        [((share, width), f32)] + [((share, width), bf16)] * (parts - 1),
        [residual, kda_out_weight, reads, intra] + starts,
        [((length, heads * DK), bf16), ((length, width), f32)],
        16,
    )

    def across_heads(pieces):
        moved = {step: trade(pieces[step], "head", step, parts) for step in far_first(parts)}
        return [pieces[0]] + [moved[step] for step in range(1, parts)]

    up = up_weight.reshape(up_weight.shape[0], -1)
    partials, up = lax.optimization_barrier((across_heads(partials), up))
    latent_width = latent_weight.shape[1]
    stream_rows, latent_rows, together = call(
        functools.partial(latent_kernel, parts),
        [
            ((share, width), bf16),
            ((share, latent_width), bf16),
            ((share, width + latent_width), bf16),
        ],
        [norm_gain[None], latent_weight, latent_gain[None]] + partials,
        limit=16,
    )
    latent_parts = across_heads([latent_rows, together] + [latent_rows] * (parts - 2))
    far_parts = []
    for step in range(2, parts, 2):
        far_parts.append(trade(stream_rows, "head", step, parts))
        far_parts.append(trade(far_parts[-1], "head", 1, parts))
    stream_parts = [stream_rows, latent_parts[1]] + far_parts
    latent = call(
        functools.partial(join_kernel, parts),
        [((length, latent_width), bf16)],
        latent_parts,
        limit=8,
    )[0]

    order, latents = [0], [latent]
    for step in far_first(count // 2):
        order.append(2 * step)
        latents.append(trade(latent, "ctx", 2 * step, count))
    for position in range(len(order)):
        order.append(order[position] + 1)
        latents.append(trade(latents[position], "ctx", 1, 2))
    heads_mla = query_weight.shape[1] // DH
    rows, latent_rows = heads_mla * length, count * length
    stream_out, attention_out = call(
        functools.partial(attend_kernel, parts, tuple(order)),
        [((length, width), bf16), ((length, heads_mla * DH), bf16)],
        [norm_gain[None], query_weight, up] + stream_parts + latents,
        [
            ((length, width), bf16),
            ((length, heads_mla * DH), bf16),
            ((rows, latent_width), bf16),
            ((latent_rows, latent_width), bf16),
            ((rows, latent_rows), f32),
            ((rows, latent_rows), bf16),
            ((rows, DH), f32),
        ],
        16 + rows * latent_rows * 8 // MIB,
        copies=2,
        cost=4.0,
        results=True,
    )
    return (stream_out, attention_out)


def solution(mesh):
    in_specs = (
        P(None, "ctx", "head"),
        P("ctx", "head"),
        P("ctx", "head"),
        P(None, None, "head"),
        P("head", None),
        P("ctx", None),
        P(),
        P(),
        P(),
        P(None, "head"),
        P(None, None, "head"),
    )
    out_specs = (P("ctx", None), P("ctx", "head"))
    return jax.shard_map(
        per_device, mesh=mesh, in_specs=in_specs, out_specs=out_specs, check_vma=False
    )
```
